32 devices in a mesh: clips: 2 (over y), frame: 4 (over z), head: 2 (over x), seq: 2 (over core).
Axes of the slice: x: 2, y: 2, z: 4, core: 2. Of those that a mesh axis runs over, the one named last changes fastest.
Arguments:
- queries: bfloat16 [32, 1024, 1536], P(('clips', 'frame'), 'seq', 'head'), parts along dimension 0, may hold values from -150 to 150, as said below
- key_rows: bfloat16 [32, 1024, 1536], P(('clips', 'frame'), 'seq', 'head'), parts along dimension 0, may hold values from -5 to 5, as said below
- value_rows: bfloat16 [32, 1024, 1536], P(('clips', 'frame'), 'seq', 'head'), parts along dimension 0, may hold values from -6 to 6
- list_one: int32 [32, 2, 4], P('clips'), parts along dimension 0, may hold values from 0 to 7, as said below
- list_two: int32 [32, 2, 2], P('clips'), parts along dimension 0, may hold values from 0 to 7, as said below
- list_four: int32 [32, 2, 1], P('clips'), parts along dimension 0, may hold values from 0 to 7, as said below
- tile_counts: int32 [32, 2, 3], P('clips'), parts along dimension 0, may hold values from 0 to 4, as said below
Outputs:
- attended: bfloat16 [32, 1024, 1536], P(('clips', 'frame'), 'seq', 'head'), parts along dimension 0
The draws below stay inside these ranges and needn't reach their ends.
There are 2 independent parts, one for each index of `clips`. The reference program is written for one: setup_inputs(seed, part) draws one part's arguments, and reference() takes and returns one part's arrays. A program takes and returns all parts, laid end to end along the dimension named above; each array names one. Nothing has to cross between parts.
Inputs may be any that keep to these rules, and one draw needn't show every extreme that they name: Real-valued queries; a few query rows of a frame may be far larger in magnitude than the others. `key_rows`: Real-valued keys of order one. The entries of list_one[f, e, :] are distinct tile numbers of the frame f - 1 (e = 0) or f + 1 (e = 1). The entries of list_two[f, e, :] are distinct tile numbers of the frame f - 2 (e = 0) or f + 2 (e = 1). The entries of list_four[f, e, :] are distinct tile numbers of the frame f - 4 (e = 0) or f + 4 (e = 1). tile_counts[f, e, j] counts the live leading entries of the list of distance 1, 2, 4 (j = 0, 1, 2) for frame f and direction e; it is 0 exactly where the source frame lies outside the clip, else at least 1 and at most that list's length; frame 0's lists toward later frames are full.
All inputs are finite; a program needn't handle non-finite values.
Results may differ from the reference program's by a relative error of at most 0.0032.
Values may be sent and summed in bfloat16 or wider, within the bound.
No kernel may reach another device: no remote copies, remote signals or barrier semaphores. Data moves between devices by JAX's collectives and lax.ppermute only.
A program may use at most 128 MiB of HBM per device.

```python
import jax
import jax.numpy as jnp
from jax import lax

HEADS = 12
HEAD_DIM = 128
FRAME_TILES = 8
TILE_TOKENS = 128
FRAMES = 16
FRAME_TOKENS = 1024
LIST_ONE = 4
LIST_TWO = 2
LIST_FOUR = 1


def paired_fields(key):
    shape = (FRAMES, FRAME_TOKENS, HEADS * HEAD_DIM)
    key_field = jnp.clip(jax.random.normal(jax.random.fold_in(key, 12), shape, jnp.float32), -5.0, 5.0)
    query_field = jnp.clip(2.5 * jax.random.normal(jax.random.fold_in(key, 11), shape, jnp.float32), -15.0, 15.0)
    return (query_field, key_field)


def draw_queries(key, part):
    return paired_fields(key)[0].astype(jnp.bfloat16)


def draw_key_rows(key, part):
    return paired_fields(key)[1].astype(jnp.bfloat16)


def tile_choice(key, length):
    ranking = jax.random.randint(key, (FRAMES, 2, FRAME_TILES), 0, 2 ** 20) * FRAME_TILES
    ranking = ranking + jnp.arange(FRAME_TILES, dtype=jnp.int32)[None, None, :]
    ordering = jnp.argsort(ranking, axis=2, stable=True)
    return ordering[:, :, :length].astype(jnp.int32)


def draw_list_one(key, part):
    return tile_choice(jax.random.fold_in(key, 21), LIST_ONE)


def draw_list_two(key, part):
    return tile_choice(jax.random.fold_in(key, 22), LIST_TWO)


def draw_list_four(key, part):
    return tile_choice(jax.random.fold_in(key, 23), LIST_FOUR)


def draw_tile_counts(key, part):
    upper = jnp.array([LIST_ONE, LIST_TWO, LIST_FOUR], jnp.int32)
    counted = jax.random.randint(jax.random.fold_in(key, 31), (FRAMES, 2, 3), 1, upper[None, None, :] + 1)
    frame_index = jnp.arange(FRAMES, dtype=jnp.int32)[:, None, None]
    distances = jnp.array([1, 2, 4], jnp.int32)[None, None, :]
    signs = (jnp.arange(2, dtype=jnp.int32) * 2 - 1)[None, :, None]
    target = frame_index + signs * distances
    inside_clip = (target >= 0) & (target < FRAMES)
    counted = jnp.where(inside_clip, counted, 0)
    counted = counted.at[0, 1, :].set(upper)
    return counted.astype(jnp.int32)


def levels(stream_key, dims, pieces, least, largest):
    level = 1.0
    for position, blocks in pieces:
        steps = jax.random.uniform(jax.random.fold_in(jax.random.fold_in(stream_key, 6), position), (blocks,), jnp.float32, least / len(pieces), largest / len(pieces))
        level = level * jnp.repeat(jnp.exp(steps), dims[position] // blocks).reshape((-1,) + (1,) * (len(dims) - 1 - position))
    return level


def noise(stream_key, dims, spread, most, shards=(), held_as=jnp.bfloat16):
    factor_of = levels(stream_key, dims, shards, -0.22, 0.18) if shards else 1.0
    result = jax.random.normal(stream_key, dims, jnp.float32) * spread * factor_of
    return jnp.minimum(jnp.maximum(result, -most), most).astype(held_as)


def setup_inputs(seed: int = 0, part: int = 0) -> dict:
    streams_of = jax.random.split(jax.random.key(seed), 8)
    part_splits = jax.random.split(jax.random.fold_in(streams_of[7], part), 8)
    return {
        "queries": draw_queries(jax.random.fold_in(jax.random.fold_in(streams_of[7], part), 71), part),
        "key_rows": draw_key_rows(jax.random.fold_in(jax.random.fold_in(streams_of[7], part), 71), part),
        "value_rows": noise(part_splits[2], (FRAMES, FRAME_TOKENS, HEADS * HEAD_DIM), 1.0, 6.0, ((0, 4), (1, 2), (2, 2))),
        "list_one": draw_list_one(jax.random.fold_in(jax.random.fold_in(streams_of[7], part), 71), part),
        "list_two": draw_list_two(jax.random.fold_in(jax.random.fold_in(streams_of[7], part), 71), part),
        "list_four": draw_list_four(jax.random.fold_in(jax.random.fold_in(streams_of[7], part), 71), part),
        "tile_counts": draw_tile_counts(jax.random.fold_in(jax.random.fold_in(streams_of[7], part), 71), part),
    }


def attend_one(frame, queries, key_rows, value_rows, list_one, list_two, list_four, tile_counts):
    width = key_rows.shape[2]
    key_tiles = key_rows.reshape(FRAMES, FRAME_TILES, TILE_TOKENS, width)
    value_tiles = value_rows.reshape(FRAMES, FRAME_TILES, TILE_TOKENS, width)
    key_parts = [key_rows[frame]]
    value_parts = [value_rows[frame]]
    live_parts = [jnp.ones((FRAME_TOKENS,), jnp.int32)]
    reaches = ((1, list_one), (2, list_two), (4, list_four))
    for direction in (0, 1):
        for slot_index, (distance, tile_list) in enumerate(reaches):
            source = jnp.clip(frame + (2 * direction - 1) * distance, 0, FRAMES - 1).astype(jnp.int32)
            chosen = tile_list[frame, direction]
            length = chosen.shape[0]
            key_parts.append(key_tiles[source][chosen].reshape(length * TILE_TOKENS, width))
            value_parts.append(value_tiles[source][chosen].reshape(length * TILE_TOKENS, width))
            slot_rank = jnp.arange(length * TILE_TOKENS, dtype=jnp.int32) // TILE_TOKENS
            live_parts.append((slot_rank < tile_counts[frame, direction, slot_index]).astype(jnp.int32))
    key_set = jnp.concatenate(key_parts, axis=0).astype(jnp.float32).reshape(-1, HEADS, HEAD_DIM)
    value_set = jnp.concatenate(value_parts, axis=0).astype(jnp.float32).reshape(-1, HEADS, HEAD_DIM)
    live_slots = jnp.concatenate(live_parts, axis=0)
    query_set = queries[frame].astype(jnp.float32).reshape(FRAME_TOKENS, HEADS, HEAD_DIM)
    score_scale = HEAD_DIM ** -0.5
    scores = jnp.einsum("thd,shd->hts", query_set, key_set, precision=lax.Precision.HIGHEST) * score_scale
    scores = jnp.where(live_slots[None, None, :] > 0, scores, -jnp.inf)
    row_max = jnp.max(scores, axis=2, keepdims=True)
    exponent = jnp.exp(scores - row_max)
    row_total = jnp.sum(exponent, axis=2, keepdims=True)
    rounded = lax.optimization_barrier(exponent.astype(jnp.bfloat16)).astype(jnp.float32)
    mixed_heads = jnp.einsum("hts,shd->htd", rounded, value_set, precision=lax.Precision.HIGHEST) / row_total
    return jnp.transpose(mixed_heads, (1, 0, 2)).reshape(FRAME_TOKENS, width).astype(jnp.bfloat16)


def reference(queries, key_rows, value_rows, list_one, list_two, list_four, tile_counts):
    def per_frame(frame):
        return attend_one(frame, queries, key_rows, value_rows, list_one, list_two, list_four, tile_counts)

    return lax.map(per_frame, jnp.arange(FRAMES, dtype=jnp.int32))
```

```python
import functools
import math

import jax
import jax.numpy as jnp
from jax import lax
from jax.experimental import pallas as pl
from jax.experimental.pallas import tpu as pltpu
from jax.sharding import PartitionSpec as P

HEAD_DIM = 128
TILE = 128
HALF = TILE // 2
DISTANCES = (1, 2, 4)
POSITIONS = sum(d * n for d, n in ((1, 4), (2, 2), (4, 1)))
EARLY = 8
STRIDE = 16
SCALE = math.log2(math.e) / math.sqrt(HEAD_DIM)
LARGE = 2.0**100
NT = (((1,), (1,)), ((), ()))
BF = jnp.bfloat16
F32 = jnp.float32
ANY = pl.BlockSpec(memory_space=pltpu.HBM)
VMEM_LIMIT = 56 * 2**20


class Layout:
    def __init__(self, frames_here, frame_tiles, frames, lengths):
        self.frames_here = frames_here
        self.frame_tiles = frame_tiles
        self.frames = frames
        self.lengths = lengths
        self.row = 2 * (sum(lengths) + 3)
        self.local = 2 * POSITIONS
        self.early = self.local + frames_here * STRIDE
        self.late = self.early + frames_here * STRIDE
        self.need = self.late + frames_here * STRIDE
        self.size = self.need + 1

    def entry(self, frame, direction, column, slot):
        start = 2 * sum(self.lengths[:column])
        return frame * self.row + start + direction * self.lengths[column] + slot

    def count(self, frame, direction, column):
        return frame * self.row + 2 * sum(self.lengths) + direction * 3 + column

    def remote(self, direction):
        found = []
        for away in reversed(range(self.frames_here)):
            for column in reversed(range(3)):
                distance = DISTANCES[column]
                if away < distance:
                    frame = away if direction == 0 else self.frames_here - 1 - away
                    source = frame - distance if direction == 0 else frame + distance
                    found.append((frame, column, source % self.frames_here))
        return found


def table_kernel(lay, place_ref, lists_ref, table_ref, seen_ref):
    first = place_ref[0]
    here = lay.frames_here

    def distinct(target, direction, on_slot, on_new):
        def clear(i, _):
            seen_ref[i] = -1
            return 0

        lax.fori_loop(0, here * lay.frame_tiles, clear, 0)
        used = jnp.int32(0)
        for frame, column, source in lay.remote(direction):
            live = lists_ref[lay.count(target + frame, direction, column)]
            for slot in range(lay.lengths[column]):
                name = lists_ref[lay.entry(target + frame, direction, column, slot)]
                name = name + source * lay.frame_tiles
                alive = slot < live
                known = seen_ref[name]
                fresh = jnp.logical_and(alive, known < 0)
                place = jnp.where(fresh, used, known)
                seen_ref[name] = place
                on_new(used, name)
                on_slot(frame, place, alive)
                used = used + fresh.astype(jnp.int32)
        return used

    def clear_table(i, _):
        table_ref[i] = 0
        return 0

    lax.fori_loop(0, lay.size, clear_table, 0)
    for direction in (0, 1):
        target = first + (here if direction == 0 else -here)
        target = jnp.clip(target, 0, lay.frames - here)

        def note(used, name, direction=direction):
            table_ref[direction * POSITIONS + jnp.minimum(used, POSITIONS - 1)] = name

        last = distinct(target, direction, lambda *_: None, note)
        del last

    def append(base, frame, item, alive):
        at = base + frame * STRIDE
        filled = table_ref[at]
        table_ref[at + 1 + filled] = item
        table_ref[at] = filled + alive.astype(jnp.int32)

    for direction in (0, 1):

        def on_slot(frame, place, alive, direction=direction):
            early = place < EARLY
            append(lay.early, frame, direction * EARLY + place, jnp.logical_and(alive, early))
            late = direction * (POSITIONS - EARLY) + place - EARLY
            append(lay.late, frame, late, jnp.logical_and(alive, jnp.logical_not(early)))

        distinct(first, direction, on_slot, lambda *_: None)
        for frame in range(here):
            for column, distance in enumerate(DISTANCES):
                source = frame + (2 * direction - 1) * distance
                if 0 <= source < here:
                    live = lists_ref[lay.count(first + frame, direction, column)]
                    for slot in range(lay.lengths[column]):
                        name = lists_ref[lay.entry(first + frame, direction, column, slot)]
                        append(lay.local, frame, source * lay.frame_tiles + name, slot < live)


def make_table(lay, place, lists):
    smem = pl.BlockSpec(memory_space=pltpu.SMEM)
    return pl.pallas_call(
        functools.partial(table_kernel, lay),
        in_specs=[smem, smem],
        out_specs=smem,
        out_shape=jax.ShapeDtypeStruct((lay.size,), jnp.int32),
        scratch_shapes=[pltpu.SMEM((lay.frames_here * lay.frame_tiles,), jnp.int32)],
        name="tile_tables",
    )(place, lists)


def pack_kernel(lay, jobs, place_ref, table_ref, *refs):
    sources, outs, sems = refs[:-1 - len(jobs)], refs[-1 - len(jobs) : -1], refs[-1]
    core = place_ref[1]
    tiles_here = lay.frame_tiles // 2
    number = 0
    waits = []
    for (pair, direction, begin, length, lead), out in zip(jobs, outs):
        for item in range(length):
            name = table_ref[direction * POSITIONS + begin + item]
            frame = name // lay.frame_tiles
            tile = name % lay.frame_tiles
            mine = tile // tiles_here == core
            row = pl.multiple_of((tile % tiles_here) * TILE + core * HALF, HALF)
            target = out.at[item] if lead is None else out.at[lead, item]
            own = sources[2 * pair].at[frame, pl.ds(row, HALF), :]
            other = sources[2 * pair + 1].at[frame, pl.ds(row, HALF), :]
            sem = sems.at[number]
            number += 1

            @pl.when(mine)
            def _(own=own, target=target, sem=sem):
                pltpu.make_async_copy(own, target, sem).start()

            @pl.when(jnp.logical_not(mine))
            def _(other=other, target=target, sem=sem):
                pltpu.make_async_copy(other, target, sem).start()

            waits.append((own, target, sem))
    for own, target, sem in waits:
        pltpu.make_async_copy(own, target, sem).wait()


def attend_tiles(q_ref, kbuf, vbuf, ids, m_s, l_s, add, heads):
    for head in range(heads):
        cols = slice(head * HEAD_DIM, (head + 1) * HEAD_DIM)
        keys = jnp.concatenate([kbuf[i, :, cols] for i in ids], axis=0)
        values = jnp.concatenate([vbuf[i, :, cols] for i in ids], axis=0)
        scores = lax.dot_general(q_ref[0, :, cols], keys, NT, preferred_element_type=F32)
        shift = jnp.concatenate([m_s[head]] * len(ids), axis=1)
        weights = jnp.exp2((scores - shift) * SCALE).astype(BF)
        mixed = jnp.dot(
            weights,
            jnp.concatenate([values, jnp.ones_like(values)], axis=1),
            preferred_element_type=F32,
        )
        add(cols, mixed[:, :HEAD_DIM])
        l_s[head] += mixed[:, HEAD_DIM:]


def attend_list(q_ref, kbuf, vbuf, table_ref, base, m_s, l_s, add, heads):
    count = table_ref[base]

    def ids(start, n):
        return [table_ref[base + 1 + start + j] for j in range(n)]

    def four(i, _):
        attend_tiles(q_ref, kbuf, vbuf, ids(4 * i, 4), m_s, l_s, add, heads)
        return 0

    lax.fori_loop(0, count // 4, four, 0)

    @pl.when(count % 4 >= 2)
    def _():
        attend_tiles(q_ref, kbuf, vbuf, ids(count // 4 * 4, 2), m_s, l_s, add, heads)

    @pl.when(count % 2 == 1)
    def _():
        attend_tiles(q_ref, kbuf, vbuf, ids(count - 1, 1), m_s, l_s, add, heads)


def save_stats(stat_ref, m_s, l_s, heads):
    rows = stat_ref.shape[1]
    lane = lax.broadcasted_iota(jnp.int32, (rows, 128), 1)
    stat = jnp.zeros((rows, 128), F32)
    for head in range(heads):
        stat = jnp.where(lane == head, l_s[head], stat)
        stat = jnp.where(lane == 64 + head, m_s[head], stat)
    stat_ref[0] = stat


def load_stats(stat_ref, m_s, l_s, heads):
    rows = stat_ref.shape[1]
    for head in range(heads):
        l_s[head] = jnp.broadcast_to(stat_ref[0, :, head : head + 1], (rows, 128))
        m_s[head] = jnp.broadcast_to(stat_ref[0, :, 64 + head : 65 + head], (rows, 128))


def local_kernel(lay, heads, place_ref, table_ref, q_ref, k_own, k_other, v_own, v_other, acc_ref, stat_ref, kbuf, vbuf, m_s, l_s, sems):
    frame = pl.program_id(0)
    core = place_ref[1]
    here, tiles = lay.frames_here, lay.frame_tiles
    half = tiles // 2

    def copies(index):
        found = []
        for piece, (source, buf, side) in enumerate(
            ((k_own, kbuf, core), (k_other, kbuf, 1 - core), (v_own, vbuf, core), (v_other, vbuf, 1 - core))
        ):
            for tile in range(half):
                found.append(
                    pltpu.make_async_copy(
                        source.at[index, pl.ds(tile * TILE, TILE), :],
                        buf.at[index * tiles + side * half + tile],
                        sems.at[index, piece * half + tile],
                    )
                )
        return found

    @pl.when(frame == 0)
    def _():
        for index in range(here):
            for copy in copies(index):
                copy.start()
        for copy in copies(0):
            copy.wait()

    for head in range(heads):
        cols = slice(head * HEAD_DIM, (head + 1) * HEAD_DIM)
        own = pl.ds(frame * tiles, tiles)
        keys = kbuf[own, :, cols].reshape(tiles * TILE, HEAD_DIM)
        values = vbuf[own, :, cols].reshape(tiles * TILE, HEAD_DIM)
        scores = lax.dot_general(q_ref[0, :, cols], keys, NT, preferred_element_type=F32)
        top = jnp.max(scores, axis=1, keepdims=True)
        weights = jnp.exp2((scores - top) * SCALE).astype(BF)
        mixed = jnp.dot(
            weights,
            jnp.concatenate([values, jnp.ones_like(values)], axis=1),
            preferred_element_type=F32,
        )
        acc_ref[0, :, cols] = mixed[:, :HEAD_DIM]
        l_s[head] = mixed[:, HEAD_DIM:]
        m_s[head] = jnp.broadcast_to(top, m_s.shape[1:])

    @pl.when(frame == 0)
    def _():
        for index in range(1, here):
            for copy in copies(index):
                copy.wait()

    def add(cols, more):
        acc_ref[0, :, cols] += more

    attend_list(q_ref, kbuf, vbuf, table_ref, lay.local + frame * STRIDE, m_s, l_s, add, heads)
    save_stats(stat_ref, m_s, l_s, heads)


def local_call(lay, heads, place, table, queries, k_own, k_other, v_own, v_other):
    here, rows, width = queries.shape
    tiles = lay.frame_tiles
    block = pl.BlockSpec((1, rows, width), lambda f, *_: (f, 0, 0))
    stat = pl.BlockSpec((1, rows, 128), lambda f, *_: (f, 0, 0))
    return pl.pallas_call(
        functools.partial(local_kernel, lay, heads),
        grid_spec=pltpu.PrefetchScalarGridSpec(
            num_scalar_prefetch=2,
            grid=(here,),
            in_specs=[block, ANY, ANY, ANY, ANY],
            out_specs=[block, stat],
            scratch_shapes=[
                pltpu.VMEM((here * tiles, TILE, width), BF),
                pltpu.VMEM((here * tiles, TILE, width), BF),
                pltpu.VMEM((heads, rows, 128), F32),
                pltpu.VMEM((heads, rows, 128), F32),
                pltpu.SemaphoreType.DMA((here, 2 * tiles)),
            ],
        ),
        out_shape=[
            jax.ShapeDtypeStruct((here, rows, width), F32),
            jax.ShapeDtypeStruct((here, rows, 128), F32),
        ],
        compiler_params=pltpu.CompilerParams(vmem_limit_bytes=VMEM_LIMIT),
        cost_estimate=cost(here * rows * heads * 16 * TILE),
        name="attend_local",
    )(place, table, queries, k_own, k_other, v_own, v_other)


def cost(scores):
    return pl.CostEstimate(flops=scores * 4 * HEAD_DIM, bytes_accessed=scores // 8, transcendentals=scores)


def exact_frame(lay, heads, frame, core, table_ref, q_ref, local, received, acc_s, m_s, l_s, tk, tv, sems):
    tiles = lay.frame_tiles
    half = tiles // 2
    m_s[...] = jnp.full(m_s.shape, -jnp.inf, F32)
    l_s[...] = jnp.zeros(l_s.shape, F32)
    acc_s[...] = jnp.zeros(acc_s.shape, F32)

    def fetch(pairs):
        found = [pltpu.make_async_copy(a, b, sems.at[i]) for i, (a, b) in enumerate(pairs)]
        for copy in found:
            copy.start()
        for copy in found:
            copy.wait()

    def tile_step():
        for head in range(heads):
            cols = slice(head * HEAD_DIM, (head + 1) * HEAD_DIM)
            scores = lax.dot_general(q_ref[0, :, cols], tk[:, cols], NT, preferred_element_type=F32)
            before = m_s[head]
            top = jnp.maximum(before, jnp.max(scores, axis=1, keepdims=True))
            fade = jnp.exp2((before - top) * SCALE)
            weights = jnp.exp2((scores - top) * SCALE).astype(BF)
            values = tv[:, cols]
            mixed = jnp.dot(
                weights,
                jnp.concatenate([values, jnp.ones_like(values)], axis=1),
                preferred_element_type=F32,
            )
            acc_s[:, cols] = acc_s[:, cols] * fade + mixed[:, :HEAD_DIM]
            l_s[head] = l_s[head] * fade + mixed[:, HEAD_DIM:]
            m_s[head] = top

    def local_tile(name):
        source, tile = name // tiles, name % tiles
        rows = pl.ds(pl.multiple_of(tile % half * TILE, TILE), TILE)
        mine = tile // half == core

        @pl.when(mine)
        def _():
            fetch(((local[0].at[source, rows, :], tk), (local[2].at[source, rows, :], tv)))

        @pl.when(jnp.logical_not(mine))
        def _():
            fetch(((local[1].at[source, rows, :], tk), (local[3].at[source, rows, :], tv)))

        tile_step()

    def own_step(i, _):
        local_tile(frame * tiles + i)
        return 0

    def list_step(i, _):
        local_tile(table_ref[lay.local + frame * STRIDE + 1 + i])
        return 0

    lax.fori_loop(0, tiles, own_step, 0)
    lax.fori_loop(0, table_ref[lay.local + frame * STRIDE], list_step, 0)
    mine = pl.ds(pl.multiple_of(core * HALF, HALF), HALF)
    others = pl.ds(pl.multiple_of((1 - core) * HALF, HALF), HALF)
    for base, length, pieces in received:

        def far_step(i, _, base=base, length=length, pieces=pieces):
            item = table_ref[base + frame * STRIDE + 1 + i]
            for direction in (0, 1):

                @pl.when(item // length == direction)
                def _():
                    at = item % length
                    fetch(
                        tuple(
                            (pieces(direction, kv, side, at), buf.at[rows, :])
                            for kv, buf in enumerate((tk, tv))
                            for side, rows in enumerate((mine, others))
                        )
                    )

            tile_step()
            return 0

        lax.fori_loop(0, table_ref[base + frame * STRIDE], far_step, 0)


def finish(out_ref, acc_s, l_s, heads):
    for head in range(heads):
        cols = slice(head * HEAD_DIM, (head + 1) * HEAD_DIM)
        out_ref[0, :, cols] = (acc_s[:, cols] / l_s[head]).astype(out_ref.dtype)


def early_piece(refs, direction, kv, side, at):
    return refs[4 * kv + 2 * side + direction].at[at]


def late_piece(refs, direction, kv, side, at):
    return refs[2 * side + direction].at[kv, at]


def far_kernel(lay, heads, final, place_ref, table_ref, q_ref, acc_ref, stat_ref, *refs):
    here = lay.frames_here
    core = place_ref[1]
    local = refs[:4]
    early_refs = refs[4:12]
    refs = refs[12:]
    received = [(lay.early, EARLY, functools.partial(early_piece, early_refs))]
    length = EARLY
    base = lay.early
    if final:
        late_refs = refs[:4]
        refs = refs[5:]
        length = POSITIONS - EARLY
        base = lay.late
        received.append((lay.late, length, functools.partial(late_piece, late_refs)))
        out_ref, kbuf, vbuf, acc_s, m_s, l_s, tk, tv, sems = refs
    else:
        out_ref, acc_out, stat_out, kbuf, vbuf, acc_s, m_s, l_s, tk, tv, sems = refs
    piece = received[-1][2]
    step = pl.program_id(0)
    frame = step * (here - 1) if final else step
    rows_of = [pl.ds(pl.multiple_of(s * HALF, HALF), HALF) for s in (core, 1 - core)]

    def copies():
        found = []
        for kv, buf in enumerate((kbuf, vbuf)):
            for side in (0, 1):
                for direction in (0, 1):
                    for at in range(length):
                        found.append(
                            pltpu.make_async_copy(
                                piece(direction, kv, side, at),
                                buf.at[direction * length + at, rows_of[side], :],
                                sems.at[len(found)],
                            )
                        )
        return found

    @pl.when(step == 0)
    def _():
        for copy in copies():
            copy.start()

    load_stats(stat_ref, m_s, l_s, heads)
    acc_s[...] = acc_ref[0]

    @pl.when(step == 0)
    def _():
        for copy in copies():
            copy.wait()

    def add(cols, more):
        acc_s[:, cols] += more

    attend_list(q_ref, kbuf, vbuf, table_ref, base + frame * STRIDE, m_s, l_s, add, heads)

    def end():
        @pl.when(jnp.max(l_s[...]) > LARGE)
        def _():
            exact_frame(lay, heads, frame, core, table_ref, q_ref, local, received, acc_s, m_s, l_s, tk, tv, sems)

        finish(out_ref, acc_s, l_s, heads)

    if final:
        end()
    else:
        edge = jnp.logical_or(frame == 0, frame == here - 1)

        @pl.when(jnp.logical_not(edge))
        def _():
            end()

        @pl.when(edge)
        def _():
            acc_out[0] = acc_s[...]
            save_stats(stat_out, m_s, l_s, heads)


def far_call(lay, heads, final, place, table, queries, acc, stats, local, early, late=(), partial_out=None):
    here, rows, width = queries.shape
    steps = 2 if final else here
    index = (lambda s, *_: (s * (here - 1), 0, 0)) if final else (lambda s, *_: (s, 0, 0))
    block = pl.BlockSpec((1, rows, width), index)
    stat = pl.BlockSpec((1, rows, 128), index)
    length = POSITIONS - EARLY if final else EARLY
    anys = [*local, *early, *late] + ([partial_out] if final else [])
    out_shape = [jax.ShapeDtypeStruct((here, rows, width), BF)]
    out_specs = [block]
    aliases = {}
    if final:
        aliases = {5 + len(anys) - 1: 0}
    else:
        out_shape += [jax.ShapeDtypeStruct(acc.shape, F32), jax.ShapeDtypeStruct(stats.shape, F32)]
        out_specs += [block, stat]
        aliases = {3: 1, 4: 2}
    return pl.pallas_call(
        functools.partial(far_kernel, lay, heads, final),
        grid_spec=pltpu.PrefetchScalarGridSpec(
            num_scalar_prefetch=2,
            grid=(steps,),
            in_specs=[block, block, stat] + [ANY] * len(anys),
            out_specs=out_specs,
            scratch_shapes=[
                pltpu.VMEM((2 * length, TILE, width), BF),
                pltpu.VMEM((2 * length, TILE, width), BF),
                pltpu.VMEM((rows, width), F32),
                pltpu.VMEM((heads, rows, 128), F32),
                pltpu.VMEM((heads, rows, 128), F32),
                pltpu.VMEM((TILE, width), BF),
                pltpu.VMEM((TILE, width), BF),
                pltpu.SemaphoreType.DMA((8 * length,)),
            ],
        ),
        out_shape=out_shape,
        input_output_aliases=aliases,
        compiler_params=pltpu.CompilerParams(vmem_limit_bytes=VMEM_LIMIT),
        cost_estimate=cost(steps * rows * heads * 4 * TILE),
        name="attend_late" if final else "attend_early",
    )(place, table, queries, acc, stats, *anys)


def pack_call(lay, jobs, place, table, sources, shapes):
    return pl.pallas_call(
        functools.partial(pack_kernel, lay, jobs),
        in_specs=[pl.BlockSpec(memory_space=pltpu.SMEM)] * 2 + [ANY] * len(sources),
        out_specs=[ANY] * len(shapes),
        out_shape=[jax.ShapeDtypeStruct(s, BF) for s in shapes],
        scratch_shapes=[pltpu.SemaphoreType.DMA((sum(j[3] for j in jobs),))],
        name="pack_tiles",
    )(place, table, *sources)


def shifted(block, axis, step):
    devices = range(lax.axis_size(axis))
    return lax.ppermute(block, axis, [(i, i + step) for i in devices if i + step in devices])


def swapped(block):
    return lax.ppermute(block, "seq", [(0, 1), (1, 0)])


def per_device(queries, key_rows, value_rows, list_one, list_two, list_four, tile_counts):
    here, rows, width = queries.shape
    heads = width // HEAD_DIM
    frames = list_one.shape[0]
    lay = Layout(here, 2 * rows // TILE, frames, (list_one.shape[2], list_two.shape[2], list_four.shape[2]))
    place = jnp.stack([lax.axis_index("frame") * here, lax.axis_index("seq")]).astype(jnp.int32)
    lists = jnp.concatenate(
        [a.reshape(frames, -1) for a in (list_one, list_two, list_four, tile_counts)], axis=1
    ).reshape(-1)

    k_other = swapped(key_rows)
    v_other = swapped(value_rows)
    table = make_table(lay, place, lists)
    late = POSITIONS - EARLY
    one = (EARLY, HALF, width)
    k_up, k_down = pack_call(
        lay, [(0, 0, 0, EARLY, None), (0, 1, 0, EARLY, None)], place, table, (key_rows, k_other), (one, one)
    )
    far_k = (shifted(k_up, "frame", 1), shifted(k_down, "frame", -1))
    v_up, v_down = pack_call(
        lay, [(0, 0, 0, EARLY, None), (0, 1, 0, EARLY, None)], place, table, (value_rows, v_other), (one, one)
    )
    far_v = (shifted(v_up, "frame", 1), shifted(v_down, "frame", -1))
    two = (2, late, HALF, width)
    late_up, late_down = late_pack(lay, place, table, (key_rows, k_other, value_rows, v_other), two)
    far_late = (shifted(late_up, "frame", 1), shifted(late_down, "frame", -1))

    local = (key_rows, k_other, value_rows, v_other)
    acc, stats = local_call(lay, heads, place, table, queries, *local)
    early = (*far_k, *map(swapped, far_k), *far_v, *map(swapped, far_v))
    out, acc, stats = far_call(lay, heads, False, place, table, queries, acc, stats, local, early)
    late_all = (*far_late, *map(swapped, far_late))
    (out,) = far_call(lay, heads, True, place, table, queries, acc, stats, local, early, late_all, out)
    return out


def late_pack_kernel(lay, late, place_ref, table_ref, k_own, k_other, v_own, v_other, up, down, sems):
    jobs = []
    refs = []
    for direction, out in ((0, up), (1, down)):
        for kv in (0, 1):
            jobs.append((kv, direction, EARLY, late, kv))
            refs.append(out)
    pack_kernel(lay, jobs, place_ref, table_ref, k_own, k_other, v_own, v_other, *refs, sems)


def late_pack(lay, place, table, sources, shape):
    late = shape[1]
    return pl.pallas_call(
        functools.partial(late_pack_kernel, lay, late),
        in_specs=[pl.BlockSpec(memory_space=pltpu.SMEM)] * 2 + [ANY] * 4,
        out_specs=[ANY] * 2,
        out_shape=[jax.ShapeDtypeStruct(shape, BF)] * 2,
        scratch_shapes=[pltpu.SemaphoreType.DMA((4 * late,))],
        name="pack_late",
    )(place, table, *sources)


def solution(mesh):
    placed = (
        P(("clips", "frame"), "seq", "head"),
        P(("clips", "frame"), "seq", "head"),
        P(("clips", "frame"), "seq", "head"),
        P("clips", None, None),
        P("clips", None, None),
        P("clips", None, None),
        P("clips", None, None),
    )
    return jax.shard_map(
        per_device,
        mesh=mesh,
        in_specs=placed,
        out_specs=P(("clips", "frame"), "seq", "head"),
        check_vma=False,
    )
```

```python
import functools
import math

import jax
import jax.numpy as jnp
from jax import lax
from jax.experimental import pallas as pl
from jax.experimental.pallas import tpu as pltpu
from jax.sharding import PartitionSpec as P

HEAD_DIM = 128
TILE = 128
HALF = TILE // 2
DISTANCES = (1, 2, 4)
STRIDE = 24
SCALE = math.log2(math.e) / math.sqrt(HEAD_DIM)
LARGE = 2.0**100
NT = (((1,), (1,)), ((), ()))
BF = jnp.bfloat16
F32 = jnp.float32
ANY = pl.BlockSpec(memory_space=pl.ANY)
SMEM = pl.BlockSpec(memory_space=pltpu.SMEM)
VMEM_LIMIT = 56 * 2**20


class Layout:
    def __init__(self, frames_here, frame_tiles, frames, lengths):
        self.here = frames_here
        self.tiles = frame_tiles
        self.half = frame_tiles // 2
        self.own = frames_here * frame_tiles
        self.frames = frames
        self.lengths = lengths
        self.early = self.late = 0
        for frame, column, _ in self.remote(0):
            if self.edge(frame):
                self.late += lengths[column]
            else:
                self.early += lengths[column]
        self.places = self.early + self.late
        self.near = 2 * self.places
        self.far = self.near + frames_here * STRIDE
        self.size = self.far + frames_here * STRIDE

    def edge(self, frame):
        return frame in (0, self.here - 1)

    def remote(self, direction):
        found = []
        for away in (*range(1, self.here - 1), self.here - 1, 0):
            for column in reversed(range(3)):
                distance = DISTANCES[column]
                if away < distance:
                    frame = away if direction == 0 else self.here - 1 - away
                    source = frame - distance if direction == 0 else frame + distance
                    found.append((frame, column, source % self.here))
        return found


def table_kernel(lay, place_ref, one_ref, two_ref, four_ref, count_ref, table_ref, seen_ref):
    lists = (one_ref, two_ref, four_ref)
    first = place_ref[0]

    def distinct(target, direction, on_slot, on_new):
        for i in range(lay.own):
            seen_ref[i] = -1
        used = jnp.int32(0)
        for frame, column, source in lay.remote(direction):
            live = count_ref[column, direction, target + frame]
            for slot in range(lay.lengths[column]):
                name = lists[column][direction, slot, target + frame] + source * lay.tiles
                alive = slot < live
                known = seen_ref[name]
                fresh = jnp.logical_and(alive, known < 0)
                place = jnp.where(fresh, used, known)
                seen_ref[name] = place
                on_new(used, name)
                on_slot(frame, place, alive)
                used = used + fresh.astype(jnp.int32)
        return used

    filled = {}

    def append(base, frame, item, alive):
        at = base + frame * STRIDE
        count = filled.get(at, jnp.int32(0))
        table_ref[at + 1 + count] = item
        filled[at] = count + alive.astype(jnp.int32)

    for direction in (0, 1):
        target = first + (lay.here if direction == 0 else -lay.here)
        target = jnp.clip(target, 0, lay.frames - lay.here)
        for place in range(lay.places):
            table_ref[direction * lay.places + place] = 0

        def note(used, name, direction=direction):
            table_ref[direction * lay.places + jnp.minimum(used, lay.places - 1)] = name

        distinct(target, direction, lambda *_: None, note)

    for direction in (0, 1):

        def on_slot(frame, place, alive, direction=direction):
            if lay.edge(frame):
                append(lay.far, frame, direction * lay.places + place, alive)
            else:
                append(lay.near, frame, lay.own + direction * lay.early + place, alive)

        distinct(first, direction, on_slot, lambda *_: None)
        for frame in range(lay.here):
            for column, distance in enumerate(DISTANCES):
                source = frame + (2 * direction - 1) * distance
                if 0 <= source < lay.here:
                    live = count_ref[column, direction, first + frame]
                    for slot in range(lay.lengths[column]):
                        name = lists[column][direction, slot, first + frame]
                        append(lay.near, frame, source * lay.tiles + name, slot < live)
    for frame in range(lay.here):
        for base in (lay.near, lay.far):
            at = base + frame * STRIDE
            table_ref[at] = filled.get(at, jnp.int32(0))


def make_table(lay, place, lists):
    return pl.pallas_call(
        functools.partial(table_kernel, lay),
        in_specs=[SMEM] * 5,
        out_specs=SMEM,
        out_shape=jax.ShapeDtypeStruct((lay.size,), jnp.int32),
        scratch_shapes=[pltpu.SMEM((lay.own,), jnp.int32)],
        compiler_params=pltpu.CompilerParams(vmem_limit_bytes=VMEM_LIMIT),
        name="tile_tables",
    )(place, *lists)


def pack_kernel(lay, begin, length, place_ref, table_ref, k_own, k_sent, v_own, v_sent, up, down, sems):
    core = place_ref[1]
    waits = []
    for direction, out in ((0, up), (1, down)):
        for item in range(length):
            name = table_ref[direction * lay.places + begin + item]
            frame = name // lay.tiles
            tile = name % lay.tiles
            mine = tile // lay.half == core
            tile = tile % lay.half
            for kv, (own, sent) in enumerate(((k_own, k_sent), (v_own, v_sent))):
                target = out.at[kv, item]
                sem = sems.at[len(waits)]
                here = pltpu.make_async_copy(own.at[frame, tile, core], target, sem)
                there = pltpu.make_async_copy(sent.at[frame, tile], target, sem)
                pl.when(mine)(here.start)
                pl.when(jnp.logical_not(mine))(there.start)
                waits.append(here)
    for copy in waits:
        copy.wait()


def pack_call(lay, begin, length, place, table, sources):
    width = sources[0].shape[-1]
    shape = jax.ShapeDtypeStruct((2, length, HALF, width), BF)
    return pl.pallas_call(
        functools.partial(pack_kernel, lay, begin, length),
        in_specs=[SMEM] * 2 + [ANY] * 4,
        out_specs=[pl.BlockSpec(memory_space=pltpu.VMEM)] * 2,
        out_shape=[shape] * 2,
        scratch_shapes=[pltpu.SemaphoreType.DMA((4 * length,))],
        compiler_params=pltpu.CompilerParams(vmem_limit_bytes=VMEM_LIMIT),
        name="pack_tiles",
    )(place, table, *sources)


def rows_of(buf, index, cols):
    tiles = buf[index, :, :, cols]
    return tiles.reshape(tiles.size // HEAD_DIM, HEAD_DIM)


def mix(weights, values):
    return jnp.dot(
        weights.astype(BF),
        jnp.concatenate([values, jnp.ones_like(values)], axis=1),
        preferred_element_type=F32,
    )


def attend_tiles(q_ref, kbuf, vbuf, ids, m_s, l_s, acc_s, heads):
    for head in range(heads):
        cols = slice(head * HEAD_DIM, (head + 1) * HEAD_DIM)
        keys = jnp.concatenate([rows_of(kbuf, i, cols) for i in ids], axis=0)
        values = jnp.concatenate([rows_of(vbuf, i, cols) for i in ids], axis=0)
        scores = lax.dot_general(q_ref[0, :, cols], keys, NT, preferred_element_type=F32)
        shift = jnp.concatenate([m_s[head]] * len(ids), axis=1)
        mixed = mix(jnp.exp2((scores - shift) * SCALE), values)
        acc_s[:, cols] += mixed[:, :HEAD_DIM]
        l_s[head] += mixed[:, HEAD_DIM:]


def attend_list(q_ref, kbuf, vbuf, table_ref, base, m_s, l_s, acc_s, heads):
    count = table_ref[base]

    def add(start, n):
        ids = [table_ref[base + 1 + start + j] for j in range(n)]
        attend_tiles(q_ref, kbuf, vbuf, ids, m_s, l_s, acc_s, heads)

    def four(i, _):
        add(4 * i, 4)
        return 0

    lax.fori_loop(0, count // 4, four, 0)

    @pl.when(count % 4 >= 2)
    def _():
        add(count // 4 * 4, 2)

    @pl.when(count % 2 == 1)
    def _():
        add(count - 1, 1)


def attend_own(lay, q_ref, kbuf, vbuf, frame, m_s, l_s, acc_s, heads):
    for head in range(heads):
        cols = slice(head * HEAD_DIM, (head + 1) * HEAD_DIM)
        own = pl.ds(frame * lay.tiles, lay.tiles)
        scores = lax.dot_general(
            q_ref[0, :, cols], rows_of(kbuf, own, cols), NT, preferred_element_type=F32
        )
        top = jnp.max(scores[:, :TILE], axis=1, keepdims=True)
        mixed = mix(jnp.exp2((scores - top) * SCALE), rows_of(vbuf, own, cols))
        acc_s[:, cols] = mixed[:, :HEAD_DIM]
        l_s[head] = mixed[:, HEAD_DIM:]
        m_s[head] = jnp.broadcast_to(top, m_s.shape[1:])


def save_stats(stat_ref, m_s, l_s, heads):
    rows = stat_ref.shape[1]
    lane = lax.broadcasted_iota(jnp.int32, (rows, 128), 1)
    stat = jnp.zeros((rows, 128), F32)
    for head in range(heads):
        stat = jnp.where(lane == head, l_s[head], stat)
        stat = jnp.where(lane == 64 + head, m_s[head], stat)
    stat_ref[0] = stat


def load_stats(stat_ref, m_s, l_s, heads):
    rows = stat_ref.shape[1]
    for head in range(heads):
        l_s[head] = jnp.broadcast_to(stat_ref[0, :, head : head + 1], (rows, 128))
        m_s[head] = jnp.broadcast_to(stat_ref[0, :, 64 + head : 65 + head], (rows, 128))


def finish(out_ref, acc_s, l_s, heads):
    for head in range(heads):
        cols = slice(head * HEAD_DIM, (head + 1) * HEAD_DIM)
        out_ref[0, :, cols] = (acc_s[:, cols] / l_s[head]).astype(out_ref.dtype)


def local_copies(lay, index, core, local, bufs, sems):
    found = []
    for kv, (buf, (own, sent, kept)) in enumerate(zip(bufs, (local[:3], local[3:]))):
        mine = pl.ds(index * lay.tiles + core * lay.half, lay.half)
        others = pl.ds(index * lay.tiles + (1 - core) * lay.half, lay.half)
        for piece, (source, target) in enumerate(
            ((own, buf.at[mine]), (sent, buf.at[others, core]), (kept, buf.at[others, 1 - core]))
        ):
            found.append(pltpu.make_async_copy(source.at[index], target, sems.at[index, 3 * kv + piece]))
    return found


def far_copies(core, parts, bufs, begins, sems):
    found = []
    for part, begin in zip(parts, begins):
        length = part[0].shape[1]
        for side in (0, 1):
            for direction in (0, 1):
                for kv in (0, 1):
                    target = bufs[kv].at[
                        pl.ds(begin[direction], length), core if side == 0 else 1 - core
                    ]
                    source = part[2 * side + direction].at[kv]
                    found.append(pltpu.make_async_copy(source, target, sems.at[len(found)]))
    return found


def exact_frame(lay, heads, frame, core, table_ref, q_ref, local, parts, acc_s, m_s, l_s, tk, tv, sems):
    m_s[...] = jnp.full(m_s.shape, -jnp.inf, F32)
    l_s[...] = jnp.zeros(l_s.shape, F32)
    acc_s[...] = jnp.zeros(acc_s.shape, F32)

    def fetch(*pairs):
        found = [pltpu.make_async_copy(a, b, sems.at[i]) for i, (a, b) in enumerate(pairs)]
        for copy in found:
            copy.start()
        for copy in found:
            copy.wait()

    def add_tile():
        for head in range(heads):
            cols = slice(head * HEAD_DIM, (head + 1) * HEAD_DIM)
            keys, values = (t[:, :, cols].reshape(TILE, HEAD_DIM) for t in (tk, tv))
            scores = lax.dot_general(q_ref[0, :, cols], keys, NT, preferred_element_type=F32)
            before = m_s[head]
            top = jnp.maximum(before, jnp.max(scores, axis=1, keepdims=True))
            fade = jnp.exp2((before - top) * SCALE)
            mixed = mix(jnp.exp2((scores - top) * SCALE), values)
            acc_s[:, cols] = acc_s[:, cols] * fade + mixed[:, :HEAD_DIM]
            l_s[head] = l_s[head] * fade + mixed[:, HEAD_DIM:]
            m_s[head] = top

    def near_tile(name):
        source, tile = name // lay.tiles, name % lay.tiles
        mine = tile // lay.half == core
        tile = tile % lay.half
        k_own, k_sent, k_kept, v_own, v_sent, v_kept = (ref.at[source, tile] for ref in local)

        @pl.when(mine)
        def _():
            fetch((k_own, tk), (v_own, tv))

        @pl.when(jnp.logical_not(mine))
        def _():
            fetch(
                (k_sent, tk.at[core]),
                (k_kept, tk.at[1 - core]),
                (v_sent, tv.at[core]),
                (v_kept, tv.at[1 - core]),
            )

    def far_tile(direction, part, item):
        up, other = part[direction], part[2 + direction]
        fetch(
            (up.at[0, item], tk.at[core]),
            (other.at[0, item], tk.at[1 - core]),
            (up.at[1, item], tv.at[core]),
            (other.at[1, item], tv.at[1 - core]),
        )

    def far_places(item, length):
        begin = 0
        for part in parts:
            size = part[0].shape[1]
            for direction in (0, 1):
                at = item - direction * length - begin

                @pl.when(jnp.logical_and(at >= 0, at < size))
                def _(direction=direction, part=part, at=at):
                    far_tile(direction, part, at)

            begin += size

    def own_step(i, _):
        near_tile(frame * lay.tiles + i)
        add_tile()
        return 0

    def near_step(i, _):
        name = table_ref[lay.near + frame * STRIDE + 1 + i]

        @pl.when(name < lay.own)
        def _():
            near_tile(name)

        @pl.when(name >= lay.own)
        def _():
            far_places(name - lay.own, lay.early)

        add_tile()
        return 0

    def far_step(i, _):
        far_places(table_ref[lay.far + frame * STRIDE + 1 + i], lay.places)
        add_tile()
        return 0

    lax.fori_loop(0, lay.tiles, own_step, 0)
    lax.fori_loop(0, table_ref[lay.near + frame * STRIDE], near_step, 0)
    lax.fori_loop(0, table_ref[lay.far + frame * STRIDE], far_step, 0)


def near_kernel(lay, heads, whole, place_ref, table_ref, q_ref, *refs):
    local, refs = refs[:6], refs[6:]
    parts = ()
    if whole:
        parts, refs = (refs[:4],), refs[4:]
        out_ref, acc_s, kbuf, vbuf, m_s, l_s, sems, tk, tv, far_sems = refs
    else:
        acc_out, stat_ref, kbuf, vbuf, m_s, l_s, sems = refs
        acc_s = acc_out.at[0]
    core = place_ref[1]
    step = pl.program_id(0)
    frame = step + 1 if whole else step * (lay.here - 1)
    begin = 1 if whole else 0

    def copies(index):
        return local_copies(lay, index, core, local, (kbuf, vbuf), sems)

    def far():
        return far_copies(core, parts, (kbuf, vbuf), [(lay.own, lay.own + lay.early)] * len(parts), far_sems)

    order = [begin] + [i for i in range(lay.here) if i != begin]

    @pl.when(step == 0)
    def _():
        for index in order:
            for copy in copies(index):
                copy.start()
        if whole:
            for copy in far():
                copy.start()
        for copy in copies(begin):
            copy.wait()

    attend_own(lay, q_ref, kbuf, vbuf, frame, m_s, l_s, acc_s, heads)

    @pl.when(step == 0)
    def _():
        for index in order[1:]:
            for copy in copies(index):
                copy.wait()
        if whole:
            for copy in far():
                copy.wait()

    attend_list(q_ref, kbuf, vbuf, table_ref, lay.near + frame * STRIDE, m_s, l_s, acc_s, heads)
    if whole:

        @pl.when(jnp.max(l_s[...]) > LARGE)
        def _():
            exact_frame(lay, heads, frame, core, table_ref, q_ref, local, parts, acc_s, m_s, l_s, tk, tv, far_sems)

        finish(out_ref, acc_s, l_s, heads)
    else:
        save_stats(stat_ref, m_s, l_s, heads)


def cost(scores):
    return pl.CostEstimate(flops=scores * 4 * HEAD_DIM, bytes_accessed=scores // 8, transcendentals=scores)


def near_call(lay, heads, whole, place, table, queries, local, early=()):
    here, rows, width = queries.shape
    steps = here - 2 if whole else 2
    index = (lambda s, *_: (s + 1, 0, 0)) if whole else (lambda s, *_: (s * (here - 1), 0, 0))
    block = pl.BlockSpec((1, rows, width), index)
    count = lay.own + (2 * lay.early if whole else 0)
    bufs = [pltpu.VMEM((count, 2, HALF, width), BF)] * 2
    sums = [pltpu.VMEM((heads, rows, 128), F32)] * 2
    sems = [pltpu.SemaphoreType.DMA((here, 6))]
    if whole:
        out_specs = [block]
        out_shape = [jax.ShapeDtypeStruct((here, rows, width), BF)]
        scratch = [pltpu.VMEM((rows, width), F32), *bufs, *sums, *sems]
        scratch += [pltpu.VMEM((2, HALF, width), BF)] * 2 + [pltpu.SemaphoreType.DMA((8,))]
    else:
        out_specs = [
            pl.BlockSpec((1, rows, width), lambda s, *_: (s, 0, 0)),
            pl.BlockSpec((1, rows, 128), lambda s, *_: (s, 0, 0)),
        ]
        out_shape = [jax.ShapeDtypeStruct((2, rows, n), F32) for n in (width, 128)]
        scratch = [*bufs, *sums, *sems]
    return pl.pallas_call(
        functools.partial(near_kernel, lay, heads, whole),
        grid_spec=pltpu.PrefetchScalarGridSpec(
            num_scalar_prefetch=2,
            grid=(steps,),
            in_specs=[block] + [ANY] * (6 + len(early)),
            out_specs=out_specs,
            scratch_shapes=scratch,
        ),
        out_shape=out_shape,
        compiler_params=pltpu.CompilerParams(vmem_limit_bytes=VMEM_LIMIT),
        cost_estimate=cost(steps * rows * heads * 16 * TILE),
        name="attend_middle" if whole else "attend_edges",
    )(place, table, queries, *local, *early)


def far_kernel(lay, heads, place_ref, table_ref, q_ref, acc_ref, stat_ref, *refs):
    local, parts = refs[:6], (refs[6:10], refs[10:14])
    out_ref, kbuf, vbuf, acc_s, m_s, l_s, tk, tv, sems = refs[15:]
    step = pl.program_id(0)
    frame = step * (lay.here - 1)
    core = place_ref[1]

    def copies():
        begins = [(0, lay.places), (lay.early, lay.places + lay.early)]
        return far_copies(core, parts, (kbuf, vbuf), begins, sems)

    @pl.when(step == 0)
    def _():
        for copy in copies():
            copy.start()

    load_stats(stat_ref, m_s, l_s, heads)
    acc_s[...] = acc_ref[0]

    @pl.when(step == 0)
    def _():
        for copy in copies():
            copy.wait()

    attend_list(q_ref, kbuf, vbuf, table_ref, lay.far + frame * STRIDE, m_s, l_s, acc_s, heads)

    @pl.when(jnp.max(l_s[...]) > LARGE)
    def _():
        exact_frame(lay, heads, frame, core, table_ref, q_ref, local, parts, acc_s, m_s, l_s, tk, tv, sems)

    finish(out_ref, acc_s, l_s, heads)


def far_call(lay, heads, place, table, queries, acc, stats, local, early, late, out):
    here, rows, width = queries.shape
    block = pl.BlockSpec((1, rows, width), lambda s, *_: (s * (here - 1), 0, 0))
    anys = [*local, *early, *late, out]
    return pl.pallas_call(
        functools.partial(far_kernel, lay, heads),
        grid_spec=pltpu.PrefetchScalarGridSpec(
            num_scalar_prefetch=2,
            grid=(2,),
            in_specs=[
                block,
                pl.BlockSpec((1, rows, width), lambda s, *_: (s, 0, 0)),
                pl.BlockSpec((1, rows, 128), lambda s, *_: (s, 0, 0)),
            ]
            + [ANY] * len(anys),
            out_specs=block,
            scratch_shapes=[
                pltpu.VMEM((2 * lay.places, 2, HALF, width), BF),
                pltpu.VMEM((2 * lay.places, 2, HALF, width), BF),
                pltpu.VMEM((rows, width), F32),
                pltpu.VMEM((heads, rows, 128), F32),
                pltpu.VMEM((heads, rows, 128), F32),
                pltpu.VMEM((2, HALF, width), BF),
                pltpu.VMEM((2, HALF, width), BF),
                pltpu.SemaphoreType.DMA((16,)),
            ],
        ),
        out_shape=jax.ShapeDtypeStruct((here, rows, width), BF),
        input_output_aliases={5 + len(anys) - 1: 0},
        compiler_params=pltpu.CompilerParams(vmem_limit_bytes=VMEM_LIMIT),
        cost_estimate=cost(2 * rows * heads * 7 * TILE),
        name="attend_late",
    )(place, table, queries, acc, stats, *anys)


def shifted(block, axis, step):
    devices = range(lax.axis_size(axis))
    return lax.ppermute(block, axis, [(i, i + step) for i in devices if i + step in devices])


def swapped(block):
    return lax.ppermute(block, "seq", [(0, 1), (1, 0)])


def per_device(queries, key_rows, value_rows, list_one, list_two, list_four, tile_counts):
    here, rows, width = queries.shape
    heads = width // HEAD_DIM
    frames = list_one.shape[0]
    lists = (list_one, list_two, list_four)
    lay = Layout(here, 2 * rows // TILE, frames, tuple(a.shape[2] for a in lists))
    core = lax.axis_index("seq")
    place = jnp.stack([lax.axis_index("frame") * here, core]).astype(jnp.int32)

    k_own, v_own = (a.reshape(here, lay.half, 2, HALF, width) for a in (key_rows, value_rows))
    k_sent, v_sent = (
        swapped(lax.dynamic_index_in_dim(a, 1 - core, 2, keepdims=False)) for a in (k_own, v_own)
    )
    by_frame = [jnp.transpose(a, (1, 2, 0)) for a in lists] + [jnp.transpose(tile_counts, (2, 1, 0))]
    table = make_table(lay, place, by_frame)
    k_kept, v_kept = (
        swapped(lax.dynamic_index_in_dim(a, core, 2, keepdims=False)) for a in (k_own, v_own)
    )

    sources = (k_own, k_sent, v_own, v_sent)
    early = pack_call(lay, 0, lay.early, place, table, sources)
    early, then = lax.optimization_barrier((early, table))
    early = (shifted(early[0], "frame", 1), shifted(early[1], "frame", -1))
    late = pack_call(lay, lay.early, lay.late, place, then, sources)
    late, k_kept = lax.optimization_barrier((late, k_kept))
    late = (shifted(late[0], "frame", 1), shifted(late[1], "frame", -1))

    local = (k_own, k_sent, k_kept, v_own, v_sent, v_kept)
    acc, stats = near_call(lay, heads, False, place, table, queries, local)
    early, stats = lax.optimization_barrier((early, stats))
    early = (*early, *map(swapped, early))
    (out,) = near_call(lay, heads, True, place, table, queries, local, early)
    late, out = lax.optimization_barrier((late, out))
    late = (*late, *map(swapped, late))
    return far_call(lay, heads, place, table, queries, acc, stats, local, early, late, out)


def solution(mesh):
    placed = (
        P(("clips", "frame"), "seq", "head"),
        P(("clips", "frame"), "seq", "head"),
        P(("clips", "frame"), "seq", "head"),
        P("clips", None, None),
        P("clips", None, None),
        P("clips", None, None),
        P("clips", None, None),
    )
    return jax.shard_map(
        per_device,
        mesh=mesh,
        in_specs=placed,
        out_specs=P(("clips", "frame"), "seq", "head"),
        check_vma=False,
    )
```

```python
import functools
import math

import jax
import jax.numpy as jnp
from jax import lax
from jax.experimental import pallas as pl
from jax.experimental.pallas import tpu as pltpu
from jax.sharding import PartitionSpec as P

HEAD_DIM = 128
TILE = 128
HALF = TILE // 2
DISTANCES = (1, 2, 4)
STRIDE = 24
SCALE = math.log2(math.e) / math.sqrt(HEAD_DIM)
LARGE = 2.0**100
NT = (((1,), (1,)), ((), ()))
BF = jnp.bfloat16
F32 = jnp.float32
ANY = pl.BlockSpec(memory_space=pl.ANY)
SMEM = pl.BlockSpec(memory_space=pltpu.SMEM)
VMEM_LIMIT = 40 * 2**20
PACK_LIMIT = 16 * 2**20


class Layout:
    def __init__(self, frames_here, frame_tiles, frames, lengths):
        self.here = frames_here
        self.tiles = frame_tiles
        self.half = frame_tiles // 2
        self.own = frames_here * frame_tiles
        self.frames = frames
        self.lengths = lengths
        self.early = self.late = 0
        for frame, column, _ in self.remote(0):
            if self.edge(frame):
                self.late += lengths[column]
            else:
                self.early += lengths[column]
        self.places = self.early + self.late
        self.near = 2 * self.places
        self.far = self.near + frames_here * STRIDE
        self.size = self.far + frames_here * STRIDE

    def edge(self, frame):
        return frame in (0, self.here - 1)

    def remote(self, direction):
        found = []
        for away in (*range(1, self.here - 1), self.here - 1, 0):
            for column in reversed(range(3)):
                distance = DISTANCES[column]
                if away < distance:
                    frame = away if direction == 0 else self.here - 1 - away
                    source = frame - distance if direction == 0 else frame + distance
                    found.append((frame, column, source % self.here))
        return found


def table_kernel(lay, place_ref, one_ref, two_ref, four_ref, count_ref, table_ref, seen_ref):
    lists = (one_ref, two_ref, four_ref)
    first = place_ref[0]

    def distinct(target, direction, on_slot, on_new):
        for i in range(lay.own):
            seen_ref[i] = -1
        used = jnp.int32(0)
        for frame, column, source in lay.remote(direction):
            live = count_ref[column, direction, target + frame]
            for slot in range(lay.lengths[column]):
                name = lists[column][direction, slot, target + frame] + source * lay.tiles
                alive = slot < live
                known = seen_ref[name]
                fresh = jnp.logical_and(alive, known < 0)
                place = jnp.where(fresh, used, known)
                seen_ref[name] = place
                on_new(used, name)
                on_slot(frame, place, alive)
                used = used + fresh.astype(jnp.int32)
        return used

    filled = {}

    def append(base, frame, item, alive):
        at = base + frame * STRIDE
        count = filled.get(at, jnp.int32(0))
        table_ref[at + 1 + count] = item
        filled[at] = count + alive.astype(jnp.int32)

    for direction in (0, 1):
        target = first + (lay.here if direction == 0 else -lay.here)
        target = jnp.clip(target, 0, lay.frames - lay.here)
        for place in range(lay.places):
            table_ref[direction * lay.places + place] = 0

        def note(used, name, direction=direction):
            table_ref[direction * lay.places + jnp.minimum(used, lay.places - 1)] = name

        distinct(target, direction, lambda *_: None, note)

    for direction in (0, 1):

        def on_slot(frame, place, alive, direction=direction):
            if lay.edge(frame):
                append(lay.far, frame, direction * lay.places + place, alive)
            else:
                append(lay.near, frame, lay.own + direction * lay.early + place, alive)

        distinct(first, direction, on_slot, lambda *_: None)
        for frame in range(lay.here):
            for column, distance in enumerate(DISTANCES):
                source = frame + (2 * direction - 1) * distance
                if 0 <= source < lay.here:
                    live = count_ref[column, direction, first + frame]
                    for slot in range(lay.lengths[column]):
                        name = lists[column][direction, slot, first + frame]
                        append(lay.near, frame, source * lay.tiles + name, slot < live)
    for frame in range(lay.here):
        for base in (lay.near, lay.far):
            at = base + frame * STRIDE
            table_ref[at] = filled.get(at, jnp.int32(0))


def make_table(lay, place, lists):
    return pl.pallas_call(
        functools.partial(table_kernel, lay),
        in_specs=[SMEM] * 5,
        out_specs=SMEM,
        out_shape=jax.ShapeDtypeStruct((lay.size,), jnp.int32),
        scratch_shapes=[pltpu.SMEM((lay.own,), jnp.int32)],
        compiler_params=pltpu.CompilerParams(vmem_limit_bytes=VMEM_LIMIT),
        name="tile_tables",
    )(place, *lists)


def pack_kernel(lay, jobs, place_ref, table_ref, *refs):
    sources, outs, sems = refs[: -1 - len(jobs)], refs[-1 - len(jobs) : -1], refs[-1]
    core = place_ref[1]
    waits = []
    for (direction, segments), out in zip(jobs, outs):
        filled = 0
        for kv, begin, length in segments:
            own, other = sources[2 * kv : 2 * kv + 2]
            for item in range(begin, begin + length):
                name = table_ref[direction * lay.places + item]
                frame = name // lay.tiles
                tile = name % lay.tiles
                mine = tile // lay.half == core
                tile = tile % lay.half
                sem = sems.at[len(waits)]
                here = pltpu.make_async_copy(own.at[frame, tile, core], out.at[filled], sem)
                there = pltpu.make_async_copy(other.at[frame, tile, core], out.at[filled], sem)
                pl.when(mine)(here.start)
                pl.when(jnp.logical_not(mine))(there.start)
                waits.append(here)
                filled += 1
    for copy in waits:
        copy.wait()


def pack_call(lay, segment_lists, place, table, sources):
    width = sources[0].shape[-1]
    jobs = [(direction, segments) for segments in segment_lists for direction in (0, 1)]
    sizes = [sum(n for _, _, n in segments) for _, segments in jobs]
    outs = pl.pallas_call(
        functools.partial(pack_kernel, lay, jobs),
        in_specs=[SMEM] * 2 + [ANY] * len(sources),
        out_specs=[pl.BlockSpec(memory_space=pltpu.VMEM)] * len(jobs),
        out_shape=[jax.ShapeDtypeStruct((n, HALF, width), BF) for n in sizes],
        scratch_shapes=[pltpu.SemaphoreType.DMA((sum(sizes),))],
        compiler_params=pltpu.CompilerParams(vmem_limit_bytes=PACK_LIMIT),
        name="pack_tiles",
    )(place, table, *sources)
    return [tuple(outs[i : i + 2]) for i in range(0, len(outs), 2)]


def rows_of(buf, index, cols):
    tiles = buf[index, :, :, cols]
    return tiles.reshape(tiles.size // HEAD_DIM, HEAD_DIM)


def mix(weights, values):
    return jnp.dot(
        weights.astype(BF),
        jnp.concatenate([values, jnp.ones_like(values)], axis=1),
        preferred_element_type=F32,
    )


def attend_tiles(q_ref, kbuf, vbuf, ids, m_s, l_s, acc_s, heads):
    for head in range(heads):
        cols = slice(head * HEAD_DIM, (head + 1) * HEAD_DIM)
        keys = jnp.concatenate([rows_of(kbuf, i, cols) for i in ids], axis=0)
        values = jnp.concatenate([rows_of(vbuf, i, cols) for i in ids], axis=0)
        scores = lax.dot_general(q_ref[0, :, cols], keys, NT, preferred_element_type=F32)
        shift = jnp.concatenate([m_s[head]] * len(ids), axis=1)
        mixed = mix(jnp.exp2((scores - shift) * SCALE), values)
        acc_s[:, cols] += mixed[:, :HEAD_DIM]
        l_s[head] += mixed[:, HEAD_DIM:]


def attend_list(q_ref, kbuf, vbuf, table_ref, base, m_s, l_s, acc_s, heads, packed=False):
    count = table_ref[base]

    def add(start, n):
        ids = [start + j if packed else table_ref[base + 1 + start + j] for j in range(n)]
        attend_tiles(q_ref, kbuf, vbuf, ids, m_s, l_s, acc_s, heads)

    def four(i, _):
        add(4 * i, 4)
        return 0

    lax.fori_loop(0, count // 4, four, 0)

    @pl.when(count % 4 >= 2)
    def _():
        add(count // 4 * 4, 2)

    @pl.when(count % 2 == 1)
    def _():
        add(count - 1, 1)


def attend_own(lay, q_ref, kbuf, vbuf, frame, m_s, l_s, acc_s, heads):
    for head in range(heads):
        cols = slice(head * HEAD_DIM, (head + 1) * HEAD_DIM)
        own = pl.ds(frame * lay.tiles, lay.tiles)
        scores = lax.dot_general(
            q_ref[0, :, cols], rows_of(kbuf, own, cols), NT, preferred_element_type=F32
        )
        top = jnp.max(scores[:, :TILE], axis=1, keepdims=True)
        mixed = mix(jnp.exp2((scores - top) * SCALE), rows_of(vbuf, own, cols))
        acc_s[:, cols] = mixed[:, :HEAD_DIM]
        l_s[head] = mixed[:, HEAD_DIM:]
        m_s[head] = jnp.broadcast_to(top, m_s.shape[1:])


def save_stats(stat_ref, m_s, l_s, heads):
    rows = stat_ref.shape[1]
    lane = lax.broadcasted_iota(jnp.int32, (rows, 128), 1)
    stat = jnp.zeros((rows, 128), F32)
    for head in range(heads):
        stat = jnp.where(lane == head, l_s[head], stat)
        stat = jnp.where(lane == 64 + head, m_s[head], stat)
    stat_ref[0] = stat


def load_stats(stat_ref, m_s, l_s, heads):
    rows = stat_ref.shape[1]
    for head in range(heads):
        l_s[head] = jnp.broadcast_to(stat_ref[0, :, head : head + 1], (rows, 128))
        m_s[head] = jnp.broadcast_to(stat_ref[0, :, 64 + head : 65 + head], (rows, 128))


def finish(out_ref, acc_s, l_s, heads):
    for head in range(heads):
        cols = slice(head * HEAD_DIM, (head + 1) * HEAD_DIM)
        out_ref[0, :, cols] = (acc_s[:, cols] / l_s[head]).astype(out_ref.dtype)


def local_copies(lay, index, core, local, bufs, sems):
    found = []
    for kv, buf in enumerate(bufs):
        for side, owner in enumerate((core, 1 - core)):
            target = buf.at[pl.ds(index * lay.tiles + owner * lay.half, lay.half)]
            source = local[2 * kv + side].at[index]
            found.append(pltpu.make_async_copy(source, target, sems.at[index, 2 * kv + side]))
    return found


class Received:
    def __init__(self, lay, core, refs):
        self.lay = lay
        self.core = core
        self.early = (refs[:4], refs[4:8])
        self.late = refs[8:12]

    def early_copies(self, bufs, sems):
        found = []
        for kv, buf in enumerate(bufs):
            for side, half in enumerate((self.core, 1 - self.core)):
                for direction in (0, 1):
                    begin = self.lay.own + direction * self.lay.early
                    target = buf.at[pl.ds(begin, self.lay.early), half]
                    source = self.early[kv][2 * side + direction]
                    found.append(pltpu.make_async_copy(source, target, sems.at[len(found)]))
        return found

    def start(self, item, length, targets, sems):
        direction = item // length
        place = item % length
        for way in (0, 1):
            for late in (False, True)[: 2 if length > self.lay.early else 1]:
                here = direction == way
                if length > self.lay.early:
                    here = jnp.logical_and(here, (place >= self.lay.early) == late)

                @pl.when(here)
                def _(way=way, late=late):
                    for kv, target in enumerate(targets):
                        for side, half in enumerate((self.core, 1 - self.core)):
                            ref = self.late if late else self.early[kv]
                            at = place + (kv * self.lay.late - self.lay.early if late else 0)
                            source = ref[2 * side + way].at[at]
                            pltpu.make_async_copy(source, target.at[half], sems.at[2 * kv + side]).start()

    def wait(self, targets, sems):
        for kv, target in enumerate(targets):
            for side in (0, 1):
                source = self.early[0][0].at[0]
                pltpu.make_async_copy(source, target.at[side], sems.at[2 * kv + side]).wait()


def exact_frame(lay, heads, frame, core, table_ref, q_ref, local, received, acc_s, m_s, l_s, tk, tv, sems):
    m_s[...] = jnp.full(m_s.shape, -jnp.inf, F32)
    l_s[...] = jnp.zeros(l_s.shape, F32)
    acc_s[...] = jnp.zeros(acc_s.shape, F32)

    def add_tile():
        for head in range(heads):
            cols = slice(head * HEAD_DIM, (head + 1) * HEAD_DIM)
            keys, values = (t[:, :, cols].reshape(TILE, HEAD_DIM) for t in (tk, tv))
            scores = lax.dot_general(q_ref[0, :, cols], keys, NT, preferred_element_type=F32)
            before = m_s[head]
            top = jnp.maximum(before, jnp.max(scores, axis=1, keepdims=True))
            fade = jnp.exp2((before - top) * SCALE)
            mixed = mix(jnp.exp2((scores - top) * SCALE), values)
            acc_s[:, cols] = acc_s[:, cols] * fade + mixed[:, :HEAD_DIM]
            l_s[head] = l_s[head] * fade + mixed[:, HEAD_DIM:]
            m_s[head] = top

    def near_tile(name):
        source, tile = name // lay.tiles, name % lay.tiles
        mine = tile // lay.half == core
        tile = tile % lay.half
        for side in (0, 1):

            @pl.when(mine if side == 0 else jnp.logical_not(mine))
            def _(side=side):
                found = [
                    pltpu.make_async_copy(local[2 * kv + side].at[source, tile], buf, sems.at[kv])
                    for kv, buf in enumerate((tk, tv))
                ]
                for copy in found:
                    copy.start()
                for copy in found:
                    copy.wait()

    def far_tile(item, length):
        received.start(item, length, (tk, tv), sems)
        received.wait((tk, tv), sems)

    def own_step(i, _):
        near_tile(frame * lay.tiles + i)
        add_tile()
        return 0

    def near_step(i, _):
        name = table_ref[lay.near + frame * STRIDE + 1 + i]

        @pl.when(name < lay.own)
        def _():
            near_tile(name)

        @pl.when(name >= lay.own)
        def _():
            far_tile(name - lay.own, lay.early)

        add_tile()
        return 0

    def far_step(i, _):
        far_tile(table_ref[lay.far + frame * STRIDE + 1 + i], lay.places)
        add_tile()
        return 0

    lax.fori_loop(0, lay.tiles, own_step, 0)
    lax.fori_loop(0, table_ref[lay.near + frame * STRIDE], near_step, 0)
    if received.late:
        lax.fori_loop(0, table_ref[lay.far + frame * STRIDE], far_step, 0)


def near_kernel(lay, heads, whole, place_ref, table_ref, q_ref, *refs):
    core = place_ref[1]
    local, refs = refs[:4], refs[4:]
    if whole:
        received, refs = Received(lay, core, refs[:8]), refs[8:]
        out_ref, acc_s, kbuf, vbuf, m_s, l_s, sems, tk, tv, far_sems = refs
    else:
        acc_out, stat_ref, kbuf, vbuf, m_s, l_s, sems = refs
        acc_s = acc_out.at[0]
    step = pl.program_id(0)
    frame = step + 1 if whole else step * (lay.here - 1)
    begin = 1 if whole else 0

    def first():
        return local_copies(lay, begin, core, local, (kbuf, vbuf), sems)

    def others():
        found = []
        for index in range(lay.here):
            if index != begin:
                found += local_copies(lay, index, core, local, (kbuf, vbuf), sems)
        return found + (received.early_copies((kbuf, vbuf), far_sems) if whole else [])

    @pl.when(step == 0)
    def _():
        for copy in first():
            copy.start()
        for copy in first():
            copy.wait()
        for copy in others():
            copy.start()

    attend_own(lay, q_ref, kbuf, vbuf, frame, m_s, l_s, acc_s, heads)

    @pl.when(step == 0)
    def _():
        for copy in others():
            copy.wait()

    attend_list(q_ref, kbuf, vbuf, table_ref, lay.near + frame * STRIDE, m_s, l_s, acc_s, heads)
    if whole:

        @pl.when(jnp.max(l_s[...]) > LARGE)
        def _():
            exact_frame(lay, heads, frame, core, table_ref, q_ref, local, received, acc_s, m_s, l_s, tk, tv, far_sems)

        finish(out_ref, acc_s, l_s, heads)
    else:
        save_stats(stat_ref, m_s, l_s, heads)


def cost(scores):
    return pl.CostEstimate(flops=scores * 4 * HEAD_DIM, bytes_accessed=scores // 8, transcendentals=scores)


def near_call(lay, heads, whole, place, table, queries, local, early=()):
    here, rows, width = queries.shape
    steps = here - 2 if whole else 2
    index = (lambda s, *_: (s + 1, 0, 0)) if whole else (lambda s, *_: (s * (here - 1), 0, 0))
    block = pl.BlockSpec((1, rows, width), index)
    count = lay.own + (2 * lay.early if whole else 0)
    bufs = [pltpu.VMEM((count, 2, HALF, width), BF)] * 2
    sums = [pltpu.VMEM((heads, rows, 128), F32)] * 2
    sems = [pltpu.SemaphoreType.DMA((here, 4))]
    if whole:
        out_specs = [block]
        out_shape = [jax.ShapeDtypeStruct((here, rows, width), BF)]
        scratch = [pltpu.VMEM((rows, width), F32), *bufs, *sums, *sems]
        scratch += [pltpu.VMEM((2, HALF, width), BF)] * 2 + [pltpu.SemaphoreType.DMA((8,))]
    else:
        out_specs = [
            pl.BlockSpec((1, rows, width), lambda s, *_: (s, 0, 0)),
            pl.BlockSpec((1, rows, 128), lambda s, *_: (s, 0, 0)),
        ]
        out_shape = [jax.ShapeDtypeStruct((2, rows, n), F32) for n in (width, 128)]
        scratch = [*bufs, *sums, *sems]
    return pl.pallas_call(
        functools.partial(near_kernel, lay, heads, whole),
        grid_spec=pltpu.PrefetchScalarGridSpec(
            num_scalar_prefetch=2,
            grid=(steps,),
            in_specs=[block] + [ANY] * (4 + len(early)),
            out_specs=out_specs,
            scratch_shapes=scratch,
        ),
        out_shape=out_shape,
        compiler_params=pltpu.CompilerParams(vmem_limit_bytes=VMEM_LIMIT),
        cost_estimate=cost(steps * rows * heads * 16 * TILE),
        name="attend_middle" if whole else "attend_edges",
    )(place, table, queries, *local, *early)


def far_kernel(lay, heads, place_ref, table_ref, q_ref, acc_ref, stat_ref, *refs):
    core = place_ref[1]
    local, received = refs[:4], Received(lay, core, refs[4:16])
    out_ref, kbuf, vbuf, acc_s, m_s, l_s, tk, tv, sems, exact_sems = refs[17:]
    step = pl.program_id(0)
    frame = step * (lay.here - 1)
    room = kbuf.shape[1]

    def bufs(at, i):
        return kbuf.at[at, i], vbuf.at[at, i]

    def start(at):
        base = lay.far + at * (lay.here - 1) * STRIDE

        def one(i, _):
            received.start(table_ref[base + 1 + i], lay.places, bufs(at, i), sems.at[at * room + i])
            return 0

        lax.fori_loop(0, table_ref[base], one, 0)

    @pl.when(step == 0)
    def _():
        start(0)
        start(1)

    load_stats(stat_ref, m_s, l_s, heads)
    acc_s[...] = acc_ref[0]
    base = lay.far + frame * STRIDE

    def wait(i, _):
        received.wait(bufs(step, i), sems.at[step * room + i])
        return 0

    lax.fori_loop(0, table_ref[base], wait, 0)
    attend_list(q_ref, kbuf.at[step], vbuf.at[step], table_ref, base, m_s, l_s, acc_s, heads, packed=True)

    @pl.when(jnp.max(l_s[...]) > LARGE)
    def _():
        exact_frame(lay, heads, frame, core, table_ref, q_ref, local, received, acc_s, m_s, l_s, tk, tv, exact_sems)

    finish(out_ref, acc_s, l_s, heads)


def far_call(lay, heads, place, table, queries, acc, stats, local, early, late, out):
    here, rows, width = queries.shape
    block = pl.BlockSpec((1, rows, width), lambda s, *_: (s * (here - 1), 0, 0))
    anys = [*local, *early, *late, out]
    room = sum(n for frame, column, _ in lay.remote(0) if frame == 0 for n in [lay.lengths[column]])
    room += sum(n for frame, column, _ in lay.remote(1) if frame == 0 for n in [lay.lengths[column]])
    return pl.pallas_call(
        functools.partial(far_kernel, lay, heads),
        grid_spec=pltpu.PrefetchScalarGridSpec(
            num_scalar_prefetch=2,
            grid=(2,),
            in_specs=[
                block,
                pl.BlockSpec((1, rows, width), lambda s, *_: (s, 0, 0)),
                pl.BlockSpec((1, rows, 128), lambda s, *_: (s, 0, 0)),
            ]
            + [ANY] * len(anys),
            out_specs=block,
            scratch_shapes=[
                pltpu.VMEM((2, room, 2, HALF, width), BF),
                pltpu.VMEM((2, room, 2, HALF, width), BF),
                pltpu.VMEM((rows, width), F32),
                pltpu.VMEM((heads, rows, 128), F32),
                pltpu.VMEM((heads, rows, 128), F32),
                pltpu.VMEM((2, HALF, width), BF),
                pltpu.VMEM((2, HALF, width), BF),
                pltpu.SemaphoreType.DMA((2 * room, 4)),
                pltpu.SemaphoreType.DMA((4,)),
            ],
        ),
        out_shape=jax.ShapeDtypeStruct((here, rows, width), BF),
        input_output_aliases={5 + len(anys) - 1: 0},
        compiler_params=pltpu.CompilerParams(vmem_limit_bytes=VMEM_LIMIT),
        cost_estimate=cost(2 * rows * heads * 7 * TILE),
        name="attend_late",
    )(place, table, queries, acc, stats, *anys)


def shifted(block, axis, step):
    devices = range(lax.axis_size(axis))
    return lax.ppermute(block, axis, [(i, i + step) for i in devices if i + step in devices])


def swapped(block):
    return lax.ppermute(block, "seq", [(0, 1), (1, 0)])


def per_device(queries, key_rows, value_rows, list_one, list_two, list_four, tile_counts):
    here, rows, width = queries.shape
    heads = width // HEAD_DIM
    frames = list_one.shape[0]
    lists = (list_one, list_two, list_four)
    lay = Layout(here, 2 * rows // TILE, frames, tuple(a.shape[2] for a in lists))
    core = lax.axis_index("seq")
    place = jnp.stack([lax.axis_index("frame") * here, core]).astype(jnp.int32)

    k_own, v_own = (a.reshape(here, lay.half, 2, HALF, width) for a in (key_rows, value_rows))
    k_other, v_other = swapped(k_own), swapped(v_own)
    by_frame = [jnp.transpose(a, (1, 2, 0)) for a in lists] + [jnp.transpose(tile_counts, (2, 1, 0))]
    table = make_table(lay, place, by_frame)

    def both_ways(pair):
        return shifted(pair[0], "frame", 1), shifted(pair[1], "frame", -1)

    def both_cores(pair):
        return (*pair, *map(swapped, pair))

    k_other, table = lax.optimization_barrier((k_other, table))
    (k_early,) = pack_call(lay, [[(0, 0, lay.early)]], place, table, (k_own, k_other))
    k_early, table = lax.optimization_barrier((k_early, table))
    k_early = both_ways(k_early)
    rest = [[(1, 0, lay.early)], [(0, lay.early, lay.late), (1, lay.early, lay.late)]]
    v_early, late = pack_call(lay, rest, place, table, (k_own, k_other, v_own, v_other))
    v_early, late = both_ways(v_early), both_ways(late)

    local = (k_own, k_other, v_own, v_other)
    acc, stats = near_call(lay, heads, False, place, table, queries, local)
    k_early, v_early, stats = lax.optimization_barrier((k_early, v_early, stats))
    early = (*both_cores(k_early), *both_cores(v_early))
    (out,) = near_call(lay, heads, True, place, table, queries, local, early)
    late, out = lax.optimization_barrier((late, out))
    return far_call(lay, heads, place, table, queries, acc, stats, local, early, both_cores(late), out)


def solution(mesh):
    placed = (
        P(("clips", "frame"), "seq", "head"),
        P(("clips", "frame"), "seq", "head"),
        P(("clips", "frame"), "seq", "head"),
        P("clips", None, None),
        P("clips", None, None),
        P("clips", None, None),
        P("clips", None, None),
    )
    return jax.shard_map(
        per_device,
        mesh=mesh,
        in_specs=placed,
        out_specs=P(("clips", "frame"), "seq", "head"),
        check_vma=False,
    )
```

```python
import functools
import math

import jax
import jax.numpy as jnp
from jax import lax
from jax.experimental import pallas as pl
from jax.experimental.pallas import tpu as pltpu
from jax.sharding import PartitionSpec as P

HEAD_DIM = 128
TILE = 128
HALF = TILE // 2
DISTANCES = (1, 2, 4)
STRIDE = 24
SCALE = math.log2(math.e) / math.sqrt(HEAD_DIM)
LARGE = 2.0**100
NT = (((1,), (1,)), ((), ()))
BF = jnp.bfloat16
F32 = jnp.float32
ANY = pl.BlockSpec(memory_space=pl.ANY)
SMEM = pl.BlockSpec(memory_space=pltpu.SMEM)
VMEM_LIMIT = 48 * 2**20
PACK_LIMIT = 16 * 2**20


class Layout:
    def __init__(self, frames_here, frame_tiles, frames, lengths):
        self.here = frames_here
        self.tiles = frame_tiles
        self.half = frame_tiles // 2
        self.own = frames_here * frame_tiles
        self.frames = frames
        self.lengths = lengths
        self.early = self.late = 0
        for frame, column, _ in self.remote(0):
            if self.edge(frame):
                self.late += lengths[column]
            else:
                self.early += lengths[column]
        self.places = self.early + self.late
        self.second = max(self.late // 2 - 1, 1)
        self.third = self.late - self.second
        self.near = 2 * self.places
        self.far = self.near + frames_here * STRIDE
        self.size = self.far + frames_here * STRIDE

    def edge(self, frame):
        return frame in (0, self.here - 1)

    def remote(self, direction):
        found = []
        for away in (*range(1, self.here - 1), self.here - 1, 0):
            for column in reversed(range(3)):
                distance = DISTANCES[column]
                if away < distance:
                    frame = away if direction == 0 else self.here - 1 - away
                    source = frame - distance if direction == 0 else frame + distance
                    found.append((frame, column, source % self.here))
        return found


def table_kernel(lay, place_ref, one_ref, two_ref, four_ref, count_ref, table_ref, seen_ref):
    lists = (one_ref, two_ref, four_ref)
    first = place_ref[0]
    odd = first // lay.here % 2

    def distinct(target, direction, on_slot, on_new):
        for i in range(lay.own):
            seen_ref[i] = -1
        used = jnp.int32(0)
        for frame, column, source in lay.remote(direction):
            live = count_ref[column, direction, target + frame]
            for slot in range(lay.lengths[column]):
                name = lists[column][direction, slot, target + frame] + source * lay.tiles
                alive = slot < live
                known = seen_ref[name]
                fresh = jnp.logical_and(alive, known < 0)
                place = jnp.where(fresh, used, known)
                seen_ref[name] = place
                on_new(used, name)
                on_slot(frame, place, alive)
                used = used + fresh.astype(jnp.int32)
        return used

    filled = {}

    def append(base, frame, item, alive):
        at = base + frame * STRIDE
        count = filled.get(at, jnp.int32(0))
        table_ref[at + 1 + count] = item
        filled[at] = count + alive.astype(jnp.int32)

    for direction in (0, 1):
        target = first + (lay.here if direction == 0 else -lay.here)
        target = jnp.clip(target, 0, lay.frames - lay.here)
        begin = (odd + direction) % 2 * lay.places
        for place in range(lay.places):
            table_ref[begin + place] = 0

        def note(used, name, begin=begin):
            table_ref[begin + jnp.minimum(used, lay.places - 1)] = name

        distinct(target, direction, lambda *_: None, note)

    for direction in (0, 1):
        way = (odd + 1 - direction) % 2

        def on_slot(frame, place, alive, way=way):
            if lay.edge(frame):
                append(lay.far, frame, way * lay.places + place, alive)
            else:
                append(lay.near, frame, lay.own + way * lay.early + place, alive)

        distinct(first, direction, on_slot, lambda *_: None)
        for frame in range(lay.here):
            for column, distance in enumerate(DISTANCES):
                source = frame + (2 * direction - 1) * distance
                if 0 <= source < lay.here:
                    live = count_ref[column, direction, first + frame]
                    for slot in range(lay.lengths[column]):
                        name = lists[column][direction, slot, first + frame]
                        append(lay.near, frame, source * lay.tiles + name, slot < live)
    for frame in range(lay.here):
        for base in (lay.near, lay.far):
            at = base + frame * STRIDE
            table_ref[at] = filled.get(at, jnp.int32(0))


def make_table(lay, place, lists):
    return pl.pallas_call(
        functools.partial(table_kernel, lay),
        in_specs=[SMEM] * 5,
        out_specs=SMEM,
        out_shape=jax.ShapeDtypeStruct((lay.size,), jnp.int32),
        scratch_shapes=[pltpu.SMEM((lay.own,), jnp.int32)],
        compiler_params=pltpu.CompilerParams(vmem_limit_bytes=VMEM_LIMIT),
        name="tile_tables",
    )(place, *lists)


def pack_kernel(lay, jobs, place_ref, table_ref, *refs):
    sources, outs, sems = refs[: -1 - len(jobs)], refs[-1 - len(jobs) : -1], refs[-1]
    core = place_ref[1]
    waits = []
    for (way, segments), out in zip(jobs, outs):
        filled = 0
        for kv, begin, length in segments:
            own, other = sources[2 * kv : 2 * kv + 2]
            for item in range(begin, begin + length):
                name = table_ref[way * lay.places + item]
                frame = name // lay.tiles
                tile = name % lay.tiles
                mine = tile // lay.half == core
                tile = tile % lay.half
                sem = sems.at[len(waits)]
                here = pltpu.make_async_copy(own.at[frame, tile, core], out.at[filled], sem)
                there = pltpu.make_async_copy(other.at[frame, tile, core], out.at[filled], sem)
                pl.when(mine)(here.start)
                pl.when(jnp.logical_not(mine))(there.start)
                waits.append(here)
                filled += 1
    for copy in waits:
        copy.wait()


def pack_call(lay, segment_lists, place, table, sources):
    width = sources[0].shape[-1]
    jobs = [(way, segments) for segments in segment_lists for way in (0, 1)]
    sizes = [sum(n for _, _, n in segments) for _, segments in jobs]
    outs = pl.pallas_call(
        functools.partial(pack_kernel, lay, jobs),
        in_specs=[SMEM] * 2 + [ANY] * len(sources),
        out_specs=[pl.BlockSpec(memory_space=pltpu.VMEM)] * len(jobs),
        out_shape=[jax.ShapeDtypeStruct((n, HALF, width), BF) for n in sizes],
        scratch_shapes=[pltpu.SemaphoreType.DMA((sum(sizes),))],
        compiler_params=pltpu.CompilerParams(vmem_limit_bytes=PACK_LIMIT),
        name="pack_tiles",
    )(place, table, *in_hbm(sources))
    return [tuple(outs[i : i + 2]) for i in range(0, len(outs), 2)]


def rows_of(buf, index, cols):
    tiles = buf[index, :, :, cols]
    return tiles.reshape(tiles.size // HEAD_DIM, HEAD_DIM)


def mix(weights, values):
    return jnp.dot(
        weights.astype(BF),
        jnp.concatenate([values, jnp.ones_like(values)], axis=1),
        preferred_element_type=F32,
    )


def attend_tiles(q_ref, kbuf, vbuf, ids, m_s, l_s, acc_s, heads):
    for head in range(heads):
        cols = slice(head * HEAD_DIM, (head + 1) * HEAD_DIM)
        keys = jnp.concatenate([rows_of(kbuf, i, cols) for i in ids], axis=0)
        values = jnp.concatenate([rows_of(vbuf, i, cols) for i in ids], axis=0)
        scores = lax.dot_general(q_ref[0, :, cols], keys, NT, preferred_element_type=F32)
        shift = jnp.concatenate([m_s[head]] * len(ids), axis=1)
        mixed = mix(jnp.exp2((scores - shift) * SCALE), values)
        acc_s[:, cols] += mixed[:, :HEAD_DIM]
        l_s[head] += mixed[:, HEAD_DIM:]


def attend_list(q_ref, kbuf, vbuf, table_ref, base, m_s, l_s, acc_s, heads, packed=False):
    count = table_ref[base]

    def add(start, n):
        ids = [start + j if packed else table_ref[base + 1 + start + j] for j in range(n)]
        attend_tiles(q_ref, kbuf, vbuf, ids, m_s, l_s, acc_s, heads)

    def four(i, _):
        add(4 * i, 4)
        return 0

    lax.fori_loop(0, count // 4, four, 0)

    @pl.when(count % 4 >= 2)
    def _():
        add(count // 4 * 4, 2)

    @pl.when(count % 2 == 1)
    def _():
        add(count - 1, 1)


def attend_own(lay, q_ref, kbuf, vbuf, frame, m_s, l_s, acc_s, heads):
    for head in range(heads):
        cols = slice(head * HEAD_DIM, (head + 1) * HEAD_DIM)
        own = pl.ds(frame * lay.tiles, lay.tiles)
        scores = lax.dot_general(
            q_ref[0, :, cols], rows_of(kbuf, own, cols), NT, preferred_element_type=F32
        )
        top = jnp.max(scores[:, :TILE], axis=1, keepdims=True)
        mixed = mix(jnp.exp2((scores - top) * SCALE), rows_of(vbuf, own, cols))
        acc_s[:, cols] = mixed[:, :HEAD_DIM]
        l_s[head] = mixed[:, HEAD_DIM:]
        m_s[head] = jnp.broadcast_to(top, m_s.shape[1:])


def save_stats(stat_ref, m_s, l_s, heads):
    rows = stat_ref.shape[1]
    lane = lax.broadcasted_iota(jnp.int32, (rows, 128), 1)
    stat = jnp.zeros((rows, 128), F32)
    for head in range(heads):
        stat = jnp.where(lane == head, l_s[head], stat)
        stat = jnp.where(lane == 64 + head, m_s[head], stat)
    stat_ref[0] = stat


def load_stats(stat_ref, m_s, l_s, heads):
    rows = stat_ref.shape[1]
    for head in range(heads):
        l_s[head] = jnp.broadcast_to(stat_ref[0, :, head : head + 1], (rows, 128))
        m_s[head] = jnp.broadcast_to(stat_ref[0, :, 64 + head : 65 + head], (rows, 128))


def finish(out_ref, acc_s, l_s, heads):
    for head in range(heads):
        cols = slice(head * HEAD_DIM, (head + 1) * HEAD_DIM)
        out_ref[0, :, cols] = (acc_s[:, cols] / l_s[head]).astype(out_ref.dtype)


def local_copies(lay, index, core, local, bufs, sems):
    found = []
    for kv, buf in enumerate(bufs):
        for side, owner in enumerate((core, 1 - core)):
            target = buf.at[pl.ds(index * lay.tiles + owner * lay.half, lay.half)]
            source = local[2 * kv + side].at[index]
            found.append(pltpu.make_async_copy(source, target, sems.at[index, 2 * kv + side]))
    return found


class Received:
    def __init__(self, lay, core, refs):
        self.lay = lay
        self.core = core
        self.parts = [refs[i : i + 4] for i in range(0, len(refs), 4)]
        first, second = lay.early, lay.second
        self.ranges = [(0, first, (0, 0), (1, 0))]
        if len(self.parts) > 2:
            self.ranges.append((first, second, (1, first), (1, first + second)))
            self.ranges.append((first + second, lay.third, (2, 0), (2, lay.third)))

    def early_copies(self, bufs, sems):
        found = []
        for buf, part in zip(bufs, self.parts):
            for side, half in enumerate((self.core, 1 - self.core)):
                for way in (0, 1):
                    begin = self.lay.own + way * self.lay.early
                    target = buf.at[pl.ds(begin, self.lay.early), half]
                    source = part[2 * side + way].at[pl.ds(0, self.lay.early)]
                    found.append(pltpu.make_async_copy(source, target, sems.at[len(found)]))
        return found

    def start(self, item, length, targets, sems):
        place = item % length
        for way in (0, 1):
            for begin, size, *rows in self.ranges:
                inside = jnp.logical_and(place >= begin, place < begin + size)

                @pl.when(jnp.logical_and(item // length == way, inside))
                def _(way=way, begin=begin, rows=rows):
                    for kv, (target, (part, row)) in enumerate(zip(targets, rows)):
                        for side, half in enumerate((self.core, 1 - self.core)):
                            source = self.parts[part][2 * side + way].at[place - begin + row]
                            pltpu.make_async_copy(source, target.at[half], sems.at[2 * kv + side]).start()

    def wait(self, targets, sems):
        for kv, target in enumerate(targets):
            for side in (0, 1):
                source = self.parts[0][0].at[0]
                pltpu.make_async_copy(source, target.at[side], sems.at[2 * kv + side]).wait()


def exact_frame(lay, heads, frame, core, table_ref, q_ref, local, received, acc_s, m_s, l_s, tk, tv, sems):
    m_s[...] = jnp.full(m_s.shape, -jnp.inf, F32)
    l_s[...] = jnp.zeros(l_s.shape, F32)
    acc_s[...] = jnp.zeros(acc_s.shape, F32)

    def add_tile():
        for head in range(heads):
            cols = slice(head * HEAD_DIM, (head + 1) * HEAD_DIM)
            keys, values = (t[:, :, cols].reshape(TILE, HEAD_DIM) for t in (tk, tv))
            scores = lax.dot_general(q_ref[0, :, cols], keys, NT, preferred_element_type=F32)
            before = m_s[head]
            top = jnp.maximum(before, jnp.max(scores, axis=1, keepdims=True))
            fade = jnp.exp2((before - top) * SCALE)
            mixed = mix(jnp.exp2((scores - top) * SCALE), values)
            acc_s[:, cols] = acc_s[:, cols] * fade + mixed[:, :HEAD_DIM]
            l_s[head] = l_s[head] * fade + mixed[:, HEAD_DIM:]
            m_s[head] = top

    def near_tile(name):
        source, tile = name // lay.tiles, name % lay.tiles
        mine = tile // lay.half == core
        tile = tile % lay.half
        for side in (0, 1):

            @pl.when(mine if side == 0 else jnp.logical_not(mine))
            def _(side=side):
                found = [
                    pltpu.make_async_copy(local[2 * kv + side].at[source, tile], buf, sems.at[kv])
                    for kv, buf in enumerate((tk, tv))
                ]
                for copy in found:
                    copy.start()
                for copy in found:
                    copy.wait()

    def far_tile(item, length):
        received.start(item, length, (tk, tv), sems)
        received.wait((tk, tv), sems)

    def own_step(i, _):
        near_tile(frame * lay.tiles + i)
        add_tile()
        return 0

    def near_step(i, _):
        name = table_ref[lay.near + frame * STRIDE + 1 + i]

        @pl.when(name < lay.own)
        def _():
            near_tile(name)

        @pl.when(name >= lay.own)
        def _():
            far_tile(name - lay.own, lay.early)

        add_tile()
        return 0

    def far_step(i, _):
        far_tile(table_ref[lay.far + frame * STRIDE + 1 + i], lay.places)
        add_tile()
        return 0

    lax.fori_loop(0, lay.tiles, own_step, 0)
    lax.fori_loop(0, table_ref[lay.near + frame * STRIDE], near_step, 0)
    if len(received.parts) > 2:
        lax.fori_loop(0, table_ref[lay.far + frame * STRIDE], far_step, 0)


def near_kernel(lay, heads, whole, place_ref, table_ref, q_ref, *refs):
    core = place_ref[1]
    local, refs = refs[:4], refs[4:]
    if whole:
        received, refs = Received(lay, core, refs[:8]), refs[8:]
        out_ref, acc_s, kbuf, vbuf, m_s, l_s, sems, tk, tv, far_sems = refs
    else:
        acc_out, stat_ref, kbuf, vbuf, m_s, l_s, sems = refs
        acc_s = acc_out.at[0]
    step = pl.program_id(0)
    frame = step + 1 if whole else step * (lay.here - 1)
    begin = 1 if whole else 0

    def first():
        return local_copies(lay, begin, core, local, (kbuf, vbuf), sems)

    def others():
        found = []
        for index in range(lay.here):
            if index != begin:
                found += local_copies(lay, index, core, local, (kbuf, vbuf), sems)
        return found + (received.early_copies((kbuf, vbuf), far_sems) if whole else [])

    @pl.when(step == 0)
    def _():
        for copy in first():
            copy.start()
        for copy in first():
            copy.wait()
        for copy in others():
            copy.start()

    attend_own(lay, q_ref, kbuf, vbuf, frame, m_s, l_s, acc_s, heads)

    @pl.when(step == 0)
    def _():
        for copy in others():
            copy.wait()

    attend_list(q_ref, kbuf, vbuf, table_ref, lay.near + frame * STRIDE, m_s, l_s, acc_s, heads)
    if whole:

        @pl.when(jnp.max(l_s[...]) > LARGE)
        def _():
            exact_frame(lay, heads, frame, core, table_ref, q_ref, local, received, acc_s, m_s, l_s, tk, tv, far_sems)

        finish(out_ref, acc_s, l_s, heads)
    else:
        save_stats(stat_ref, m_s, l_s, heads)


def cost(scores):
    return pl.CostEstimate(flops=scores * 4 * HEAD_DIM, bytes_accessed=scores // 8, transcendentals=scores)


def near_call(lay, heads, whole, place, table, queries, local, early=()):
    here, rows, width = queries.shape
    steps = here - 2 if whole else 2
    index = (lambda s, *_: (s + 1, 0, 0)) if whole else (lambda s, *_: (s * (here - 1), 0, 0))
    block = pl.BlockSpec((1, rows, width), index)
    count = lay.own + (2 * lay.early if whole else 0)
    bufs = [pltpu.VMEM((count, 2, HALF, width), BF)] * 2
    sums = [pltpu.VMEM((heads, rows, 128), F32)] * 2
    sems = [pltpu.SemaphoreType.DMA((here, 4))]
    if whole:
        out_specs = [block]
        out_shape = [jax.ShapeDtypeStruct((here, rows, width), BF)]
        scratch = [pltpu.VMEM((rows, width), F32), *bufs, *sums, *sems]
        scratch += [pltpu.VMEM((2, HALF, width), BF)] * 2 + [pltpu.SemaphoreType.DMA((8,))]
    else:
        out_specs = [
            pl.BlockSpec((1, rows, width), lambda s, *_: (s, 0, 0)),
            pl.BlockSpec((1, rows, 128), lambda s, *_: (s, 0, 0)),
        ]
        out_shape = [jax.ShapeDtypeStruct((2, rows, n), F32) for n in (width, 128)]
        scratch = [*bufs, *sums, *sems]
    return pl.pallas_call(
        functools.partial(near_kernel, lay, heads, whole),
        grid_spec=pltpu.PrefetchScalarGridSpec(
            num_scalar_prefetch=2,
            grid=(steps,),
            in_specs=[block] + [ANY] * (4 + len(early)),
            out_specs=out_specs,
            scratch_shapes=scratch,
        ),
        out_shape=out_shape,
        compiler_params=pltpu.CompilerParams(vmem_limit_bytes=VMEM_LIMIT),
        cost_estimate=cost(steps * rows * heads * (TILE if whole else 16 * TILE)),
        name="attend_middle" if whole else "attend_edges",
    )(place, table, queries, *in_hbm((*local, *early)))


def far_kernel(lay, heads, place_ref, table_ref, q_ref, acc_ref, stat_ref, *refs):
    core = place_ref[1]
    local, received = refs[:4], Received(lay, core, refs[4:16])
    out_ref, kbuf, vbuf, acc_s, m_s, l_s, tk, tv, sems, exact_sems = refs[17:]
    step = pl.program_id(0)
    frame = step * (lay.here - 1)
    room = kbuf.shape[1]

    def bufs(at, i):
        return kbuf.at[at, i], vbuf.at[at, i]

    def start(at):
        base = lay.far + at * (lay.here - 1) * STRIDE

        def one(i, _):
            received.start(table_ref[base + 1 + i], lay.places, bufs(at, i), sems.at[at * room + i])
            return 0

        lax.fori_loop(0, table_ref[base], one, 0)

    @pl.when(step == 0)
    def _():
        start(0)
        start(1)

    load_stats(stat_ref, m_s, l_s, heads)
    acc_s[...] = acc_ref[0]
    base = lay.far + frame * STRIDE

    def wait(i, _):
        received.wait(bufs(step, i), sems.at[step * room + i])
        return 0

    lax.fori_loop(0, table_ref[base], wait, 0)
    attend_list(q_ref, kbuf.at[step], vbuf.at[step], table_ref, base, m_s, l_s, acc_s, heads, packed=True)

    @pl.when(jnp.max(l_s[...]) > LARGE)
    def _():
        exact_frame(lay, heads, frame, core, table_ref, q_ref, local, received, acc_s, m_s, l_s, tk, tv, exact_sems)

    finish(out_ref, acc_s, l_s, heads)


def far_call(lay, heads, place, table, queries, acc, stats, local, early, late, out):
    here, rows, width = queries.shape
    block = pl.BlockSpec((1, rows, width), lambda s, *_: (s * (here - 1), 0, 0))
    anys = [*local, *early, *late, out]
    room = sum(n for frame, column, _ in lay.remote(0) if frame == 0 for n in [lay.lengths[column]])
    room += sum(n for frame, column, _ in lay.remote(1) if frame == 0 for n in [lay.lengths[column]])
    return pl.pallas_call(
        functools.partial(far_kernel, lay, heads),
        grid_spec=pltpu.PrefetchScalarGridSpec(
            num_scalar_prefetch=2,
            grid=(2,),
            in_specs=[
                block,
                pl.BlockSpec((1, rows, width), lambda s, *_: (s, 0, 0)),
                pl.BlockSpec((1, rows, 128), lambda s, *_: (s, 0, 0)),
            ]
            + [ANY] * len(anys),
            out_specs=block,
            scratch_shapes=[
                pltpu.VMEM((2, room, 2, HALF, width), BF),
                pltpu.VMEM((2, room, 2, HALF, width), BF),
                pltpu.VMEM((rows, width), F32),
                pltpu.VMEM((heads, rows, 128), F32),
                pltpu.VMEM((heads, rows, 128), F32),
                pltpu.VMEM((2, HALF, width), BF),
                pltpu.VMEM((2, HALF, width), BF),
                pltpu.SemaphoreType.DMA((2 * room, 4)),
                pltpu.SemaphoreType.DMA((4,)),
            ],
        ),
        out_shape=jax.ShapeDtypeStruct((here, rows, width), BF),
        input_output_aliases={5 + len(anys) - 1: 0},
        compiler_params=pltpu.CompilerParams(vmem_limit_bytes=VMEM_LIMIT),
        cost_estimate=cost(2 * rows * heads * 7 * TILE),
        name="attend_late",
    )(place, table, queries, acc, stats, *in_hbm(anys[:-1]), out)


def in_hbm(arrays):
    return [pltpu.with_memory_space_constraint(a, pltpu.HBM) for a in arrays]


def paired(block, way):
    pairs = range(way, lax.axis_size("frame") - 1, 2)
    return lax.ppermute(block, "frame", [p for i in pairs for p in ((i, i + 1), (i + 1, i))])


def swapped(block):
    return lax.ppermute(block, "seq", [(0, 1), (1, 0)])


def per_device(queries, key_rows, value_rows, list_one, list_two, list_four, tile_counts):
    here, rows, width = queries.shape
    heads = width // HEAD_DIM
    frames = list_one.shape[0]
    lists = (list_one, list_two, list_four)
    lay = Layout(here, 2 * rows // TILE, frames, tuple(a.shape[2] for a in lists))
    core = lax.axis_index("seq")
    place = jnp.stack([lax.axis_index("frame") * here, core]).astype(jnp.int32)

    k_own, v_own = (a.reshape(here, lay.half, 2, HALF, width) for a in (key_rows, value_rows))
    k_other = swapped(k_own)
    by_frame = [jnp.transpose(a, (1, 2, 0)) for a in lists] + [jnp.transpose(tile_counts, (2, 1, 0))]
    table = make_table(lay, place, by_frame)

    def both_ways(pair):
        return paired(pair[0], 0), paired(pair[1], 1)

    def both_cores(pair):
        return (*pair, *map(swapped, pair))

    k_other, v_own, table = lax.optimization_barrier((k_other, v_own, table))
    v_other = swapped(v_own)
    (first,) = pack_call(lay, [[(0, 0, lay.early)]], place, table, (k_own, k_other))
    first, table = lax.optimization_barrier((first, table))
    first = both_ways(first)
    at = lay.early + lay.second
    rest = [
        [(1, 0, lay.early), (0, lay.early, lay.second), (1, lay.early, lay.second)],
        [(0, at, lay.third), (1, at, lay.third)],
    ]
    second, third = pack_call(lay, rest, place, table, (k_own, k_other, v_own, v_other))
    second, third = both_ways(second), both_ways(third)

    local = (k_own, k_other, v_own, v_other)
    first, table = lax.optimization_barrier((first, table))
    acc, stats = near_call(lay, heads, False, place, table, queries, local)
    second, stats = lax.optimization_barrier((second, stats))
    early = (*both_cores(first), *both_cores(second))
    (out,) = near_call(lay, heads, True, place, table, queries, local, early)
    third, out = lax.optimization_barrier((third, out))
    return far_call(lay, heads, place, table, queries, acc, stats, local, early, both_cores(third), out)


def solution(mesh):
    placed = (
        P(("clips", "frame"), "seq", "head"),
        P(("clips", "frame"), "seq", "head"),
        P(("clips", "frame"), "seq", "head"),
        P("clips", None, None),
        P("clips", None, None),
        P("clips", None, None),
        P("clips", None, None),
    )
    return jax.shard_map(
        per_device,
        mesh=mesh,
        in_specs=placed,
        out_specs=P(("clips", "frame"), "seq", "head"),
        check_vma=False,
    )
```

```python
import functools
import math

import jax
import jax.numpy as jnp
from jax import lax
from jax.experimental import pallas as pl
from jax.experimental.pallas import tpu as pltpu
from jax.sharding import PartitionSpec as P

HEAD_DIM = 128
TILE = 128
DISTANCES = (1, 2, 4)
STRIDE = 24
SCALE = math.log2(math.e) / math.sqrt(HEAD_DIM)
LARGE = 2.0**100
NT = (((1,), (1,)), ((), ()))
BF = jnp.bfloat16
F32 = jnp.float32
ANY = pl.BlockSpec(memory_space=pl.ANY)
SMEM = pl.BlockSpec(memory_space=pltpu.SMEM)
VMEM_LIMIT = 48 * 2**20
PACK_LIMIT = 16 * 2**20


class Layout:
    def __init__(self, frames_here, frame_tiles, frames, lengths):
        self.here = frames_here
        self.tiles = frame_tiles
        self.half = frame_tiles // 2
        self.own = frames_here * frame_tiles
        self.frames = frames
        self.lengths = lengths
        self.early = self.late = 0
        for frame, column, _ in self.remote(0):
            if self.edge(frame):
                self.late += lengths[column]
            else:
                self.early += lengths[column]
        self.places = self.early + self.late
        self.first = self.early + self.late // 4
        self.second = self.places - self.first
        self.near = 2 * self.places
        self.far = self.near + frames_here * STRIDE
        self.size = self.far + frames_here * STRIDE

    def edge(self, frame):
        return frame in (0, self.here - 1)

    def remote(self, direction):
        found = []
        for away in (*range(1, self.here - 1), self.here - 1, 0):
            for column in reversed(range(3)):
                distance = DISTANCES[column]
                if away < distance:
                    frame = away if direction == 0 else self.here - 1 - away
                    source = frame - distance if direction == 0 else frame + distance
                    found.append((frame, column, source % self.here))
        return found


def table_kernel(lay, place_ref, one_ref, two_ref, four_ref, count_ref, table_ref, seen_ref):
    lists = (one_ref, two_ref, four_ref)
    first = place_ref[0]
    odd = first // lay.here % 2

    def distinct(target, direction, on_slot, on_new):
        for i in range(lay.own):
            seen_ref[i] = -1
        used = jnp.int32(0)
        for frame, column, source in lay.remote(direction):
            live = count_ref[column, direction, target + frame]
            for slot in range(lay.lengths[column]):
                name = lists[column][direction, slot, target + frame] + source * lay.tiles
                alive = slot < live
                known = seen_ref[name]
                fresh = jnp.logical_and(alive, known < 0)
                place = jnp.where(fresh, used, known)
                seen_ref[name] = place
                on_new(used, name)
                on_slot(frame, place, alive)
                used = used + fresh.astype(jnp.int32)
        return used

    filled = {}

    def append(base, frame, item, alive):
        at = base + frame * STRIDE
        count = filled.get(at, jnp.int32(0))
        table_ref[at + 1 + count] = item
        filled[at] = count + alive.astype(jnp.int32)

    for direction in (0, 1):
        target = first + (lay.here if direction == 0 else -lay.here)
        target = jnp.clip(target, 0, lay.frames - lay.here)
        begin = (odd + direction) % 2 * lay.places
        for place in range(lay.places):
            table_ref[begin + place] = 0

        def note(used, name, begin=begin):
            table_ref[begin + jnp.minimum(used, lay.places - 1)] = name

        distinct(target, direction, lambda *_: None, note)

    for direction in (0, 1):
        way = (odd + 1 - direction) % 2

        def on_slot(frame, place, alive, way=way):
            if lay.edge(frame):
                append(lay.far, frame, way * lay.places + place, alive)
            else:
                append(lay.near, frame, lay.own + way * lay.early + place, alive)

        distinct(first, direction, on_slot, lambda *_: None)
        for frame in range(lay.here):
            for column, distance in enumerate(DISTANCES):
                source = frame + (2 * direction - 1) * distance
                if 0 <= source < lay.here:
                    live = count_ref[column, direction, first + frame]
                    for slot in range(lay.lengths[column]):
                        name = lists[column][direction, slot, first + frame]
                        append(lay.near, frame, source * lay.tiles + name, slot < live)
    for frame in range(lay.here):
        for base in (lay.near, lay.far):
            at = base + frame * STRIDE
            table_ref[at] = filled.get(at, jnp.int32(0))


def make_table(lay, place, lists):
    return pl.pallas_call(
        functools.partial(table_kernel, lay),
        in_specs=[SMEM] * 5,
        out_specs=SMEM,
        out_shape=jax.ShapeDtypeStruct((lay.size,), jnp.int32),
        scratch_shapes=[pltpu.SMEM((lay.own,), jnp.int32)],
        compiler_params=pltpu.CompilerParams(vmem_limit_bytes=VMEM_LIMIT),
        name="tile_tables",
    )(place, *lists)


def columns(core, width):
    return pl.ds(pl.multiple_of(core * width, HEAD_DIM), width)


def pack_kernel(lay, begin, length, place_ref, table_ref, k_own, k_other, v_own, v_other, *refs):
    outs, sems = refs[:2], refs[2]
    core = place_ref[1]
    cols = columns(core, outs[0].shape[-1])
    waits = []
    for way, out in enumerate(outs):
        for item in range(length):
            name = table_ref[way * lay.places + begin + item]
            frame = name // lay.tiles
            tile = name % lay.tiles
            mine = tile // lay.half == core
            tile = tile % lay.half
            for kv, (own, other) in enumerate(((k_own, k_other), (v_own, v_other))):
                target = out.at[kv * length + item]
                sem = sems.at[len(waits)]
                here = pltpu.make_async_copy(own.at[frame, tile, :, cols], target, sem)
                there = pltpu.make_async_copy(other.at[frame, tile], target, sem)
                pl.when(mine)(here.start)
                pl.when(jnp.logical_not(mine))(there.start)
                waits.append(here)
    for copy in waits:
        copy.wait()


def pack_call(lay, begin, length, place, table, local):
    shape = jax.ShapeDtypeStruct((2 * length, TILE, local[1].shape[-1]), BF)
    return pl.pallas_call(
        functools.partial(pack_kernel, lay, begin, length),
        in_specs=[SMEM] * 2 + [ANY] * 4,
        out_specs=[pl.BlockSpec(memory_space=pltpu.VMEM)] * 2,
        out_shape=[shape] * 2,
        scratch_shapes=[pltpu.SemaphoreType.DMA((4 * length,))],
        compiler_params=pltpu.CompilerParams(vmem_limit_bytes=PACK_LIMIT),
        name="pack_tiles",
    )(place, table, *in_hbm(local))


def rows_of(buf, index, cols):
    tiles = buf[index, :, cols]
    return tiles.reshape(tiles.size // HEAD_DIM, HEAD_DIM)


def units(heads):
    for part in (0, 1):
        for head in range(heads):
            yield part * heads + head, part, slice(head * HEAD_DIM, (head + 1) * HEAD_DIM)


def mix(weights, values):
    return jnp.dot(
        weights.astype(BF),
        jnp.concatenate([values, jnp.ones_like(values)], axis=1),
        preferred_element_type=F32,
    )


def attend_tiles(q_refs, kbuf, vbuf, ids, m_s, l_s, acc_s, heads):
    for unit, part, cols in units(heads):
        keys = jnp.concatenate([rows_of(kbuf, i, cols) for i in ids], axis=0)
        values = jnp.concatenate([rows_of(vbuf, i, cols) for i in ids], axis=0)
        scores = lax.dot_general(q_refs[part][0, :, cols], keys, NT, preferred_element_type=F32)
        shift = jnp.concatenate([m_s[unit]] * len(ids), axis=1)
        mixed = mix(jnp.exp2((scores - shift) * SCALE), values)
        acc_s[unit] += mixed[:, :HEAD_DIM]
        l_s[unit] += mixed[:, HEAD_DIM:]


def attend_list(q_refs, kbuf, vbuf, table_ref, base, m_s, l_s, acc_s, heads, packed=False):
    count = table_ref[base]

    def add(start, n):
        ids = [start + j if packed else table_ref[base + 1 + start + j] for j in range(n)]
        attend_tiles(q_refs, kbuf, vbuf, ids, m_s, l_s, acc_s, heads)

    def four(i, _):
        add(4 * i, 4)
        return 0

    lax.fori_loop(0, count // 4, four, 0)

    @pl.when(count % 4 >= 2)
    def _():
        add(count // 4 * 4, 2)

    @pl.when(count % 2 == 1)
    def _():
        add(count - 1, 1)


def attend_own(lay, q_refs, kbuf, vbuf, frame, m_s, l_s, acc_s, heads):
    own = pl.ds(frame * lay.tiles, lay.tiles)
    for unit, part, cols in units(heads):
        scores = lax.dot_general(
            q_refs[part][0, :, cols], rows_of(kbuf, own, cols), NT, preferred_element_type=F32
        )
        top = jnp.max(scores[:, :TILE], axis=1, keepdims=True)
        mixed = mix(jnp.exp2((scores - top) * SCALE), rows_of(vbuf, own, cols))
        acc_s[unit] = mixed[:, :HEAD_DIM]
        l_s[unit] = mixed[:, HEAD_DIM:]
        m_s[unit] = jnp.broadcast_to(top, m_s.shape[1:])


def save_stats(stat_ref, m_s, l_s, heads):
    rows = stat_ref.shape[1]
    lane = lax.broadcasted_iota(jnp.int32, (rows, 128), 1)
    stat = jnp.zeros((rows, 128), F32)
    for unit, _, _ in units(heads):
        stat = jnp.where(lane == unit, l_s[unit], stat)
        stat = jnp.where(lane == 64 + unit, m_s[unit], stat)
    stat_ref[0] = stat


def load_stats(stat_ref, m_s, l_s, heads):
    rows = stat_ref.shape[1]
    for unit, _, _ in units(heads):
        l_s[unit] = jnp.broadcast_to(stat_ref[0, :, unit : unit + 1], (rows, 128))
        m_s[unit] = jnp.broadcast_to(stat_ref[0, :, 64 + unit : 65 + unit], (rows, 128))


def finish(out_refs, acc_s, l_s, heads):
    for unit, part, cols in units(heads):
        out_refs[part][0, :, cols] = (acc_s[unit] / l_s[unit]).astype(BF)


def local_copies(lay, index, core, local, bufs, sems):
    found = []
    for kv, buf in enumerate(bufs):
        own = local[2 * kv].at[index, :, :, columns(core, buf.shape[-1])]
        for side, source in enumerate((own, local[2 * kv + 1].at[index])):
            owner = core if side == 0 else 1 - core
            target = buf.at[pl.ds(index * lay.tiles + owner * lay.half, lay.half)]
            found.append(pltpu.make_async_copy(source, target, sems.at[index, 2 * kv + side]))
    return found


class Received:
    def __init__(self, lay, refs):
        self.lay = lay
        self.parts = [(0, lay.first, refs[:2])]
        if len(refs) > 2:
            self.parts.append((lay.first, lay.second, refs[2:4]))

    def early_copies(self, bufs, sems):
        _, size, refs = self.parts[0]
        found = []
        for kv, buf in enumerate(bufs):
            for way in (0, 1):
                source = refs[way].at[pl.ds(kv * size, self.lay.early)]
                target = buf.at[pl.ds(self.lay.own + way * self.lay.early, self.lay.early)]
                found.append(pltpu.make_async_copy(source, target, sems.at[len(found)]))
        return found

    def start(self, item, length, targets, sems):
        place = item % length
        for way in (0, 1):
            for begin, size, refs in self.parts:
                inside = jnp.logical_and(place >= begin, place < begin + size)

                @pl.when(jnp.logical_and(item // length == way, inside))
                def _(way=way, begin=begin, size=size, refs=refs):
                    for kv, target in enumerate(targets):
                        source = refs[way].at[place - begin + kv * size]
                        pltpu.make_async_copy(source, target, sems.at[kv]).start()

    def wait(self, targets, sems):
        for kv, target in enumerate(targets):
            pltpu.make_async_copy(self.parts[0][2][0].at[0], target, sems.at[kv]).wait()


def exact_frame(lay, heads, frame, core, table_ref, q_refs, local, received, acc_s, m_s, l_s, tk, tv, sems):
    m_s[...] = jnp.full(m_s.shape, -jnp.inf, F32)
    l_s[...] = jnp.zeros(l_s.shape, F32)
    acc_s[...] = jnp.zeros(acc_s.shape, F32)

    def add_tile():
        for unit, part, cols in units(heads):
            scores = lax.dot_general(
                q_refs[part][0, :, cols], tk[:, cols], NT, preferred_element_type=F32
            )
            before = m_s[unit]
            top = jnp.maximum(before, jnp.max(scores, axis=1, keepdims=True))
            fade = jnp.exp2((before - top) * SCALE)
            mixed = mix(jnp.exp2((scores - top) * SCALE), tv[:, cols])
            acc_s[unit] = acc_s[unit] * fade + mixed[:, :HEAD_DIM]
            l_s[unit] = l_s[unit] * fade + mixed[:, HEAD_DIM:]
            m_s[unit] = top

    def near_tile(name):
        source, tile = name // lay.tiles, name % lay.tiles
        mine = tile // lay.half == core
        tile = tile % lay.half
        cols = columns(core, tk.shape[-1])
        for side in (0, 1):

            @pl.when(mine if side == 0 else jnp.logical_not(mine))
            def _(side=side):
                at = (source, tile, slice(None), cols) if side == 0 else (source, tile)
                found = [
                    pltpu.make_async_copy(local[2 * kv + side].at[at], buf, sems.at[kv])
                    for kv, buf in enumerate((tk, tv))
                ]
                for copy in found:
                    copy.start()
                for copy in found:
                    copy.wait()

    def far_tile(item, length):
        received.start(item, length, (tk, tv), sems)
        received.wait((tk, tv), sems)

    def own_step(i, _):
        near_tile(frame * lay.tiles + i)
        add_tile()
        return 0

    def near_step(i, _):
        name = table_ref[lay.near + frame * STRIDE + 1 + i]

        @pl.when(name < lay.own)
        def _():
            near_tile(name)

        @pl.when(name >= lay.own)
        def _():
            far_tile(name - lay.own, lay.early)

        add_tile()
        return 0

    def far_step(i, _):
        far_tile(table_ref[lay.far + frame * STRIDE + 1 + i], lay.places)
        add_tile()
        return 0

    lax.fori_loop(0, lay.tiles, own_step, 0)
    lax.fori_loop(0, table_ref[lay.near + frame * STRIDE], near_step, 0)
    if len(received.parts) > 1:
        lax.fori_loop(0, table_ref[lay.far + frame * STRIDE], far_step, 0)


def near_kernel(lay, heads, whole, place_ref, table_ref, q_own, q_other, *refs):
    core = place_ref[1]
    q_refs = (q_own, q_other)
    local, refs = refs[:4], refs[4:]
    if whole:
        received, out_refs, refs = Received(lay, refs[:2]), refs[2:4], refs[4:]
        acc_s, kbuf, vbuf, m_s, l_s, sems, tk, tv, far_sems = refs
    else:
        acc_out, stat_ref, kbuf, vbuf, m_s, l_s, sems = refs
        acc_s = acc_out.at[0]
    step = pl.program_id(0)
    frame = step + 1 if whole else step * (lay.here - 1)
    begin = 1 if whole else 0

    def first():
        return local_copies(lay, begin, core, local, (kbuf, vbuf), sems)

    def others():
        found = []
        for index in range(lay.here):
            if index != begin:
                found += local_copies(lay, index, core, local, (kbuf, vbuf), sems)
        return found + (received.early_copies((kbuf, vbuf), far_sems) if whole else [])

    @pl.when(step == 0)
    def _():
        for copy in first():
            copy.start()
        for copy in first():
            copy.wait()
        for copy in others():
            copy.start()

    attend_own(lay, q_refs, kbuf, vbuf, frame, m_s, l_s, acc_s, heads)

    @pl.when(step == 0)
    def _():
        for copy in others():
            copy.wait()

    attend_list(q_refs, kbuf, vbuf, table_ref, lay.near + frame * STRIDE, m_s, l_s, acc_s, heads)
    if whole:

        @pl.when(jnp.max(l_s[...]) > LARGE)
        def _():
            exact_frame(lay, heads, frame, core, table_ref, q_refs, local, received, acc_s, m_s, l_s, tk, tv, far_sems)

        finish(out_refs, acc_s, l_s, heads)
    else:
        save_stats(stat_ref, m_s, l_s, heads)


def cost(scores):
    return pl.CostEstimate(flops=scores * 4 * HEAD_DIM, bytes_accessed=scores // 8, transcendentals=scores)


def token_blocks(rows, width, frame_of):
    return (
        pl.BlockSpec((1, rows, width), lambda s, place, _: (frame_of(s), 0, place[1])),
        pl.BlockSpec((1, rows, width), lambda s, *_: (frame_of(s), 0, 0)),
    )


def near_call(lay, heads, whole, place, table, queries, local, early=()):
    here, rows, width = queries[1].shape
    steps = here - 2 if whole else 2
    own, other = token_blocks(rows, width, (lambda s: s + 1) if whole else (lambda s: s * (here - 1)))
    count = lay.own + (2 * lay.early if whole else 0)
    bufs = [pltpu.VMEM((count, TILE, width), BF)] * 2
    sums = [pltpu.VMEM((2 * heads, rows, 128), F32)] * 2
    sems = [pltpu.SemaphoreType.DMA((here, 4))]
    if whole:
        out_specs = [own, pl.BlockSpec((1, rows, width), lambda s, *_: (s, 0, 0))]
        out_shape = [jax.ShapeDtypeStruct(queries[0].shape, BF), jax.ShapeDtypeStruct((steps, rows, width), BF)]
        scratch = [sums[0], *bufs, *sums, *sems]
        scratch += [pltpu.VMEM((TILE, width), BF)] * 2 + [pltpu.SemaphoreType.DMA((4,))]
    else:
        out_specs = [
            pl.BlockSpec((1, 2 * heads, rows, 128), lambda s, *_: (s, 0, 0, 0)),
            pl.BlockSpec((1, rows, 128), lambda s, *_: (s, 0, 0)),
        ]
        out_shape = [jax.ShapeDtypeStruct((2, 2 * heads, rows, 128), F32), jax.ShapeDtypeStruct((2, rows, 128), F32)]
        scratch = [*bufs, *sums, *sems]
    return pl.pallas_call(
        functools.partial(near_kernel, lay, heads, whole),
        grid_spec=pltpu.PrefetchScalarGridSpec(
            num_scalar_prefetch=2,
            grid=(steps,),
            in_specs=[own, other] + [ANY] * (4 + len(early)),
            out_specs=out_specs,
            scratch_shapes=scratch,
        ),
        out_shape=out_shape,
        compiler_params=pltpu.CompilerParams(vmem_limit_bytes=VMEM_LIMIT),
        cost_estimate=cost(steps * rows * heads * 32 * TILE),
        name="attend_middle" if whole else "attend_edges",
    )(place, table, *queries, *in_hbm((*local, *early)))


def far_kernel(lay, heads, place_ref, table_ref, q_own, q_other, acc_ref, stat_ref, *refs):
    core = place_ref[1]
    q_refs = (q_own, q_other)
    local, received, out_refs = refs[:4], Received(lay, refs[4:8]), refs[9:11]
    kbuf, vbuf, acc_s, m_s, l_s, tk, tv, sems, exact_sems = refs[11:]
    step = pl.program_id(0)
    frame = step * (lay.here - 1)
    room = kbuf.shape[1]

    def bufs(at, i):
        return kbuf.at[at, i], vbuf.at[at, i]

    def start(at):
        base = lay.far + at * (lay.here - 1) * STRIDE

        def one(i, _):
            received.start(table_ref[base + 1 + i], lay.places, bufs(at, i), sems.at[at * room + i])
            return 0

        lax.fori_loop(0, table_ref[base], one, 0)

    @pl.when(step == 0)
    def _():
        start(0)
        start(1)

    load_stats(stat_ref, m_s, l_s, heads)
    acc_s[...] = acc_ref[0]
    base = lay.far + frame * STRIDE

    def wait(i, _):
        received.wait(bufs(step, i), sems.at[step * room + i])
        return 0

    lax.fori_loop(0, table_ref[base], wait, 0)
    attend_list(q_refs, kbuf.at[step], vbuf.at[step], table_ref, base, m_s, l_s, acc_s, heads, packed=True)

    @pl.when(jnp.max(l_s[...]) > LARGE)
    def _():
        exact_frame(lay, heads, frame, core, table_ref, q_refs, local, received, acc_s, m_s, l_s, tk, tv, exact_sems)

    finish(out_refs, acc_s, l_s, heads)


def far_call(lay, heads, place, table, queries, acc, stats, local, early, late, out):
    here, rows, width = queries[1].shape
    own, other = token_blocks(rows, width, lambda s: s * (here - 1))
    anys = [*local, *early, *late]
    room = sum(lay.lengths[column] for way in (0, 1) for frame, column, _ in lay.remote(way) if frame == 0)
    sums = pltpu.VMEM((2 * heads, rows, 128), F32)
    return pl.pallas_call(
        functools.partial(far_kernel, lay, heads),
        grid_spec=pltpu.PrefetchScalarGridSpec(
            num_scalar_prefetch=2,
            grid=(2,),
            in_specs=[
                own,
                other,
                pl.BlockSpec((1, 2 * heads, rows, 128), lambda s, *_: (s, 0, 0, 0)),
                pl.BlockSpec((1, rows, 128), lambda s, *_: (s, 0, 0)),
            ]
            + [ANY] * (len(anys) + 1),
            out_specs=[own, pl.BlockSpec((1, rows, width), lambda s, *_: (s, 0, 0))],
            scratch_shapes=[
                pltpu.VMEM((2, room, TILE, width), BF),
                pltpu.VMEM((2, room, TILE, width), BF),
                sums,
                sums,
                sums,
                pltpu.VMEM((TILE, width), BF),
                pltpu.VMEM((TILE, width), BF),
                pltpu.SemaphoreType.DMA((2 * room, 2)),
                pltpu.SemaphoreType.DMA((2,)),
            ],
        ),
        out_shape=[jax.ShapeDtypeStruct(out.shape, BF), jax.ShapeDtypeStruct((2, rows, width), BF)],
        input_output_aliases={6 + len(anys): 0},
        compiler_params=pltpu.CompilerParams(vmem_limit_bytes=VMEM_LIMIT),
        cost_estimate=cost(2 * rows * heads * 14 * TILE),
        name="attend_late",
    )(place, table, *queries, acc, stats, *in_hbm(anys), out)


def place_kernel(place_ref, block_ref, _, out_ref):
    out_ref[...] = block_ref[...]


def place_call(place, blocks, out, frame_of):
    steps, rows, width = blocks.shape
    return pl.pallas_call(
        place_kernel,
        grid_spec=pltpu.PrefetchScalarGridSpec(
            num_scalar_prefetch=1,
            grid=(steps,),
            in_specs=[pl.BlockSpec((1, rows, width), lambda s, place: (s, 0, 0)), ANY],
            out_specs=pl.BlockSpec((1, rows, width), lambda s, place: (frame_of(s), 0, 1 - place[1])),
        ),
        out_shape=jax.ShapeDtypeStruct(out.shape, BF),
        input_output_aliases={2: 0},
        compiler_params=pltpu.CompilerParams(vmem_limit_bytes=VMEM_LIMIT),
        name="place_columns",
    )(place, blocks, out)


def in_hbm(arrays):
    return [pltpu.with_memory_space_constraint(a, pltpu.HBM) for a in arrays]


def paired(block, way):
    pairs = range(way, lax.axis_size("frame") - 1, 2)
    return lax.ppermute(block, "frame", [p for i in pairs for p in ((i, i + 1), (i + 1, i))])


def swapped(block):
    return lax.ppermute(block, "seq", [(0, 1), (1, 0)])


def per_device(queries, key_rows, value_rows, list_one, list_two, list_four, tile_counts):
    here, rows, width = queries.shape
    heads = -(-width // HEAD_DIM // 2)
    part = heads * HEAD_DIM
    frames = list_one.shape[0]
    lists = (list_one, list_two, list_four)
    lay = Layout(here, 2 * rows // TILE, frames, tuple(a.shape[2] for a in lists))
    core = lax.axis_index("seq")
    place = jnp.stack([lax.axis_index("frame") * here, core]).astype(jnp.int32)
    if width < 2 * part:
        spare = ((0, 0), (0, 0), (0, 2 * part - width))
        queries, key_rows, value_rows = (jnp.pad(a, spare) for a in (queries, key_rows, value_rows))

    def exchanged(a):
        return swapped(lax.dynamic_slice_in_dim(a, (1 - core) * part, part, axis=2))

    def tiled(a):
        return a.reshape(here, lay.half, TILE, a.shape[2])

    k_other = tiled(exchanged(key_rows))
    v_other = tiled(exchanged(value_rows))
    queries = (queries, exchanged(queries))
    by_frame = [jnp.transpose(a, (1, 2, 0)) for a in lists] + [jnp.transpose(tile_counts, (2, 1, 0))]
    table = make_table(lay, place, by_frame)
    local = (tiled(key_rows), k_other, tiled(value_rows), v_other)

    def both_ways(pair):
        return paired(pair[0], 0), paired(pair[1], 1)

    early = pack_call(lay, 0, lay.first, place, table, local)
    early, table = lax.optimization_barrier((early, table))
    early = both_ways(early)
    late = both_ways(pack_call(lay, lay.first, lay.second, place, table, local))
    acc, stats = near_call(lay, heads, False, place, table, queries, local)
    early, stats = lax.optimization_barrier((early, stats))
    out, sent = near_call(lay, heads, True, place, table, queries, local, early)
    late, sent = lax.optimization_barrier((late, sent))
    middle = swapped(sent)
    out, sent = far_call(lay, heads, place, table, queries, acc, stats, local, early, late, out)
    out = place_call(place, middle, out, lambda s: s + 1)
    out = place_call(place, swapped(sent), out, lambda s: s * (here - 1))
    return out[:, :, :width]


def solution(mesh):
    placed = (
        P(("clips", "frame"), "seq", "head"),
        P(("clips", "frame"), "seq", "head"),
        P(("clips", "frame"), "seq", "head"),
        P("clips", None, None),
        P("clips", None, None),
        P("clips", None, None),
        P("clips", None, None),
    )
    return jax.shard_map(
        per_device,
        mesh=mesh,
        in_specs=placed,
        out_specs=P(("clips", "frame"), "seq", "head"),
        check_vma=False,
    )
```

```python
import functools
import math

import jax
import jax.numpy as jnp
from jax import lax
from jax.experimental import pallas as pl
from jax.experimental.pallas import tpu as pltpu
from jax.sharding import PartitionSpec as P

HEAD_DIM = 128
TILE = 128
DISTANCES = (1, 2, 4)
STRIDE = 24
SCALE = math.log2(math.e) / math.sqrt(HEAD_DIM)
LARGE = 2.0**100
NT = (((1,), (1,)), ((), ()))
BF = jnp.bfloat16
F32 = jnp.float32
ANY = pl.BlockSpec(memory_space=pl.ANY)
SMEM = pl.BlockSpec(memory_space=pltpu.SMEM)
VMEM_LIMIT = 48 * 2**20
PACK_LIMIT = 16 * 2**20


class Layout:
    def __init__(self, frames_here, frame_tiles, frames, lengths):
        self.here = frames_here
        self.tiles = frame_tiles
        self.half = frame_tiles // 2
        self.own = frames_here * frame_tiles
        self.frames = frames
        self.lengths = lengths
        self.early = self.late = 0
        for frame, column, _ in self.remote(0):
            if self.edge(frame):
                self.late += lengths[column]
            else:
                self.early += lengths[column]
        self.places = self.early + self.late
        self.first = self.early + self.late // 4
        self.second = self.places - self.first
        self.near = 2 * self.places
        self.far = self.near + frames_here * STRIDE
        self.size = self.far + frames_here * STRIDE

    def edge(self, frame):
        return frame in (0, self.here - 1)

    def remote(self, direction):
        found = []
        for away in (*range(1, self.here - 1), self.here - 1, 0):
            for column in reversed(range(3)):
                distance = DISTANCES[column]
                if away < distance:
                    frame = away if direction == 0 else self.here - 1 - away
                    source = frame - distance if direction == 0 else frame + distance
                    found.append((frame, column, source % self.here))
        return found


def table_kernel(lay, place_ref, one_ref, two_ref, four_ref, count_ref, table_ref, seen_ref):
    lists = (one_ref, two_ref, four_ref)
    first = place_ref[0]
    odd = first // lay.here % 2

    def distinct(target, direction, on_slot, on_new):
        for i in range(lay.own):
            seen_ref[i] = -1
        used = jnp.int32(0)
        for frame, column, source in lay.remote(direction):
            live = count_ref[column, direction, target + frame]
            for slot in range(lay.lengths[column]):
                name = lists[column][direction, slot, target + frame] + source * lay.tiles
                alive = slot < live
                known = seen_ref[name]
                fresh = jnp.logical_and(alive, known < 0)
                place = jnp.where(fresh, used, known)
                seen_ref[name] = place
                on_new(used, name)
                on_slot(frame, place, alive)
                used = used + fresh.astype(jnp.int32)
        return used

    filled = {}

    def append(base, frame, item, alive):
        at = base + frame * STRIDE
        count = filled.get(at, jnp.int32(0))
        table_ref[at + 1 + count] = item
        filled[at] = count + alive.astype(jnp.int32)

    for direction in (0, 1):
        target = first + (lay.here if direction == 0 else -lay.here)
        target = jnp.clip(target, 0, lay.frames - lay.here)
        begin = (odd + direction + 1) % 2 * lay.places
        for place in range(lay.places):
            table_ref[begin + place] = 0

        def note(used, name, begin=begin):
            table_ref[begin + jnp.minimum(used, lay.places - 1)] = name

        distinct(target, direction, lambda *_: None, note)

    for direction in (0, 1):
        way = (odd + direction) % 2

        def on_slot(frame, place, alive, way=way):
            if lay.edge(frame):
                append(lay.far, frame, way * lay.places + place, alive)
            else:
                append(lay.near, frame, lay.own + way * lay.early + place, alive)

        distinct(first, direction, on_slot, lambda *_: None)
        for frame in range(lay.here):
            for column, distance in enumerate(DISTANCES):
                source = frame + (2 * direction - 1) * distance
                if 0 <= source < lay.here:
                    live = count_ref[column, direction, first + frame]
                    for slot in range(lay.lengths[column]):
                        name = lists[column][direction, slot, first + frame]
                        append(lay.near, frame, source * lay.tiles + name, slot < live)
    for frame in range(lay.here):
        for base in (lay.near, lay.far):
            at = base + frame * STRIDE
            table_ref[at] = filled.get(at, jnp.int32(0))


def make_table(lay, place, lists):
    return pl.pallas_call(
        functools.partial(table_kernel, lay),
        in_specs=[SMEM] * 5,
        out_specs=SMEM,
        out_shape=jax.ShapeDtypeStruct((lay.size,), jnp.int32),
        scratch_shapes=[pltpu.SMEM((lay.own,), jnp.int32)],
        compiler_params=pltpu.CompilerParams(vmem_limit_bytes=VMEM_LIMIT),
        name="tile_tables",
    )(place, *lists)


def columns(core, width):
    return pl.ds(pl.multiple_of(core * width, HEAD_DIM), width)


def pack_kernel(lay, begin, length, place_ref, table_ref, k_own, k_other, v_own, v_other, *refs):
    outs, sems = refs[:2], refs[2]
    core = place_ref[1]
    cols = columns(core, outs[0].shape[-1])
    waits = []
    for way, out in enumerate(outs):
        for item in range(length):
            name = table_ref[way * lay.places + begin + item]
            frame = name // lay.tiles
            tile = name % lay.tiles
            mine = tile // lay.half == core
            tile = tile % lay.half
            for kv, (own, other) in enumerate(((k_own, k_other), (v_own, v_other))):
                target = out.at[kv * length + item]
                sem = sems.at[len(waits)]
                here = pltpu.make_async_copy(own.at[frame, tile, :, cols], target, sem)
                there = pltpu.make_async_copy(other.at[frame, tile], target, sem)
                pl.when(mine)(here.start)
                pl.when(jnp.logical_not(mine))(there.start)
                waits.append(here)
    for copy in waits:
        copy.wait()


def pack_call(lay, begin, length, place, table, local):
    shape = jax.ShapeDtypeStruct((2 * length, TILE, local[1].shape[-1]), BF)
    return pl.pallas_call(
        functools.partial(pack_kernel, lay, begin, length),
        in_specs=[SMEM] * 2 + [ANY] * 4,
        out_specs=[pl.BlockSpec(memory_space=pltpu.VMEM)] * 2,
        out_shape=[shape] * 2,
        scratch_shapes=[pltpu.SemaphoreType.DMA((4 * length,))],
        compiler_params=pltpu.CompilerParams(vmem_limit_bytes=PACK_LIMIT),
        name="pack_tiles",
    )(place, table, *in_hbm(local))


def rows_of(buf, index, cols):
    tiles = buf[index, :, cols]
    return tiles.reshape(tiles.size // HEAD_DIM, HEAD_DIM)


def units(heads):
    for part in (0, 1):
        for head in range(heads):
            yield part * heads + head, part, slice(head * HEAD_DIM, (head + 1) * HEAD_DIM)


def mix(weights, values):
    return jnp.dot(
        weights.astype(BF),
        jnp.concatenate([values, jnp.ones_like(values)], axis=1),
        preferred_element_type=F32,
    )


def attend_tiles(q_refs, kbuf, vbuf, ids, m_s, l_s, acc_s, heads):
    for unit, part, cols in units(heads):
        keys = jnp.concatenate([rows_of(kbuf, i, cols) for i in ids], axis=0)
        values = jnp.concatenate([rows_of(vbuf, i, cols) for i in ids], axis=0)
        scores = lax.dot_general(q_refs[part][0, :, cols], keys, NT, preferred_element_type=F32)
        shift = jnp.concatenate([m_s[unit]] * len(ids), axis=1)
        mixed = mix(jnp.exp2((scores - shift) * SCALE), values)
        acc_s[unit] += mixed[:, :HEAD_DIM]
        l_s[unit] += mixed[:, HEAD_DIM:]


def attend_list(q_refs, kbuf, vbuf, table_ref, base, m_s, l_s, acc_s, heads, packed=False):
    count = table_ref[base]

    def add(start, n):
        ids = [start + j if packed else table_ref[base + 1 + start + j] for j in range(n)]
        attend_tiles(q_refs, kbuf, vbuf, ids, m_s, l_s, acc_s, heads)

    def four(i, _):
        add(4 * i, 4)
        return 0

    lax.fori_loop(0, count // 4, four, 0)

    @pl.when(count % 4 >= 2)
    def _():
        add(count // 4 * 4, 2)

    @pl.when(count % 2 == 1)
    def _():
        add(count - 1, 1)


def attend_own(lay, q_refs, kbuf, vbuf, frame, m_s, l_s, acc_s, heads):
    own = pl.ds(frame * lay.tiles, lay.tiles)
    for unit, part, cols in units(heads):
        scores = lax.dot_general(
            q_refs[part][0, :, cols], rows_of(kbuf, own, cols), NT, preferred_element_type=F32
        )
        top = jnp.max(scores[:, :TILE], axis=1, keepdims=True)
        mixed = mix(jnp.exp2((scores - top) * SCALE), rows_of(vbuf, own, cols))
        acc_s[unit] = mixed[:, :HEAD_DIM]
        l_s[unit] = mixed[:, HEAD_DIM:]
        m_s[unit] = jnp.broadcast_to(top, m_s.shape[1:])


def save_stats(stat_ref, m_s, l_s, heads):
    rows = stat_ref.shape[1]
    lane = lax.broadcasted_iota(jnp.int32, (rows, 128), 1)
    stat = jnp.zeros((rows, 128), F32)
    for unit, _, _ in units(heads):
        stat = jnp.where(lane == unit, l_s[unit], stat)
        stat = jnp.where(lane == 64 + unit, m_s[unit], stat)
    stat_ref[0] = stat


def load_stats(stat_ref, m_s, l_s, heads):
    rows = stat_ref.shape[1]
    for unit, _, _ in units(heads):
        l_s[unit] = jnp.broadcast_to(stat_ref[0, :, unit : unit + 1], (rows, 128))
        m_s[unit] = jnp.broadcast_to(stat_ref[0, :, 64 + unit : 65 + unit], (rows, 128))


def finish(out_refs, acc_s, l_s, heads):
    for unit, part, cols in units(heads):
        out_refs[part][0, :, cols] = (acc_s[unit] / l_s[unit]).astype(BF)


def local_copies(lay, index, core, local, bufs, sems):
    found = []
    for kv, buf in enumerate(bufs):
        own = local[2 * kv].at[index, :, :, columns(core, buf.shape[-1])]
        for side, source in enumerate((own, local[2 * kv + 1].at[index])):
            owner = core if side == 0 else 1 - core
            target = buf.at[pl.ds(index * lay.tiles + owner * lay.half, lay.half)]
            found.append(pltpu.make_async_copy(source, target, sems.at[index, 2 * kv + side]))
    return found


class Received:
    def __init__(self, lay, refs):
        self.lay = lay
        self.parts = [(0, lay.first, refs[:2])]
        if len(refs) > 2:
            self.parts.append((lay.first, lay.second, refs[2:4]))

    def early_copies(self, bufs, sems):
        _, size, refs = self.parts[0]
        found = []
        for kv, buf in enumerate(bufs):
            for way in (0, 1):
                source = refs[way].at[pl.ds(kv * size, self.lay.early)]
                target = buf.at[pl.ds(self.lay.own + way * self.lay.early, self.lay.early)]
                found.append(pltpu.make_async_copy(source, target, sems.at[len(found)]))
        return found

    def start(self, item, length, targets, sems):
        place = item % length
        for way in (0, 1):
            for begin, size, refs in self.parts:
                inside = jnp.logical_and(place >= begin, place < begin + size)

                @pl.when(jnp.logical_and(item // length == way, inside))
                def _(way=way, begin=begin, size=size, refs=refs):
                    for kv, target in enumerate(targets):
                        source = refs[way].at[place - begin + kv * size]
                        pltpu.make_async_copy(source, target, sems.at[kv]).start()

    def wait(self, targets, sems):
        for kv, target in enumerate(targets):
            pltpu.make_async_copy(self.parts[0][2][0].at[0], target, sems.at[kv]).wait()


def exact_frame(lay, heads, frame, core, table_ref, q_refs, local, received, acc_s, m_s, l_s, tk, tv, sems):
    m_s[...] = jnp.full(m_s.shape, -jnp.inf, F32)
    l_s[...] = jnp.zeros(l_s.shape, F32)
    acc_s[...] = jnp.zeros(acc_s.shape, F32)

    def add_tile():
        for unit, part, cols in units(heads):
            scores = lax.dot_general(
                q_refs[part][0, :, cols], tk[:, cols], NT, preferred_element_type=F32
            )
            before = m_s[unit]
            top = jnp.maximum(before, jnp.max(scores, axis=1, keepdims=True))
            fade = jnp.exp2((before - top) * SCALE)
            mixed = mix(jnp.exp2((scores - top) * SCALE), tv[:, cols])
            acc_s[unit] = acc_s[unit] * fade + mixed[:, :HEAD_DIM]
            l_s[unit] = l_s[unit] * fade + mixed[:, HEAD_DIM:]
            m_s[unit] = top

    def near_tile(name):
        source, tile = name // lay.tiles, name % lay.tiles
        mine = tile // lay.half == core
        tile = tile % lay.half
        cols = columns(core, tk.shape[-1])
        for side in (0, 1):

            @pl.when(mine if side == 0 else jnp.logical_not(mine))
            def _(side=side):
                at = (source, tile, slice(None), cols) if side == 0 else (source, tile)
                found = [
                    pltpu.make_async_copy(local[2 * kv + side].at[at], buf, sems.at[kv])
                    for kv, buf in enumerate((tk, tv))
                ]
                for copy in found:
                    copy.start()
                for copy in found:
                    copy.wait()

    def far_tile(item, length):
        received.start(item, length, (tk, tv), sems)
        received.wait((tk, tv), sems)

    def own_step(i, _):
        near_tile(frame * lay.tiles + i)
        add_tile()
        return 0

    def near_step(i, _):
        name = table_ref[lay.near + frame * STRIDE + 1 + i]

        @pl.when(name < lay.own)
        def _():
            near_tile(name)

        @pl.when(name >= lay.own)
        def _():
            far_tile(name - lay.own, lay.early)

        add_tile()
        return 0

    def far_step(i, _):
        far_tile(table_ref[lay.far + frame * STRIDE + 1 + i], lay.places)
        add_tile()
        return 0

    lax.fori_loop(0, lay.tiles, own_step, 0)
    lax.fori_loop(0, table_ref[lay.near + frame * STRIDE], near_step, 0)
    if len(received.parts) > 1:
        lax.fori_loop(0, table_ref[lay.far + frame * STRIDE], far_step, 0)


def near_kernel(lay, heads, whole, place_ref, table_ref, q_own, q_other, *refs):
    core = place_ref[1]
    q_refs = (q_own, q_other)
    local, refs = refs[:4], refs[4:]
    if whole:
        received, out_refs, refs = Received(lay, refs[:2]), refs[2:4], refs[4:]
        acc_s, kbuf, vbuf, m_s, l_s, sems, tk, tv, far_sems = refs
    else:
        acc_out, stat_ref, kbuf, vbuf, m_s, l_s, sems = refs
        acc_s = acc_out.at[0]
    step = pl.program_id(0)
    frame = step + 1 if whole else step * (lay.here - 1)
    begin = 1 if whole else 0

    def first():
        return local_copies(lay, begin, core, local, (kbuf, vbuf), sems)

    def others():
        found = []
        for index in range(lay.here):
            if index != begin:
                found += local_copies(lay, index, core, local, (kbuf, vbuf), sems)
        return found + (received.early_copies((kbuf, vbuf), far_sems) if whole else [])

    @pl.when(step == 0)
    def _():
        for copy in first():
            copy.start()
        for copy in first():
            copy.wait()
        for copy in others():
            copy.start()

    attend_own(lay, q_refs, kbuf, vbuf, frame, m_s, l_s, acc_s, heads)

    @pl.when(step == 0)
    def _():
        for copy in others():
            copy.wait()

    attend_list(q_refs, kbuf, vbuf, table_ref, lay.near + frame * STRIDE, m_s, l_s, acc_s, heads)
    if whole:

        @pl.when(jnp.max(l_s[...]) > LARGE)
        def _():
            exact_frame(lay, heads, frame, core, table_ref, q_refs, local, received, acc_s, m_s, l_s, tk, tv, far_sems)

        finish(out_refs, acc_s, l_s, heads)
    else:
        save_stats(stat_ref, m_s, l_s, heads)


def cost(scores):
    return pl.CostEstimate(flops=scores * 4 * HEAD_DIM, bytes_accessed=scores // 8, transcendentals=scores)


def token_blocks(rows, width, frame_of):
    return (
        pl.BlockSpec((1, rows, width), lambda s, place, _: (frame_of(s), 0, place[1])),
        pl.BlockSpec((1, rows, width), lambda s, *_: (frame_of(s), 0, 0)),
    )


def near_call(lay, heads, whole, place, table, queries, local, early=()):
    here, rows, width = queries[1].shape
    steps = here - 2 if whole else 2
    own, other = token_blocks(rows, width, (lambda s: s + 1) if whole else (lambda s: s * (here - 1)))
    count = lay.own + (2 * lay.early if whole else 0)
    bufs = [pltpu.VMEM((count, TILE, width), BF)] * 2
    sums = [pltpu.VMEM((2 * heads, rows, 128), F32)] * 2
    sems = [pltpu.SemaphoreType.DMA((here, 4))]
    if whole:
        out_specs = [own, pl.BlockSpec((1, rows, width), lambda s, *_: (s, 0, 0))]
        out_shape = [pltpu.HBM(queries[0].shape, BF), jax.ShapeDtypeStruct((steps, rows, width), BF)]
        scratch = [sums[0], *bufs, *sums, *sems]
        scratch += [pltpu.VMEM((TILE, width), BF)] * 2 + [pltpu.SemaphoreType.DMA((4,))]
    else:
        out_specs = [
            pl.BlockSpec((1, 2 * heads, rows, 128), lambda s, *_: (s, 0, 0, 0)),
            pl.BlockSpec((1, rows, 128), lambda s, *_: (s, 0, 0)),
        ]
        out_shape = [pltpu.HBM((2, 2 * heads, rows, 128), F32), pltpu.HBM((2, rows, 128), F32)]
        scratch = [*bufs, *sums, *sems]
    return pl.pallas_call(
        functools.partial(near_kernel, lay, heads, whole),
        grid_spec=pltpu.PrefetchScalarGridSpec(
            num_scalar_prefetch=2,
            grid=(steps,),
            in_specs=[own, other] + [ANY] * (4 + len(early)),
            out_specs=out_specs,
            scratch_shapes=scratch,
        ),
        out_shape=out_shape,
        compiler_params=pltpu.CompilerParams(vmem_limit_bytes=VMEM_LIMIT),
        cost_estimate=cost(steps * rows * heads * 32 * TILE),
        name="attend_middle" if whole else "attend_edges",
    )(place, table, *queries, *in_hbm((*local, *early)))


def far_kernel(lay, heads, place_ref, table_ref, q_own, q_other, acc_ref, stat_ref, *refs):
    core = place_ref[1]
    q_refs = (q_own, q_other)
    local, received, out_refs = refs[:4], Received(lay, refs[4:8]), refs[9:11]
    kbuf, vbuf, acc_s, m_s, l_s, tk, tv, sems, exact_sems = refs[11:]
    step = pl.program_id(0)
    frame = step * (lay.here - 1)
    room = kbuf.shape[1]

    def bufs(at, i):
        return kbuf.at[at, i], vbuf.at[at, i]

    def start(at):
        base = lay.far + at * (lay.here - 1) * STRIDE

        def one(i, _):
            received.start(table_ref[base + 1 + i], lay.places, bufs(at, i), sems.at[at * room + i])
            return 0

        lax.fori_loop(0, table_ref[base], one, 0)

    @pl.when(step == 0)
    def _():
        start(0)
        start(1)

    load_stats(stat_ref, m_s, l_s, heads)
    acc_s[...] = acc_ref[0]
    base = lay.far + frame * STRIDE

    def wait(i, _):
        received.wait(bufs(step, i), sems.at[step * room + i])
        return 0

    lax.fori_loop(0, table_ref[base], wait, 0)
    attend_list(q_refs, kbuf.at[step], vbuf.at[step], table_ref, base, m_s, l_s, acc_s, heads, packed=True)

    @pl.when(jnp.max(l_s[...]) > LARGE)
    def _():
        exact_frame(lay, heads, frame, core, table_ref, q_refs, local, received, acc_s, m_s, l_s, tk, tv, exact_sems)

    finish(out_refs, acc_s, l_s, heads)


def far_call(lay, heads, place, table, queries, acc, stats, local, early, late, out):
    here, rows, width = queries[1].shape
    own, other = token_blocks(rows, width, lambda s: s * (here - 1))
    anys = [*local, *early, *late]
    room = sum(lay.lengths[column] for way in (0, 1) for frame, column, _ in lay.remote(way) if frame == 0)
    sums = pltpu.VMEM((2 * heads, rows, 128), F32)
    return pl.pallas_call(
        functools.partial(far_kernel, lay, heads),
        grid_spec=pltpu.PrefetchScalarGridSpec(
            num_scalar_prefetch=2,
            grid=(2,),
            in_specs=[
                own,
                other,
                pl.BlockSpec((1, 2 * heads, rows, 128), lambda s, *_: (s, 0, 0, 0)),
                pl.BlockSpec((1, rows, 128), lambda s, *_: (s, 0, 0)),
            ]
            + [ANY] * (len(anys) + 1),
            out_specs=[own, pl.BlockSpec((1, rows, width), lambda s, *_: (s, 0, 0))],
            scratch_shapes=[
                pltpu.VMEM((2, room, TILE, width), BF),
                pltpu.VMEM((2, room, TILE, width), BF),
                sums,
                sums,
                sums,
                pltpu.VMEM((TILE, width), BF),
                pltpu.VMEM((TILE, width), BF),
                pltpu.SemaphoreType.DMA((2 * room, 2)),
                pltpu.SemaphoreType.DMA((2,)),
            ],
        ),
        out_shape=[jax.ShapeDtypeStruct(out.shape, BF), jax.ShapeDtypeStruct((2, rows, width), BF)],
        input_output_aliases={6 + len(anys): 0},
        compiler_params=pltpu.CompilerParams(vmem_limit_bytes=VMEM_LIMIT),
        cost_estimate=cost(2 * rows * heads * 14 * TILE),
        name="attend_late",
    )(place, table, *queries, acc, stats, *in_hbm(anys), out)


def place_kernel(place_ref, block_ref, _, out_ref):
    out_ref[...] = block_ref[...]


def place_call(place, blocks, out, frame_of):
    steps, rows, width = blocks.shape
    return pl.pallas_call(
        place_kernel,
        grid_spec=pltpu.PrefetchScalarGridSpec(
            num_scalar_prefetch=1,
            grid=(steps,),
            in_specs=[pl.BlockSpec((1, rows, width), lambda s, place: (s, 0, 0)), ANY],
            out_specs=pl.BlockSpec((1, rows, width), lambda s, place: (frame_of(s), 0, 1 - place[1])),
        ),
        out_shape=jax.ShapeDtypeStruct(out.shape, BF),
        input_output_aliases={2: 0},
        compiler_params=pltpu.CompilerParams(vmem_limit_bytes=VMEM_LIMIT),
        name="place_columns",
    )(place, blocks, out)


def in_hbm(arrays):
    return [pltpu.with_memory_space_constraint(a, pltpu.HBM) for a in arrays]


def paired(block, way):
    pairs = range(1 - way, lax.axis_size("frame") - 1, 2)
    return lax.ppermute(block, "frame", [p for i in pairs for p in ((i, i + 1), (i + 1, i))])


def swapped(block):
    return lax.ppermute(block, "seq", [(0, 1), (1, 0)])


def per_device(queries, key_rows, value_rows, list_one, list_two, list_four, tile_counts):
    here, rows, width = queries.shape
    heads = -(-width // HEAD_DIM // 2)
    part = heads * HEAD_DIM
    frames = list_one.shape[0]
    lists = (list_one, list_two, list_four)
    lay = Layout(here, 2 * rows // TILE, frames, tuple(a.shape[2] for a in lists))
    core = lax.axis_index("seq")
    place = jnp.stack([lax.axis_index("frame") * here, core]).astype(jnp.int32)
    if width < 2 * part:
        spare = ((0, 0), (0, 0), (0, 2 * part - width))
        queries, key_rows, value_rows = (jnp.pad(a, spare) for a in (queries, key_rows, value_rows))

    def exchanged(a):
        return swapped(lax.dynamic_slice_in_dim(a, (1 - core) * part, part, axis=2))

    def tiled(a):
        return a.reshape(here, lay.half, TILE, a.shape[2])

    k_other = tiled(exchanged(key_rows))
    v_other = tiled(exchanged(value_rows))
    queries = (queries, exchanged(queries))
    by_frame = [jnp.transpose(a, (1, 2, 0)) for a in lists] + [jnp.transpose(tile_counts, (2, 1, 0))]
    table = make_table(lay, place, by_frame)
    local = (tiled(key_rows), k_other, tiled(value_rows), v_other)

    def both_ways(pair):
        return paired(pair[0], 0), paired(pair[1], 1)

    early = pack_call(lay, 0, lay.first, place, table, local)
    early, table = lax.optimization_barrier((early, table))
    early = both_ways(early)
    late = both_ways(pack_call(lay, lay.first, lay.second, place, table, local))
    acc, stats = near_call(lay, heads, False, place, table, queries, local)
    early, stats = lax.optimization_barrier((early, stats))
    out, sent = near_call(lay, heads, True, place, table, queries, local, early)
    out = place_call(place, swapped(sent), out, lambda s: s + 1)
    late, out = lax.optimization_barrier((late, out))
    out, sent = far_call(lay, heads, place, table, queries, acc, stats, local, early, late, out)
    out = place_call(place, swapped(sent), out, lambda s: s * (here - 1))
    return out[:, :, :width]


def solution(mesh):
    placed = (
        P(("clips", "frame"), "seq", "head"),
        P(("clips", "frame"), "seq", "head"),
        P(("clips", "frame"), "seq", "head"),
        P("clips", None, None),
        P("clips", None, None),
        P("clips", None, None),
        P("clips", None, None),
    )
    return jax.shard_map(
        per_device,
        mesh=mesh,
        in_specs=placed,
        out_specs=P(("clips", "frame"), "seq", "head"),
        check_vma=False,
    )
```

```python
import functools
import math

import jax
import jax.numpy as jnp
from jax import lax
from jax.experimental import pallas as pl
from jax.experimental.pallas import tpu as pltpu
from jax.sharding import PartitionSpec as P

HEAD_DIM = 128
TILE = 128
DISTANCES = (1, 2, 4)
STRIDE = 24
SCALE = math.log2(math.e) / math.sqrt(HEAD_DIM)
LARGE = 2.0**100
NT = (((1,), (1,)), ((), ()))
BF = jnp.bfloat16
F32 = jnp.float32
ANY = pl.BlockSpec(memory_space=pl.ANY)
SMEM = pl.BlockSpec(memory_space=pltpu.SMEM)
VMEM_LIMIT = 62 * 2**20
PACK_LIMIT = 16 * 2**20


class Layout:
    def __init__(self, frames_here, frame_tiles, frames, lengths):
        self.here = frames_here
        self.tiles = frame_tiles
        self.half = frame_tiles // 2
        self.own = frames_here * frame_tiles
        self.frames = frames
        self.lengths = lengths
        self.early = self.late = 0
        for frame, column, _ in self.remote(0):
            if self.edge(frame):
                self.late += lengths[column]
            else:
                self.early += lengths[column]
        self.places = self.early + self.late
        self.first = self.early
        self.second = self.late
        self.near = 2 * self.places
        self.far = self.near + frames_here * STRIDE
        self.size = self.far + frames_here * STRIDE

    def edge(self, frame):
        return frame in (0, self.here - 1)

    def remote(self, direction):
        found = []
        for away in (*range(1, self.here - 1), self.here - 1, 0):
            for column in reversed(range(3)):
                distance = DISTANCES[column]
                if away < distance:
                    frame = away if direction == 0 else self.here - 1 - away
                    source = frame - distance if direction == 0 else frame + distance
                    found.append((frame, column, source % self.here))
        return found


def table_kernel(lay, place_ref, one_ref, two_ref, four_ref, count_ref, table_ref, seen_ref):
    lists = (one_ref, two_ref, four_ref)
    first = place_ref[0]
    odd = first // lay.here % 2

    def distinct(target, direction, on_slot, on_new):
        for i in range(lay.own):
            seen_ref[i] = -1
        used = jnp.int32(0)
        for frame, column, source in lay.remote(direction):
            live = count_ref[column, direction, target + frame]
            for slot in range(lay.lengths[column]):
                name = lists[column][direction, slot, target + frame] + source * lay.tiles
                alive = slot < live
                known = seen_ref[name]
                fresh = jnp.logical_and(alive, known < 0)
                place = jnp.where(fresh, used, known)
                seen_ref[name] = place
                on_new(used, name)
                on_slot(frame, place, alive)
                used = used + fresh.astype(jnp.int32)
        return used

    filled = {}

    def append(base, frame, item, alive):
        at = base + frame * STRIDE
        count = filled.get(at, jnp.int32(0))
        table_ref[at + 1 + count] = item
        filled[at] = count + alive.astype(jnp.int32)

    for direction in (0, 1):
        target = first + (lay.here if direction == 0 else -lay.here)
        target = jnp.clip(target, 0, lay.frames - lay.here)
        begin = (odd + direction + 1) % 2 * lay.places
        for place in range(lay.places):
            table_ref[begin + place] = 0

        def note(used, name, begin=begin):
            table_ref[begin + jnp.minimum(used, lay.places - 1)] = name

        distinct(target, direction, lambda *_: None, note)

    for direction in (0, 1):
        way = (odd + direction) % 2

        def on_slot(frame, place, alive, way=way):
            if lay.edge(frame):
                append(lay.far, frame, way * lay.places + place, alive)
            else:
                append(lay.near, frame, lay.own + way * lay.early + place, alive)

        distinct(first, direction, on_slot, lambda *_: None)
        for frame in range(lay.here):
            for column, distance in enumerate(DISTANCES):
                source = frame + (2 * direction - 1) * distance
                if 0 <= source < lay.here:
                    live = count_ref[column, direction, first + frame]
                    for slot in range(lay.lengths[column]):
                        name = lists[column][direction, slot, first + frame]
                        append(lay.near, frame, source * lay.tiles + name, slot < live)
    for frame in range(lay.here):
        for base in (lay.near, lay.far):
            at = base + frame * STRIDE
            table_ref[at] = filled.get(at, jnp.int32(0))


def make_table(lay, place, lists):
    return pl.pallas_call(
        functools.partial(table_kernel, lay),
        in_specs=[SMEM] * 5,
        out_specs=SMEM,
        out_shape=jax.ShapeDtypeStruct((lay.size,), jnp.int32),
        scratch_shapes=[pltpu.SMEM((lay.own,), jnp.int32)],
        compiler_params=pltpu.CompilerParams(vmem_limit_bytes=VMEM_LIMIT),
        name="tile_tables",
    )(place, *lists)


def columns(core, width):
    return pl.ds(pl.multiple_of(core * width, HEAD_DIM), width)


def pack_kernel(lay, begin, length, place_ref, table_ref, k_own, k_other, v_own, v_other, *refs):
    outs, sems = refs[:2], refs[2]
    core = place_ref[1]
    cols = columns(core, outs[0].shape[-1])
    waits = []
    for way, out in enumerate(outs):
        for item in range(length):
            name = table_ref[way * lay.places + begin + item]
            frame = name // lay.tiles
            tile = name % lay.tiles
            mine = tile // lay.half == core
            tile = tile % lay.half
            for kv, (own, other) in enumerate(((k_own, k_other), (v_own, v_other))):
                target = out.at[kv * length + item]
                sem = sems.at[len(waits)]
                here = pltpu.make_async_copy(own.at[frame, tile, :, cols], target, sem)
                there = pltpu.make_async_copy(other.at[frame, tile], target, sem)
                pl.when(mine)(here.start)
                pl.when(jnp.logical_not(mine))(there.start)
                waits.append(here)
    for copy in waits:
        copy.wait()


def pack_call(lay, begin, length, place, table, local):
    shape = jax.ShapeDtypeStruct((2 * length, TILE, local[1].shape[-1]), BF)
    return pl.pallas_call(
        functools.partial(pack_kernel, lay, begin, length),
        in_specs=[SMEM] * 2 + [ANY] * 4,
        out_specs=[pl.BlockSpec(memory_space=pltpu.VMEM)] * 2,
        out_shape=[shape] * 2,
        scratch_shapes=[pltpu.SemaphoreType.DMA((4 * length,))],
        compiler_params=pltpu.CompilerParams(vmem_limit_bytes=PACK_LIMIT),
        name="pack_tiles",
    )(place, table, *in_hbm(local))


def rows_of(buf, index, cols):
    tiles = buf[index, :, cols]
    return tiles.reshape(tiles.size // HEAD_DIM, HEAD_DIM)


def units(heads):
    for part in (0, 1):
        for head in range(heads):
            yield part * heads + head, part, slice(head * HEAD_DIM, (head + 1) * HEAD_DIM)


def mix(weights, values):
    return jnp.dot(
        weights.astype(BF),
        jnp.concatenate([values, jnp.ones_like(values)], axis=1),
        preferred_element_type=F32,
    )


def attend_tiles(q_refs, kbuf, vbuf, ids, m_s, l_s, acc_s, heads):
    for unit, part, cols in units(heads):
        keys = jnp.concatenate([rows_of(kbuf, i, cols) for i in ids], axis=0)
        values = jnp.concatenate([rows_of(vbuf, i, cols) for i in ids], axis=0)
        scores = lax.dot_general(q_refs[part][0, :, cols], keys, NT, preferred_element_type=F32)
        shift = jnp.concatenate([m_s[unit]] * len(ids), axis=1)
        mixed = mix(jnp.exp2((scores - shift) * SCALE), values)
        acc_s[unit] += mixed[:, :HEAD_DIM]
        l_s[unit] += mixed[:, HEAD_DIM:]


def attend_list(q_refs, kbuf, vbuf, table_ref, base, m_s, l_s, acc_s, heads, packed=False):
    count = table_ref[base]

    def add(start, n):
        ids = [start + j if packed else table_ref[base + 1 + start + j] for j in range(n)]
        attend_tiles(q_refs, kbuf, vbuf, ids, m_s, l_s, acc_s, heads)

    def four(i, _):
        add(4 * i, 4)
        return 0

    lax.fori_loop(0, count // 4, four, 0)

    @pl.when(count % 4 >= 2)
    def _():
        add(count // 4 * 4, 2)

    @pl.when(count % 2 == 1)
    def _():
        add(count - 1, 1)


def attend_own(lay, q_refs, kbuf, vbuf, frame, m_s, l_s, acc_s, heads):
    own = pl.ds(frame * lay.tiles, lay.tiles)
    for unit, part, cols in units(heads):
        scores = lax.dot_general(
            q_refs[part][0, :, cols], rows_of(kbuf, own, cols), NT, preferred_element_type=F32
        )
        top = jnp.max(scores[:, :TILE], axis=1, keepdims=True)
        mixed = mix(jnp.exp2((scores - top) * SCALE), rows_of(vbuf, own, cols))
        acc_s[unit] = mixed[:, :HEAD_DIM]
        l_s[unit] = mixed[:, HEAD_DIM:]
        m_s[unit] = jnp.broadcast_to(top, m_s.shape[1:])


def save_stats(stat_ref, m_s, l_s, heads):
    rows = stat_ref.shape[1]
    lane = lax.broadcasted_iota(jnp.int32, (rows, 128), 1)
    stat = jnp.zeros((rows, 128), F32)
    for unit, _, _ in units(heads):
        stat = jnp.where(lane == unit, l_s[unit], stat)
        stat = jnp.where(lane == 64 + unit, m_s[unit], stat)
    stat_ref[0] = stat


def load_stats(stat_ref, m_s, l_s, heads):
    rows = stat_ref.shape[1]
    for unit, _, _ in units(heads):
        l_s[unit] = jnp.broadcast_to(stat_ref[0, :, unit : unit + 1], (rows, 128))
        m_s[unit] = jnp.broadcast_to(stat_ref[0, :, 64 + unit : 65 + unit], (rows, 128))


def finish(out_refs, acc_s, l_s, heads):
    for unit, part, cols in units(heads):
        out_refs[part][0, :, cols] = (acc_s[unit] / l_s[unit]).astype(BF)


def local_copies(lay, index, core, local, bufs, sems):
    found = []
    for kv, buf in enumerate(bufs):
        own = local[2 * kv].at[index, :, :, columns(core, buf.shape[-1])]
        for side, source in enumerate((own, local[2 * kv + 1].at[index])):
            owner = core if side == 0 else 1 - core
            target = buf.at[pl.ds(index * lay.tiles + owner * lay.half, lay.half)]
            found.append(pltpu.make_async_copy(source, target, sems.at[index, 2 * kv + side]))
    return found


class Received:
    def __init__(self, lay, refs):
        self.lay = lay
        self.parts = [(0, lay.first, refs[:2])]
        if len(refs) > 2:
            self.parts.append((lay.first, lay.second, refs[2:4]))

    def early_copies(self, bufs, sems):
        _, size, refs = self.parts[0]
        found = []
        for kv, buf in enumerate(bufs):
            for way in (0, 1):
                source = refs[way].at[pl.ds(kv * size, self.lay.early)]
                target = buf.at[pl.ds(self.lay.own + way * self.lay.early, self.lay.early)]
                found.append(pltpu.make_async_copy(source, target, sems.at[len(found)]))
        return found

    def start(self, item, length, targets, sems):
        place = item % length
        for way in (0, 1):
            for begin, size, refs in self.parts:
                inside = jnp.logical_and(place >= begin, place < begin + size)

                @pl.when(jnp.logical_and(item // length == way, inside))
                def _(way=way, begin=begin, size=size, refs=refs):
                    for kv, target in enumerate(targets):
                        source = refs[way].at[place - begin + kv * size]
                        pltpu.make_async_copy(source, target, sems.at[kv]).start()

    def wait(self, targets, sems):
        for kv, target in enumerate(targets):
            pltpu.make_async_copy(self.parts[0][2][0].at[0], target, sems.at[kv]).wait()


def exact_frame(lay, heads, frame, core, table_ref, q_refs, local, received, acc_s, m_s, l_s, tk, tv, sems):
    m_s[...] = jnp.full(m_s.shape, -jnp.inf, F32)
    l_s[...] = jnp.zeros(l_s.shape, F32)
    acc_s[...] = jnp.zeros(acc_s.shape, F32)

    def add_tile():
        for unit, part, cols in units(heads):
            scores = lax.dot_general(
                q_refs[part][0, :, cols], tk[:, cols], NT, preferred_element_type=F32
            )
            before = m_s[unit]
            top = jnp.maximum(before, jnp.max(scores, axis=1, keepdims=True))
            fade = jnp.exp2((before - top) * SCALE)
            mixed = mix(jnp.exp2((scores - top) * SCALE), tv[:, cols])
            acc_s[unit] = acc_s[unit] * fade + mixed[:, :HEAD_DIM]
            l_s[unit] = l_s[unit] * fade + mixed[:, HEAD_DIM:]
            m_s[unit] = top

    def near_tile(name):
        source, tile = name // lay.tiles, name % lay.tiles
        mine = tile // lay.half == core
        tile = tile % lay.half
        cols = columns(core, tk.shape[-1])
        for side in (0, 1):

            @pl.when(mine if side == 0 else jnp.logical_not(mine))
            def _(side=side):
                at = (source, tile, slice(None), cols) if side == 0 else (source, tile)
                found = [
                    pltpu.make_async_copy(local[2 * kv + side].at[at], buf, sems.at[kv])
                    for kv, buf in enumerate((tk, tv))
                ]
                for copy in found:
                    copy.start()
                for copy in found:
                    copy.wait()

    def far_tile(item, length):
        received.start(item, length, (tk, tv), sems)
        received.wait((tk, tv), sems)

    def own_step(i, _):
        near_tile(frame * lay.tiles + i)
        add_tile()
        return 0

    def near_step(i, _):
        name = table_ref[lay.near + frame * STRIDE + 1 + i]

        @pl.when(name < lay.own)
        def _():
            near_tile(name)

        @pl.when(name >= lay.own)
        def _():
            far_tile(name - lay.own, lay.early)

        add_tile()
        return 0

    def far_step(i, _):
        far_tile(table_ref[lay.far + frame * STRIDE + 1 + i], lay.places)
        add_tile()
        return 0

    lax.fori_loop(0, lay.tiles, own_step, 0)
    lax.fori_loop(0, table_ref[lay.near + frame * STRIDE], near_step, 0)
    if len(received.parts) > 1:
        lax.fori_loop(0, table_ref[lay.far + frame * STRIDE], far_step, 0)


def near_kernel(lay, heads, whole, place_ref, table_ref, q_own, q_other, *refs):
    core = place_ref[1]
    q_refs = (q_own, q_other)
    local, refs = refs[:4], refs[4:]
    if whole:
        received, out_refs, refs = Received(lay, refs[:2]), refs[2:4], refs[4:]
        acc_s, kbuf, vbuf, m_s, l_s, sems, tk, tv, far_sems = refs
    else:
        acc_out, stat_ref, kbuf, vbuf, m_s, l_s, sems = refs
        acc_s = acc_out.at[0]
    step = pl.program_id(0)
    frame = step + 1 if whole else step * (lay.here - 1)
    begin = 1 if whole else 0

    def first():
        return local_copies(lay, begin, core, local, (kbuf, vbuf), sems)

    def others():
        found = []
        for index in range(lay.here):
            if index != begin:
                found += local_copies(lay, index, core, local, (kbuf, vbuf), sems)
        return found + (received.early_copies((kbuf, vbuf), far_sems) if whole else [])

    @pl.when(step == 0)
    def _():
        for copy in first():
            copy.start()
        for copy in first():
            copy.wait()
        for copy in others():
            copy.start()

    attend_own(lay, q_refs, kbuf, vbuf, frame, m_s, l_s, acc_s, heads)

    @pl.when(step == 0)
    def _():
        for copy in others():
            copy.wait()

    attend_list(q_refs, kbuf, vbuf, table_ref, lay.near + frame * STRIDE, m_s, l_s, acc_s, heads)
    if whole:

        too_large = jnp.max(l_s[...]) > LARGE
        finish(out_refs, acc_s, l_s, heads)

        @pl.when(too_large)
        def _():
            exact_frame(lay, heads, frame, core, table_ref, q_refs, local, received, acc_s, m_s, l_s, tk, tv, far_sems)
            finish(out_refs, acc_s, l_s, heads)

    else:
        save_stats(stat_ref, m_s, l_s, heads)


def cost(scores):
    return pl.CostEstimate(flops=scores * 4 * HEAD_DIM, bytes_accessed=scores // 8, transcendentals=scores)


def token_blocks(rows, width, frame_of):
    return (
        pl.BlockSpec((1, rows, width), lambda s, place, _: (frame_of(s), 0, place[1])),
        pl.BlockSpec((1, rows, width), lambda s, *_: (frame_of(s), 0, 0)),
    )


def near_call(lay, heads, whole, place, table, queries, local, early=()):
    here, rows, width = queries[1].shape
    steps = here - 2 if whole else 2
    own, other = token_blocks(rows, width, (lambda s: s + 1) if whole else (lambda s: s * (here - 1)))
    count = lay.own + (2 * lay.early if whole else 0)
    bufs = [pltpu.VMEM((count, TILE, width), BF)] * 2
    sums = [pltpu.VMEM((2 * heads, rows, 128), F32)] * 2
    sems = [pltpu.SemaphoreType.DMA((here, 4))]
    if whole:
        out_specs = [own, pl.BlockSpec((1, rows, width), lambda s, *_: (s, 0, 0))]
        out_shape = [pltpu.HBM(queries[0].shape, BF), jax.ShapeDtypeStruct((steps, rows, width), BF)]
        scratch = [sums[0], *bufs, *sums, *sems]
        scratch += [pltpu.VMEM((TILE, width), BF)] * 2 + [pltpu.SemaphoreType.DMA((4,))]
    else:
        out_specs = [
            pl.BlockSpec((1, 2 * heads, rows, 128), lambda s, *_: (s, 0, 0, 0)),
            pl.BlockSpec((1, rows, 128), lambda s, *_: (s, 0, 0)),
        ]
        out_shape = [pltpu.HBM((2, 2 * heads, rows, 128), F32), pltpu.HBM((2, rows, 128), F32)]
        scratch = [*bufs, *sums, *sems]
    return pl.pallas_call(
        functools.partial(near_kernel, lay, heads, whole),
        grid_spec=pltpu.PrefetchScalarGridSpec(
            num_scalar_prefetch=2,
            grid=(steps,),
            in_specs=[own, other] + [ANY] * (4 + len(early)),
            out_specs=out_specs,
            scratch_shapes=scratch,
        ),
        out_shape=out_shape,
        compiler_params=pltpu.CompilerParams(vmem_limit_bytes=VMEM_LIMIT),
        cost_estimate=cost(steps * rows * heads * (4 if whole else 32) * TILE),
        name="attend_middle" if whole else "attend_edges",
    )(place, table, *queries, *in_hbm((*local, *early)))


def far_kernel(lay, heads, place_ref, table_ref, q_own, q_other, acc_ref, stat_ref, *refs):
    core = place_ref[1]
    q_refs = (q_own, q_other)
    local, received, out_refs = refs[:4], Received(lay, refs[4:8]), refs[9:11]
    kbuf, vbuf, acc_s, m_s, l_s, tk, tv, sems, exact_sems = refs[11:]
    step = pl.program_id(0)
    frame = step * (lay.here - 1)
    room = kbuf.shape[1]

    def bufs(at, i):
        return kbuf.at[at, i], vbuf.at[at, i]

    def start(at):
        base = lay.far + at * (lay.here - 1) * STRIDE

        def one(i, _):
            received.start(table_ref[base + 1 + i], lay.places, bufs(at, i), sems.at[at * room + i])
            return 0

        lax.fori_loop(0, table_ref[base], one, 0)

    @pl.when(step == 0)
    def _():
        start(0)
        start(1)

    load_stats(stat_ref, m_s, l_s, heads)
    acc_s[...] = acc_ref[0]
    base = lay.far + frame * STRIDE

    def wait(i, _):
        received.wait(bufs(step, i), sems.at[step * room + i])
        return 0

    lax.fori_loop(0, table_ref[base], wait, 0)
    attend_list(q_refs, kbuf.at[step], vbuf.at[step], table_ref, base, m_s, l_s, acc_s, heads, packed=True)

    too_large = jnp.max(l_s[...]) > LARGE
    finish(out_refs, acc_s, l_s, heads)

    @pl.when(too_large)
    def _():
        exact_frame(lay, heads, frame, core, table_ref, q_refs, local, received, acc_s, m_s, l_s, tk, tv, exact_sems)
        finish(out_refs, acc_s, l_s, heads)


def far_call(lay, heads, place, table, queries, acc, stats, local, early, late, out):
    here, rows, width = queries[1].shape
    own, other = token_blocks(rows, width, lambda s: s * (here - 1))
    anys = [*local, *early, *late]
    room = sum(lay.lengths[column] for way in (0, 1) for frame, column, _ in lay.remote(way) if frame == 0)
    sums = pltpu.VMEM((2 * heads, rows, 128), F32)
    return pl.pallas_call(
        functools.partial(far_kernel, lay, heads),
        grid_spec=pltpu.PrefetchScalarGridSpec(
            num_scalar_prefetch=2,
            grid=(2,),
            in_specs=[
                own,
                other,
                pl.BlockSpec((1, 2 * heads, rows, 128), lambda s, *_: (s, 0, 0, 0)),
                pl.BlockSpec((1, rows, 128), lambda s, *_: (s, 0, 0)),
            ]
            + [ANY] * (len(anys) + 1),
            out_specs=[own, pl.BlockSpec((1, rows, width), lambda s, *_: (s, 0, 0))],
            scratch_shapes=[
                pltpu.VMEM((2, room, TILE, width), BF),
                pltpu.VMEM((2, room, TILE, width), BF),
                sums,
                sums,
                sums,
                pltpu.VMEM((TILE, width), BF),
                pltpu.VMEM((TILE, width), BF),
                pltpu.SemaphoreType.DMA((2 * room, 2)),
                pltpu.SemaphoreType.DMA((2,)),
            ],
        ),
        out_shape=[jax.ShapeDtypeStruct(out.shape, BF), jax.ShapeDtypeStruct((2, rows, width), BF)],
        input_output_aliases={6 + len(anys): 0},
        compiler_params=pltpu.CompilerParams(vmem_limit_bytes=VMEM_LIMIT),
        cost_estimate=cost(2 * rows * heads * 14 * TILE),
        name="attend_late",
    )(place, table, *queries, acc, stats, *in_hbm(anys), out)


def place_kernel(place_ref, block_ref, _, out_ref):
    out_ref[...] = block_ref[...]


def place_call(place, blocks, out, frame_of):
    steps, rows, width = blocks.shape
    return pl.pallas_call(
        place_kernel,
        grid_spec=pltpu.PrefetchScalarGridSpec(
            num_scalar_prefetch=1,
            grid=(steps,),
            in_specs=[pl.BlockSpec((1, rows, width), lambda s, place: (s, 0, 0)), ANY],
            out_specs=pl.BlockSpec((1, rows, width), lambda s, place: (frame_of(s), 0, 1 - place[1])),
        ),
        out_shape=jax.ShapeDtypeStruct(out.shape, BF),
        input_output_aliases={2: 0},
        compiler_params=pltpu.CompilerParams(vmem_limit_bytes=PACK_LIMIT),
        name="place_columns",
    )(place, blocks, out)


def in_hbm(arrays):
    return [pltpu.with_memory_space_constraint(a, pltpu.HBM) for a in arrays]


def paired(block, way):
    pairs = range(1 - way, lax.axis_size("frame") - 1, 2)
    return lax.ppermute(block, "frame", [p for i in pairs for p in ((i, i + 1), (i + 1, i))])


def swapped(block):
    return lax.ppermute(block, "seq", [(0, 1), (1, 0)])


def per_device(queries, key_rows, value_rows, list_one, list_two, list_four, tile_counts):
    here, rows, width = queries.shape
    heads = -(-width // HEAD_DIM // 2)
    part = heads * HEAD_DIM
    frames = list_one.shape[0]
    lists = (list_one, list_two, list_four)
    lay = Layout(here, 2 * rows // TILE, frames, tuple(a.shape[2] for a in lists))
    core = lax.axis_index("seq")
    place = jnp.stack([lax.axis_index("frame") * here, core]).astype(jnp.int32)
    if width < 2 * part:
        spare = ((0, 0), (0, 0), (0, 2 * part - width))
        queries, key_rows, value_rows = (jnp.pad(a, spare) for a in (queries, key_rows, value_rows))

    def exchanged(a):
        return swapped(lax.dynamic_slice_in_dim(a, (1 - core) * part, part, axis=2))

    def tiled(a):
        return a.reshape(here, lay.half, TILE, a.shape[2])

    k_other = tiled(exchanged(key_rows))
    v_other = tiled(exchanged(value_rows))
    queries = (queries, exchanged(queries))
    by_frame = [jnp.transpose(a, (1, 2, 0)) for a in lists] + [jnp.transpose(tile_counts, (2, 1, 0))]
    table = make_table(lay, place, by_frame)
    local = (tiled(key_rows), k_other, tiled(value_rows), v_other)

    def both_ways(pair):
        return paired(pair[0], 0), paired(pair[1], 1)

    early = pack_call(lay, 0, lay.first, place, table, local)
    early, table = lax.optimization_barrier((early, table))
    early = both_ways(early)
    late = both_ways(pack_call(lay, lay.first, lay.second, place, table, local))
    acc, stats = near_call(lay, heads, False, place, table, queries, local)
    early, stats = lax.optimization_barrier((early, stats))
    out, sent = near_call(lay, heads, True, place, table, queries, local, early)
    out = place_call(place, swapped(sent), out, lambda s: s + 1)
    late, out = lax.optimization_barrier((late, out))
    out, sent = far_call(lay, heads, place, table, queries, acc, stats, local, early, late, out)
    out = place_call(place, swapped(sent), out, lambda s: s * (here - 1))
    return out[:, :, :width]


def solution(mesh):
    placed = (
        P(("clips", "frame"), "seq", "head"),
        P(("clips", "frame"), "seq", "head"),
        P(("clips", "frame"), "seq", "head"),
        P("clips", None, None),
        P("clips", None, None),
        P("clips", None, None),
        P("clips", None, None),
    )
    return jax.shard_map(
        per_device,
        mesh=mesh,
        in_specs=placed,
        out_specs=P(("clips", "frame"), "seq", "head"),
        check_vma=False,
    )
```

```python
import functools
import math

import jax
import jax.numpy as jnp
from jax import lax
from jax.experimental import pallas as pl
from jax.experimental.pallas import tpu as pltpu
from jax.sharding import PartitionSpec as P

HEAD_DIM = 128
TILE = 128
DISTANCES = (1, 2, 4)
STRIDE = 24
SCALE = math.log2(math.e) / math.sqrt(HEAD_DIM)
LARGE = 2.0**100
NT = (((1,), (1,)), ((), ()))
BF = jnp.bfloat16
F32 = jnp.float32
ANY = pl.BlockSpec(memory_space=pl.ANY)
SMEM = pl.BlockSpec(memory_space=pltpu.SMEM)
VMEM_LIMIT = 62 * 2**20
EDGE_LIMIT = 48 * 2**20
PACK_LIMIT = 16 * 2**20


class Layout:
    def __init__(self, frames_here, frame_tiles, frames, lengths):
        self.here = frames_here
        self.tiles = frame_tiles
        self.half = frame_tiles // 2
        self.own = frames_here * frame_tiles
        self.frames = frames
        self.lengths = lengths
        self.early = self.late = 0
        for frame, column, _ in self.remote(0):
            if self.edge(frame):
                self.late += lengths[column]
            else:
                self.early += lengths[column]
        self.places = self.early + self.late
        self.near = 2 * self.places
        self.far = self.near + frames_here * STRIDE
        self.size = self.far + frames_here * STRIDE

    def edge(self, frame):
        return frame in (0, self.here - 1)

    def remote(self, direction):
        found = []
        for away in (*range(1, self.here - 1), self.here - 1, 0):
            for column in reversed(range(3)):
                distance = DISTANCES[column]
                if away < distance:
                    frame = away if direction == 0 else self.here - 1 - away
                    source = frame - distance if direction == 0 else frame + distance
                    found.append((frame, column, source % self.here))
        return found


def table_kernel(lay, place_ref, one_ref, two_ref, four_ref, count_ref, table_ref, need_ref, seen_ref):
    lists = (one_ref, two_ref, four_ref)
    first = place_ref[0]
    odd = first // lay.here % 2

    def distinct(target, direction, on_slot, on_new):
        for i in range(lay.own):
            seen_ref[i] = -1
        used = jnp.int32(0)
        for frame, column, source in lay.remote(direction):
            live = count_ref[column, direction, target + frame]
            for slot in range(lay.lengths[column]):
                name = lists[column][direction, slot, target + frame] + source * lay.tiles
                alive = slot < live
                known = seen_ref[name]
                fresh = jnp.logical_and(alive, known < 0)
                place = jnp.where(fresh, used, known)
                seen_ref[name] = place
                on_new(used, name)
                on_slot(frame, place, alive)
                used = used + fresh.astype(jnp.int32)
        return used

    def block_need(block, most):
        for direction in (0, 1):
            most = jnp.maximum(most, distinct(block * lay.here, direction, lambda *_: None, lambda *_: None))
        return most

    need_ref[0] = lax.fori_loop(0, lay.frames // lay.here, block_need, jnp.int32(0))
    filled = {}

    def append(base, frame, item, alive):
        at = base + frame * STRIDE
        count = filled.get(at, jnp.int32(0))
        table_ref[at + 1 + count] = item
        filled[at] = count + alive.astype(jnp.int32)

    for direction in (0, 1):
        target = first + (lay.here if direction == 0 else -lay.here)
        target = jnp.clip(target, 0, lay.frames - lay.here)
        begin = (odd + direction + 1) % 2 * lay.places
        for place in range(lay.places):
            table_ref[begin + place] = 0

        def note(used, name, begin=begin):
            table_ref[begin + jnp.minimum(used, lay.places - 1)] = name

        distinct(target, direction, lambda *_: None, note)

    for direction in (0, 1):
        way = (odd + direction) % 2

        def on_slot(frame, place, alive, way=way):
            if lay.edge(frame):
                append(lay.far, frame, way * lay.places + place, alive)
            else:
                append(lay.near, frame, lay.own + way * lay.early + place, alive)

        distinct(first, direction, on_slot, lambda *_: None)
        for frame in range(lay.here):
            for column, distance in enumerate(DISTANCES):
                source = frame + (2 * direction - 1) * distance
                if 0 <= source < lay.here:
                    live = count_ref[column, direction, first + frame]
                    for slot in range(lay.lengths[column]):
                        name = lists[column][direction, slot, first + frame]
                        append(lay.near, frame, source * lay.tiles + name, slot < live)
    for frame in range(lay.here):
        for base in (lay.near, lay.far):
            at = base + frame * STRIDE
            table_ref[at] = filled.get(at, jnp.int32(0))


def make_table(lay, place, lists):
    return pl.pallas_call(
        functools.partial(table_kernel, lay),
        in_specs=[SMEM] * 5,
        out_specs=[SMEM] * 2,
        out_shape=[jax.ShapeDtypeStruct((lay.size,), jnp.int32), jax.ShapeDtypeStruct((1,), jnp.int32)],
        scratch_shapes=[pltpu.SMEM((lay.own,), jnp.int32)],
        compiler_params=pltpu.CompilerParams(vmem_limit_bytes=VMEM_LIMIT),
        name="tile_tables",
    )(place, *lists)


def columns(core, width):
    return pl.ds(pl.multiple_of(core * width, HEAD_DIM), width)


def pack_kernel(lay, begin, length, place_ref, table_ref, k_own, k_other, v_own, v_other, *refs):
    outs, sems = refs[:2], refs[2]
    core = place_ref[1]
    cols = columns(core, outs[0].shape[-1])
    waits = []
    for way, out in enumerate(outs):
        for item in range(length):
            name = table_ref[way * lay.places + begin + item]
            frame = name // lay.tiles
            tile = name % lay.tiles
            mine = tile // lay.half == core
            tile = tile % lay.half
            for kv, (own, other) in enumerate(((k_own, k_other), (v_own, v_other))):
                target = out.at[kv * length + item]
                sem = sems.at[len(waits)]
                here = pltpu.make_async_copy(own.at[frame, tile, :, cols], target, sem)
                there = pltpu.make_async_copy(other.at[frame, tile], target, sem)
                pl.when(mine)(here.start)
                pl.when(jnp.logical_not(mine))(there.start)
                waits.append(here)
    for copy in waits:
        copy.wait()


def pack_call(lay, begin, length, place, table, local):
    shape = jax.ShapeDtypeStruct((2 * length, TILE, local[1].shape[-1]), BF)
    return pl.pallas_call(
        functools.partial(pack_kernel, lay, begin, length),
        in_specs=[SMEM] * 2 + [ANY] * 4,
        out_specs=[pl.BlockSpec(memory_space=pltpu.VMEM)] * 2,
        out_shape=[shape] * 2,
        scratch_shapes=[pltpu.SemaphoreType.DMA((4 * length,))],
        compiler_params=pltpu.CompilerParams(vmem_limit_bytes=PACK_LIMIT),
        name="pack_tiles",
    )(place, table, *in_hbm(local))


def rows_of(buf, index, cols):
    tiles = buf[index, :, cols]
    return tiles.reshape(tiles.size // HEAD_DIM, HEAD_DIM)


def units(heads):
    for part in (0, 1):
        for head in range(heads):
            yield part * heads + head, part, slice(head * HEAD_DIM, (head + 1) * HEAD_DIM)


def mix(weights, values):
    return jnp.dot(
        weights.astype(BF),
        jnp.concatenate([values, jnp.ones_like(values)], axis=1),
        preferred_element_type=F32,
    )


def attend_tiles(q_refs, kbuf, vbuf, ids, m_s, l_s, acc_s, heads):
    for unit, part, cols in units(heads):
        keys = jnp.concatenate([rows_of(kbuf, i, cols) for i in ids], axis=0)
        values = jnp.concatenate([rows_of(vbuf, i, cols) for i in ids], axis=0)
        scores = lax.dot_general(q_refs[part][0, :, cols], keys, NT, preferred_element_type=F32)
        shift = jnp.concatenate([m_s[unit]] * len(ids), axis=1)
        mixed = mix(jnp.exp2((scores - shift) * SCALE), values)
        acc_s[unit] += mixed[:, :HEAD_DIM]
        l_s[unit] += mixed[:, HEAD_DIM:]


def attend_list(q_refs, kbuf, vbuf, table_ref, base, m_s, l_s, acc_s, heads, packed=False):
    count = table_ref[base]

    def add(start, n):
        ids = [start + j if packed else table_ref[base + 1 + start + j] for j in range(n)]
        attend_tiles(q_refs, kbuf, vbuf, ids, m_s, l_s, acc_s, heads)

    def four(i, _):
        add(4 * i, 4)
        return 0

    lax.fori_loop(0, count // 4, four, 0)

    @pl.when(count % 4 >= 2)
    def _():
        add(count // 4 * 4, 2)

    @pl.when(count % 2 == 1)
    def _():
        add(count - 1, 1)


def attend_own(lay, q_refs, kbuf, vbuf, frame, m_s, l_s, acc_s, heads):
    own = pl.ds(frame * lay.tiles, lay.tiles)
    for unit, part, cols in units(heads):
        scores = lax.dot_general(
            q_refs[part][0, :, cols], rows_of(kbuf, own, cols), NT, preferred_element_type=F32
        )
        top = jnp.max(scores[:, :TILE], axis=1, keepdims=True)
        mixed = mix(jnp.exp2((scores - top) * SCALE), rows_of(vbuf, own, cols))
        acc_s[unit] = mixed[:, :HEAD_DIM]
        l_s[unit] = mixed[:, HEAD_DIM:]
        m_s[unit] = jnp.broadcast_to(top, m_s.shape[1:])


def save_stats(stat_ref, m_s, l_s, heads):
    rows = stat_ref.shape[1]
    lane = lax.broadcasted_iota(jnp.int32, (rows, 128), 1)
    stat = jnp.zeros((rows, 128), F32)
    for unit, _, _ in units(heads):
        stat = jnp.where(lane == unit, l_s[unit], stat)
        stat = jnp.where(lane == 64 + unit, m_s[unit], stat)
    stat_ref[0] = stat


def load_stats(stat_ref, m_s, l_s, heads):
    rows = stat_ref.shape[1]
    for unit, _, _ in units(heads):
        l_s[unit] = jnp.broadcast_to(stat_ref[0, :, unit : unit + 1], (rows, 128))
        m_s[unit] = jnp.broadcast_to(stat_ref[0, :, 64 + unit : 65 + unit], (rows, 128))


def finish(out_refs, acc_s, l_s, heads):
    for unit, part, cols in units(heads):
        out_refs[part][0, :, cols] = (acc_s[unit] / l_s[unit]).astype(BF)


def local_copies(lay, index, core, local, bufs, sems):
    found = []
    for kv, buf in enumerate(bufs):
        own = local[2 * kv].at[index, :, :, columns(core, buf.shape[-1])]
        for side, source in enumerate((own, local[2 * kv + 1].at[index])):
            owner = core if side == 0 else 1 - core
            target = buf.at[pl.ds(index * lay.tiles + owner * lay.half, lay.half)]
            found.append(pltpu.make_async_copy(source, target, sems.at[index, 2 * kv + side]))
    return found


class Received:
    def __init__(self, lay, refs):
        self.lay = lay
        self.parts = [(0, lay.early, refs[:2])]
        if len(refs) > 2:
            self.parts.append((lay.early, refs[2].shape[0] // 2, refs[2:4]))

    def early_copies(self, bufs, sems):
        _, size, refs = self.parts[0]
        found = []
        for kv, buf in enumerate(bufs):
            for way in (0, 1):
                source = refs[way].at[pl.ds(kv * size, self.lay.early)]
                target = buf.at[pl.ds(self.lay.own + way * self.lay.early, self.lay.early)]
                found.append(pltpu.make_async_copy(source, target, sems.at[len(found)]))
        return found

    def start(self, item, length, targets, sems):
        place = item % length
        for way in (0, 1):
            for begin, size, refs in self.parts:
                inside = jnp.logical_and(place >= begin, place < begin + size)

                @pl.when(jnp.logical_and(item // length == way, inside))
                def _(way=way, begin=begin, size=size, refs=refs):
                    for kv, target in enumerate(targets):
                        source = refs[way].at[place - begin + kv * size]
                        pltpu.make_async_copy(source, target, sems.at[kv]).start()

    def wait(self, targets, sems):
        for kv, target in enumerate(targets):
            pltpu.make_async_copy(self.parts[0][2][0].at[0], target, sems.at[kv]).wait()


def exact_frame(lay, heads, frame, core, table_ref, q_refs, local, received, acc_s, m_s, l_s, tk, tv, sems):
    m_s[...] = jnp.full(m_s.shape, -jnp.inf, F32)
    l_s[...] = jnp.zeros(l_s.shape, F32)
    acc_s[...] = jnp.zeros(acc_s.shape, F32)

    def add_tile():
        for unit, part, cols in units(heads):
            scores = lax.dot_general(
                q_refs[part][0, :, cols], tk[:, cols], NT, preferred_element_type=F32
            )
            before = m_s[unit]
            top = jnp.maximum(before, jnp.max(scores, axis=1, keepdims=True))
            fade = jnp.exp2((before - top) * SCALE)
            mixed = mix(jnp.exp2((scores - top) * SCALE), tv[:, cols])
            acc_s[unit] = acc_s[unit] * fade + mixed[:, :HEAD_DIM]
            l_s[unit] = l_s[unit] * fade + mixed[:, HEAD_DIM:]
            m_s[unit] = top

    def near_tile(name):
        source, tile = name // lay.tiles, name % lay.tiles
        mine = tile // lay.half == core
        tile = tile % lay.half
        cols = columns(core, tk.shape[-1])
        for side in (0, 1):

            @pl.when(mine if side == 0 else jnp.logical_not(mine))
            def _(side=side):
                at = (source, tile, slice(None), cols) if side == 0 else (source, tile)
                found = [
                    pltpu.make_async_copy(local[2 * kv + side].at[at], buf, sems.at[kv])
                    for kv, buf in enumerate((tk, tv))
                ]
                for copy in found:
                    copy.start()
                for copy in found:
                    copy.wait()

    def far_tile(item, length):
        received.start(item, length, (tk, tv), sems)
        received.wait((tk, tv), sems)

    def own_step(i, _):
        near_tile(frame * lay.tiles + i)
        add_tile()
        return 0

    def near_step(i, _):
        name = table_ref[lay.near + frame * STRIDE + 1 + i]

        @pl.when(name < lay.own)
        def _():
            near_tile(name)

        @pl.when(name >= lay.own)
        def _():
            far_tile(name - lay.own, lay.early)

        add_tile()
        return 0

    def far_step(i, _):
        far_tile(table_ref[lay.far + frame * STRIDE + 1 + i], lay.places)
        add_tile()
        return 0

    lax.fori_loop(0, lay.tiles, own_step, 0)
    lax.fori_loop(0, table_ref[lay.near + frame * STRIDE], near_step, 0)
    if len(received.parts) > 1:
        lax.fori_loop(0, table_ref[lay.far + frame * STRIDE], far_step, 0)


def near_kernel(lay, heads, whole, place_ref, table_ref, q_own, q_other, *refs):
    core = place_ref[1]
    q_refs = (q_own, q_other)
    local, refs = refs[:4], refs[4:]
    if whole:
        received, out_refs, refs = Received(lay, refs[:2]), refs[2:4], refs[4:]
        acc_s, kbuf, vbuf, m_s, l_s, sems, tk, tv, far_sems = refs
    else:
        acc_out, stat_ref, kbuf, vbuf, m_s, l_s, sems = refs
        acc_s = acc_out.at[0]
    step = pl.program_id(0)
    frame = step + 1 if whole else step * (lay.here - 1)
    begin = 1 if whole else 0

    def first():
        return local_copies(lay, begin, core, local, (kbuf, vbuf), sems)

    def others():
        found = []
        for index in range(lay.here):
            if index != begin:
                found += local_copies(lay, index, core, local, (kbuf, vbuf), sems)
        return found + (received.early_copies((kbuf, vbuf), far_sems) if whole else [])

    @pl.when(step == 0)
    def _():
        for copy in first():
            copy.start()
        for copy in first():
            copy.wait()
        for copy in others():
            copy.start()

    attend_own(lay, q_refs, kbuf, vbuf, frame, m_s, l_s, acc_s, heads)

    @pl.when(step == 0)
    def _():
        for copy in others():
            copy.wait()

    attend_list(q_refs, kbuf, vbuf, table_ref, lay.near + frame * STRIDE, m_s, l_s, acc_s, heads)
    if whole:

        too_large = jnp.max(l_s[...]) > LARGE
        finish(out_refs, acc_s, l_s, heads)

        @pl.when(too_large)
        def _():
            exact_frame(lay, heads, frame, core, table_ref, q_refs, local, received, acc_s, m_s, l_s, tk, tv, far_sems)
            finish(out_refs, acc_s, l_s, heads)

    else:
        save_stats(stat_ref, m_s, l_s, heads)


def cost(scores):
    return pl.CostEstimate(flops=scores * 4 * HEAD_DIM, bytes_accessed=scores // 8, transcendentals=scores)


def token_blocks(rows, width, frame_of):
    return (
        pl.BlockSpec((1, rows, width), lambda s, place, _: (frame_of(s), 0, place[1])),
        pl.BlockSpec((1, rows, width), lambda s, *_: (frame_of(s), 0, 0)),
    )


def near_call(lay, heads, whole, place, table, queries, local, early=()):
    here, rows, width = queries[1].shape
    steps = here - 2 if whole else 2
    own, other = token_blocks(rows, width, (lambda s: s + 1) if whole else (lambda s: s * (here - 1)))
    count = lay.own + (2 * lay.early if whole else 0)
    bufs = [pltpu.VMEM((count, TILE, width), BF)] * 2
    sums = [pltpu.VMEM((2 * heads, rows, 128), F32)] * 2
    sems = [pltpu.SemaphoreType.DMA((here, 4))]
    if whole:
        out_specs = [own, pl.BlockSpec((1, rows, width), lambda s, *_: (s, 0, 0))]
        out_shape = [pltpu.HBM(queries[0].shape, BF), jax.ShapeDtypeStruct((steps, rows, width), BF)]
        scratch = [sums[0], *bufs, *sums, *sems]
        scratch += [pltpu.VMEM((TILE, width), BF)] * 2 + [pltpu.SemaphoreType.DMA((4,))]
    else:
        out_specs = [
            pl.BlockSpec((1, 2 * heads, rows, 128), lambda s, *_: (s, 0, 0, 0)),
            pl.BlockSpec((1, rows, 128), lambda s, *_: (s, 0, 0)),
        ]
        out_shape = [pltpu.HBM((2, 2 * heads, rows, 128), F32), pltpu.HBM((2, rows, 128), F32)]
        scratch = [*bufs, *sums, *sems]
    return pl.pallas_call(
        functools.partial(near_kernel, lay, heads, whole),
        grid_spec=pltpu.PrefetchScalarGridSpec(
            num_scalar_prefetch=2,
            grid=(steps,),
            in_specs=[own, other] + [ANY] * (4 + len(early)),
            out_specs=out_specs,
            scratch_shapes=scratch,
        ),
        out_shape=out_shape,
        compiler_params=pltpu.CompilerParams(vmem_limit_bytes=VMEM_LIMIT if whole else EDGE_LIMIT),
        cost_estimate=cost(steps * rows * heads * (128 if whole else 8) * TILE),
        name="attend_middle" if whole else "attend_edges",
    )(place, table, *queries, *in_hbm((*local, *early)))


def far_kernel(lay, heads, place_ref, table_ref, q_own, q_other, acc_ref, stat_ref, *refs):
    core = place_ref[1]
    q_refs = (q_own, q_other)
    local, received, out_refs = refs[:4], Received(lay, refs[4:8]), refs[9:11]
    kbuf, vbuf, acc_s, m_s, l_s, tk, tv, sems, exact_sems = refs[11:]
    step = pl.program_id(0)
    frame = step * (lay.here - 1)
    room = kbuf.shape[1]

    def bufs(at, i):
        return kbuf.at[at, i], vbuf.at[at, i]

    def start(at):
        base = lay.far + at * (lay.here - 1) * STRIDE

        def one(i, _):
            received.start(table_ref[base + 1 + i], lay.places, bufs(at, i), sems.at[at * room + i])
            return 0

        lax.fori_loop(0, table_ref[base], one, 0)

    @pl.when(step == 0)
    def _():
        start(0)
        start(1)

    load_stats(stat_ref, m_s, l_s, heads)
    acc_s[...] = acc_ref[0]
    base = lay.far + frame * STRIDE

    def wait(i, _):
        received.wait(bufs(step, i), sems.at[step * room + i])
        return 0

    lax.fori_loop(0, table_ref[base], wait, 0)
    attend_list(q_refs, kbuf.at[step], vbuf.at[step], table_ref, base, m_s, l_s, acc_s, heads, packed=True)

    too_large = jnp.max(l_s[...]) > LARGE
    finish(out_refs, acc_s, l_s, heads)

    @pl.when(too_large)
    def _():
        exact_frame(lay, heads, frame, core, table_ref, q_refs, local, received, acc_s, m_s, l_s, tk, tv, exact_sems)
        finish(out_refs, acc_s, l_s, heads)


def far_call(lay, heads, place, table, queries, acc, stats, local, early, late, out):
    here, rows, width = queries[1].shape
    own, other = token_blocks(rows, width, lambda s: s * (here - 1))
    anys = [*local, *early, *late]
    room = sum(lay.lengths[column] for way in (0, 1) for frame, column, _ in lay.remote(way) if frame == 0)
    sums = pltpu.VMEM((2 * heads, rows, 128), F32)
    return pl.pallas_call(
        functools.partial(far_kernel, lay, heads),
        grid_spec=pltpu.PrefetchScalarGridSpec(
            num_scalar_prefetch=2,
            grid=(2,),
            in_specs=[
                own,
                other,
                pl.BlockSpec((1, 2 * heads, rows, 128), lambda s, *_: (s, 0, 0, 0)),
                pl.BlockSpec((1, rows, 128), lambda s, *_: (s, 0, 0)),
            ]
            + [ANY] * (len(anys) + 1),
            out_specs=[own, pl.BlockSpec((1, rows, width), lambda s, *_: (s, 0, 0))],
            scratch_shapes=[
                pltpu.VMEM((2, room, TILE, width), BF),
                pltpu.VMEM((2, room, TILE, width), BF),
                sums,
                sums,
                sums,
                pltpu.VMEM((TILE, width), BF),
                pltpu.VMEM((TILE, width), BF),
                pltpu.SemaphoreType.DMA((2 * room, 2)),
                pltpu.SemaphoreType.DMA((2,)),
            ],
        ),
        out_shape=[jax.ShapeDtypeStruct(out.shape, BF), jax.ShapeDtypeStruct((2, rows, width), BF)],
        input_output_aliases={6 + len(anys): 0},
        compiler_params=pltpu.CompilerParams(vmem_limit_bytes=VMEM_LIMIT),
        cost_estimate=cost(2 * rows * heads * 14 * TILE),
        name="attend_late",
    )(place, table, *queries, acc, stats, *in_hbm(anys), out)


def place_kernel(place_ref, block_ref, _, out_ref):
    out_ref[...] = block_ref[...]


def place_call(place, blocks, out, frame_of):
    steps, rows, width = blocks.shape
    return pl.pallas_call(
        place_kernel,
        grid_spec=pltpu.PrefetchScalarGridSpec(
            num_scalar_prefetch=1,
            grid=(steps,),
            in_specs=[pl.BlockSpec((1, rows, width), lambda s, place: (s, 0, 0)), ANY],
            out_specs=pl.BlockSpec((1, rows, width), lambda s, place: (frame_of(s), 0, 1 - place[1])),
        ),
        out_shape=jax.ShapeDtypeStruct(out.shape, BF),
        input_output_aliases={2: 0},
        compiler_params=pltpu.CompilerParams(vmem_limit_bytes=PACK_LIMIT),
        name="place_columns",
    )(place, blocks, out)


def in_hbm(arrays):
    return [pltpu.with_memory_space_constraint(a, pltpu.HBM) for a in arrays]


def paired(block, way):
    pairs = range(1 - way, lax.axis_size("frame") - 1, 2)
    return lax.ppermute(block, "frame", [p for i in pairs for p in ((i, i + 1), (i + 1, i))])


def swapped(block):
    return lax.ppermute(block, "seq", [(0, 1), (1, 0)])


def per_device(queries, key_rows, value_rows, list_one, list_two, list_four, tile_counts):
    here, rows, width = queries.shape
    heads = -(-width // HEAD_DIM // 2)
    part = heads * HEAD_DIM
    frames = list_one.shape[0]
    lists = (list_one, list_two, list_four)
    lay = Layout(here, 2 * rows // TILE, frames, tuple(a.shape[2] for a in lists))
    core = lax.axis_index("seq")
    place = jnp.stack([lax.axis_index("frame") * here, core]).astype(jnp.int32)
    if width < 2 * part:
        spare = ((0, 0), (0, 0), (0, 2 * part - width))
        queries, key_rows, value_rows = (jnp.pad(a, spare) for a in (queries, key_rows, value_rows))

    def exchanged(a):
        return swapped(lax.dynamic_slice_in_dim(a, (1 - core) * part, part, axis=2))

    def tiled(a):
        return a.reshape(here, lay.half, TILE, a.shape[2])

    k_other = tiled(exchanged(key_rows))
    v_other = tiled(exchanged(value_rows))
    by_frame = [jnp.transpose(a, (1, 2, 0)) for a in lists] + [jnp.transpose(tile_counts, (2, 1, 0))]
    table, need = make_table(lay, place, by_frame)
    queries, table = lax.optimization_barrier((queries, table))
    queries = (queries, exchanged(queries))
    need = largest(need, "clips")[0]
    local = (tiled(key_rows), k_other, tiled(value_rows), v_other)
    early = pack_call(lay, 0, lay.early, place, table, local)
    sizes = range(max(1, lay.late - 3), lay.late + 1)
    return lax.switch(
        jnp.clip(need - lay.early - sizes[0], 0, len(sizes) - 1),
        [functools.partial(attend, lay, heads, width, size) for size in sizes],
        place,
        table,
        early,
        queries,
        local,
    )


def largest(number, axis):
    count = lax.axis_size(axis)
    most = number
    for step in range(1, count):
        most = jnp.maximum(most, lax.ppermute(number, axis, [(i, (i + step) % count) for i in range(count)]))
    return most


def attend(lay, heads, width, late_size, place, table, early, queries, local):
    def both_ways(pair):
        return paired(pair[0], 0), paired(pair[1], 1)

    early, table = lax.optimization_barrier((early, table))
    early = both_ways(early)
    late = both_ways(pack_call(lay, lay.early, late_size, place, table, local))
    acc, stats = near_call(lay, heads, False, place, table, queries, local)
    early, stats = lax.optimization_barrier((early, stats))
    out, sent = near_call(lay, heads, True, place, table, queries, local, early)
    late, sent = lax.optimization_barrier((late, sent))
    middle = swapped(sent)
    out, sent = far_call(lay, heads, place, table, queries, acc, stats, local, early, late, out)
    out = place_call(place, middle, out, lambda s: s + 1)
    out = place_call(place, swapped(sent), out, lambda s: s * (lay.here - 1))
    return out[:, :, :width]


def solution(mesh):
    placed = (
        P(("clips", "frame"), "seq", "head"),
        P(("clips", "frame"), "seq", "head"),
        P(("clips", "frame"), "seq", "head"),
        P("clips", None, None),
        P("clips", None, None),
        P("clips", None, None),
        P("clips", None, None),
    )
    return jax.shard_map(
        per_device,
        mesh=mesh,
        in_specs=placed,
        out_specs=P(("clips", "frame"), "seq", "head"),
        check_vma=False,
    )
```

```python
import functools
import math

import jax
import jax.numpy as jnp
from jax import lax
from jax.experimental import pallas as pl
from jax.experimental.pallas import tpu as pltpu
from jax.sharding import PartitionSpec as P

HEAD_DIM = 128
TILE = 128
DISTANCES = (1, 2, 4)
STRIDE = 24
SCALE = math.log2(math.e) / math.sqrt(HEAD_DIM)
LARGE = 2.0**100
NT = (((1,), (1,)), ((), ()))
BF = jnp.bfloat16
F32 = jnp.float32
ANY = pl.BlockSpec(memory_space=pl.ANY)
SMEM = pl.BlockSpec(memory_space=pltpu.SMEM)
VMEM_LIMIT = 48 * 2**20
PACK_LIMIT = 16 * 2**20


class Layout:
    def __init__(self, frames_here, frame_tiles, frames, lengths):
        self.here = frames_here
        self.tiles = frame_tiles
        self.half = frame_tiles // 2
        self.own = frames_here * frame_tiles
        self.frames = frames
        self.lengths = lengths
        self.early = self.late = 0
        for frame, column, _ in self.remote(0):
            if self.edge(frame):
                self.late += lengths[column]
            else:
                self.early += lengths[column]
        self.places = self.early + self.late
        self.first = self.early
        self.second = self.places - self.first
        self.near = 2 * self.places
        self.far = self.near + frames_here * STRIDE
        self.size = self.far + frames_here * STRIDE

    def edge(self, frame):
        return frame in (0, self.here - 1)

    def remote(self, direction):
        found = []
        for away in (*range(1, self.here - 1), self.here - 1, 0):
            for column in reversed(range(3)):
                distance = DISTANCES[column]
                if away < distance:
                    frame = away if direction == 0 else self.here - 1 - away
                    source = frame - distance if direction == 0 else frame + distance
                    found.append((frame, column, source % self.here))
        return found


def table_kernel(lay, place_ref, one_ref, two_ref, four_ref, count_ref, table_ref, seen_ref):
    lists = (one_ref, two_ref, four_ref)
    first = place_ref[0]
    odd = first // lay.here % 2

    def distinct(target, direction, on_slot, on_new):
        for i in range(lay.own):
            seen_ref[i] = -1
        used = jnp.int32(0)
        for frame, column, source in lay.remote(direction):
            live = count_ref[column, direction, target + frame]
            for slot in range(lay.lengths[column]):
                name = lists[column][direction, slot, target + frame] + source * lay.tiles
                alive = slot < live
                known = seen_ref[name]
                fresh = jnp.logical_and(alive, known < 0)
                place = jnp.where(fresh, used, known)
                seen_ref[name] = place
                on_new(used, name)
                on_slot(frame, place, alive)
                used = used + fresh.astype(jnp.int32)
        return used

    filled = {}

    def append(base, frame, item, alive):
        at = base + frame * STRIDE
        count = filled.get(at, jnp.int32(0))
        table_ref[at + 1 + count] = item
        filled[at] = count + alive.astype(jnp.int32)

    for direction in (0, 1):
        target = first + (lay.here if direction == 0 else -lay.here)
        target = jnp.clip(target, 0, lay.frames - lay.here)
        begin = (odd + direction) % 2 * lay.places
        for place in range(lay.places):
            table_ref[begin + place] = 0

        def note(used, name, begin=begin):
            table_ref[begin + jnp.minimum(used, lay.places - 1)] = name

        distinct(target, direction, lambda *_: None, note)

    for direction in (0, 1):
        way = (odd + 1 - direction) % 2

        def on_slot(frame, place, alive, way=way):
            if lay.edge(frame):
                append(lay.far, frame, way * lay.places + place, alive)
            else:
                append(lay.near, frame, lay.own + way * lay.early + place, alive)

        distinct(first, direction, on_slot, lambda *_: None)
        for frame in range(lay.here):
            for column, distance in enumerate(DISTANCES):
                source = frame + (2 * direction - 1) * distance
                if 0 <= source < lay.here:
                    live = count_ref[column, direction, first + frame]
                    for slot in range(lay.lengths[column]):
                        name = lists[column][direction, slot, first + frame]
                        append(lay.near, frame, source * lay.tiles + name, slot < live)
    for frame in range(lay.here):
        for base in (lay.near, lay.far):
            at = base + frame * STRIDE
            table_ref[at] = filled.get(at, jnp.int32(0))


def make_table(lay, place, lists):
    return pl.pallas_call(
        functools.partial(table_kernel, lay),
        in_specs=[SMEM] * 5,
        out_specs=SMEM,
        out_shape=jax.ShapeDtypeStruct((lay.size,), jnp.int32),
        scratch_shapes=[pltpu.SMEM((lay.own,), jnp.int32)],
        compiler_params=pltpu.CompilerParams(vmem_limit_bytes=VMEM_LIMIT),
        name="tile_tables",
    )(place, *lists)


def columns(core, width):
    return pl.ds(pl.multiple_of(core * width, HEAD_DIM), width)


def pack_kernel(lay, begin, length, place_ref, table_ref, *refs):
    sources, outs, sems = refs[:-3], refs[-3:-1], refs[-1]
    core = place_ref[1]
    cols = columns(core, outs[0].shape[-1])
    waits = []
    for way, out in enumerate(outs):
        for item in range(length):
            name = table_ref[way * lay.places + begin + item]
            frame = name // lay.tiles
            tile = name % lay.tiles
            mine = tile // lay.half == core
            tile = tile % lay.half
            for kv in range(len(sources) // 2):
                own, other = sources[2 * kv : 2 * kv + 2]
                target = out.at[kv * length + item]
                sem = sems.at[len(waits)]
                here = pltpu.make_async_copy(own.at[frame, tile, :, cols], target, sem)
                there = pltpu.make_async_copy(other.at[frame, tile], target, sem)
                pl.when(mine)(here.start)
                pl.when(jnp.logical_not(mine))(there.start)
                waits.append(here)
    for copy in waits:
        copy.wait()


def pack_call(lay, begin, length, place, table, local):
    kinds = len(local) // 2
    shape = jax.ShapeDtypeStruct((kinds * length, TILE, local[1].shape[-1]), BF)
    return pl.pallas_call(
        functools.partial(pack_kernel, lay, begin, length),
        in_specs=[SMEM] * 2 + [ANY] * len(local),
        out_specs=[pl.BlockSpec(memory_space=pltpu.VMEM)] * 2,
        out_shape=[shape] * 2,
        scratch_shapes=[pltpu.SemaphoreType.DMA((2 * kinds * length,))],
        compiler_params=pltpu.CompilerParams(vmem_limit_bytes=PACK_LIMIT),
        name="pack_tiles",
    )(place, table, *in_hbm(local))


def rows_of(buf, index, cols):
    tiles = buf[index, :, cols]
    return tiles.reshape(tiles.size // HEAD_DIM, HEAD_DIM)


def units(heads):
    for part in (0, 1):
        for head in range(heads):
            yield part * heads + head, part, slice(head * HEAD_DIM, (head + 1) * HEAD_DIM)


def mix(weights, values):
    return jnp.dot(
        weights.astype(BF),
        jnp.concatenate([values, jnp.ones_like(values)], axis=1),
        preferred_element_type=F32,
    )


def attend_tiles(q_refs, kbuf, vbuf, ids, m_s, l_s, acc_s, heads):
    for unit, part, cols in units(heads):
        keys = jnp.concatenate([rows_of(kbuf, i, cols) for i in ids], axis=0)
        values = jnp.concatenate([rows_of(vbuf, i, cols) for i in ids], axis=0)
        scores = lax.dot_general(q_refs[part][0, :, cols], keys, NT, preferred_element_type=F32)
        shift = jnp.concatenate([m_s[unit]] * len(ids), axis=1)
        mixed = mix(jnp.exp2((scores - shift) * SCALE), values)
        acc_s[unit] += mixed[:, :HEAD_DIM]
        l_s[unit] += mixed[:, HEAD_DIM:]


def attend_list(q_refs, kbuf, vbuf, table_ref, base, m_s, l_s, acc_s, heads, packed=False):
    count = table_ref[base]

    def add(start, n):
        ids = [start + j if packed else table_ref[base + 1 + start + j] for j in range(n)]
        attend_tiles(q_refs, kbuf, vbuf, ids, m_s, l_s, acc_s, heads)

    def four(i, _):
        add(4 * i, 4)
        return 0

    lax.fori_loop(0, count // 4, four, 0)

    @pl.when(count % 4 >= 2)
    def _():
        add(count // 4 * 4, 2)

    @pl.when(count % 2 == 1)
    def _():
        add(count - 1, 1)


def attend_own(lay, q_refs, kbuf, vbuf, frame, m_s, l_s, acc_s, heads):
    own = pl.ds(frame * lay.tiles, lay.tiles)
    for unit, part, cols in units(heads):
        scores = lax.dot_general(
            q_refs[part][0, :, cols], rows_of(kbuf, own, cols), NT, preferred_element_type=F32
        )
        top = jnp.max(scores[:, :TILE], axis=1, keepdims=True)
        mixed = mix(jnp.exp2((scores - top) * SCALE), rows_of(vbuf, own, cols))
        acc_s[unit] = mixed[:, :HEAD_DIM]
        l_s[unit] = mixed[:, HEAD_DIM:]
        m_s[unit] = jnp.broadcast_to(top, m_s.shape[1:])


def save_stats(stat_ref, m_s, l_s, heads):
    rows = stat_ref.shape[1]
    lane = lax.broadcasted_iota(jnp.int32, (rows, 128), 1)
    stat = jnp.zeros((rows, 128), F32)
    for unit, _, _ in units(heads):
        stat = jnp.where(lane == unit, l_s[unit], stat)
        stat = jnp.where(lane == 64 + unit, m_s[unit], stat)
    stat_ref[0] = stat


def load_stats(stat_ref, m_s, l_s, heads):
    rows = stat_ref.shape[1]
    for unit, _, _ in units(heads):
        l_s[unit] = jnp.broadcast_to(stat_ref[0, :, unit : unit + 1], (rows, 128))
        m_s[unit] = jnp.broadcast_to(stat_ref[0, :, 64 + unit : 65 + unit], (rows, 128))


def finish(out_refs, acc_s, l_s, heads):
    for unit, part, cols in units(heads):
        out_refs[part][0, :, cols] = (acc_s[unit] / l_s[unit]).astype(BF)


def local_copies(lay, index, core, local, bufs, sems):
    found = []
    for kv, buf in enumerate(bufs):
        own = local[2 * kv].at[index, :, :, columns(core, buf.shape[-1])]
        for side, source in enumerate((own, local[2 * kv + 1].at[index])):
            owner = core if side == 0 else 1 - core
            target = buf.at[pl.ds(index * lay.tiles + owner * lay.half, lay.half)]
            found.append(pltpu.make_async_copy(source, target, sems.at[index, 2 * kv + side]))
    return found


class Received:
    def __init__(self, lay, refs):
        self.lay = lay
        self.parts = [(0, lay.first, ((refs[:2], 0), (refs[2:4], 0)))]
        if len(refs) > 4:
            self.parts.append((lay.first, lay.second, ((refs[4:6], 0), (refs[4:6], lay.second))))

    def early_copies(self, bufs, sems):
        found = []
        for buf, (refs, _) in zip(bufs, self.parts[0][2]):
            for way in (0, 1):
                source = refs[way].at[pl.ds(0, self.lay.early)]
                target = buf.at[pl.ds(self.lay.own + way * self.lay.early, self.lay.early)]
                found.append(pltpu.make_async_copy(source, target, sems.at[len(found)]))
        return found

    def start(self, item, length, targets, sems):
        place = item % length
        for way in (0, 1):
            for begin, size, kinds in self.parts:
                inside = jnp.logical_and(place >= begin, place < begin + size)

                @pl.when(jnp.logical_and(item // length == way, inside))
                def _(way=way, begin=begin, kinds=kinds):
                    for kv, (target, (refs, row)) in enumerate(zip(targets, kinds)):
                        source = refs[way].at[place - begin + row]
                        pltpu.make_async_copy(source, target, sems.at[kv]).start()

    def wait(self, targets, sems):
        for kv, target in enumerate(targets):
            pltpu.make_async_copy(self.parts[0][2][0][0][0].at[0], target, sems.at[kv]).wait()


def exact_frame(lay, heads, frame, core, table_ref, q_refs, local, received, acc_s, m_s, l_s, tk, tv, sems):
    m_s[...] = jnp.full(m_s.shape, -jnp.inf, F32)
    l_s[...] = jnp.zeros(l_s.shape, F32)
    acc_s[...] = jnp.zeros(acc_s.shape, F32)

    def add_tile():
        for unit, part, cols in units(heads):
            scores = lax.dot_general(
                q_refs[part][0, :, cols], tk[:, cols], NT, preferred_element_type=F32
            )
            before = m_s[unit]
            top = jnp.maximum(before, jnp.max(scores, axis=1, keepdims=True))
            fade = jnp.exp2((before - top) * SCALE)
            mixed = mix(jnp.exp2((scores - top) * SCALE), tv[:, cols])
            acc_s[unit] = acc_s[unit] * fade + mixed[:, :HEAD_DIM]
            l_s[unit] = l_s[unit] * fade + mixed[:, HEAD_DIM:]
            m_s[unit] = top

    def near_tile(name):
        source, tile = name // lay.tiles, name % lay.tiles
        mine = tile // lay.half == core
        tile = tile % lay.half
        cols = columns(core, tk.shape[-1])
        for side in (0, 1):

            @pl.when(mine if side == 0 else jnp.logical_not(mine))
            def _(side=side):
                at = (source, tile, slice(None), cols) if side == 0 else (source, tile)
                found = [
                    pltpu.make_async_copy(local[2 * kv + side].at[at], buf, sems.at[kv])
                    for kv, buf in enumerate((tk, tv))
                ]
                for copy in found:
                    copy.start()
                for copy in found:
                    copy.wait()

    def far_tile(item, length):
        received.start(item, length, (tk, tv), sems)
        received.wait((tk, tv), sems)

    def own_step(i, _):
        near_tile(frame * lay.tiles + i)
        add_tile()
        return 0

    def near_step(i, _):
        name = table_ref[lay.near + frame * STRIDE + 1 + i]

        @pl.when(name < lay.own)
        def _():
            near_tile(name)

        @pl.when(name >= lay.own)
        def _():
            far_tile(name - lay.own, lay.early)

        add_tile()
        return 0

    def far_step(i, _):
        far_tile(table_ref[lay.far + frame * STRIDE + 1 + i], lay.places)
        add_tile()
        return 0

    lax.fori_loop(0, lay.tiles, own_step, 0)
    lax.fori_loop(0, table_ref[lay.near + frame * STRIDE], near_step, 0)
    if len(received.parts) > 1:
        lax.fori_loop(0, table_ref[lay.far + frame * STRIDE], far_step, 0)


def near_kernel(lay, heads, whole, place_ref, table_ref, q_own, q_other, *refs):
    core = place_ref[1]
    q_refs = (q_own, q_other)
    local, refs = refs[:4], refs[4:]
    if whole:
        received, out_refs, refs = Received(lay, refs[:4]), refs[4:6], refs[6:]
        acc_s, kbuf, vbuf, m_s, l_s, sems, tk, tv, far_sems = refs
    else:
        acc_out, stat_ref, kbuf, vbuf, m_s, l_s, sems = refs
        acc_s = acc_out.at[0]
    step = pl.program_id(0)
    frame = step + 1 if whole else step * (lay.here - 1)
    begin = 1 if whole else 0

    def first():
        return local_copies(lay, begin, core, local, (kbuf, vbuf), sems)

    def others():
        found = []
        for index in range(lay.here):
            if index != begin:
                found += local_copies(lay, index, core, local, (kbuf, vbuf), sems)
        return found + (received.early_copies((kbuf, vbuf), far_sems) if whole else [])

    @pl.when(step == 0)
    def _():
        for copy in first():
            copy.start()
        for copy in first():
            copy.wait()
        for copy in others():
            copy.start()

    attend_own(lay, q_refs, kbuf, vbuf, frame, m_s, l_s, acc_s, heads)

    @pl.when(step == 0)
    def _():
        for copy in others():
            copy.wait()

    attend_list(q_refs, kbuf, vbuf, table_ref, lay.near + frame * STRIDE, m_s, l_s, acc_s, heads)
    if whole:

        @pl.when(jnp.max(l_s[...]) > LARGE)
        def _():
            exact_frame(lay, heads, frame, core, table_ref, q_refs, local, received, acc_s, m_s, l_s, tk, tv, far_sems)

        finish(out_refs, acc_s, l_s, heads)
    else:
        save_stats(stat_ref, m_s, l_s, heads)


def cost(scores):
    return pl.CostEstimate(flops=scores * 4 * HEAD_DIM, bytes_accessed=scores // 8, transcendentals=scores)


def token_blocks(rows, width, frame_of):
    return (
        pl.BlockSpec((1, rows, width), lambda s, place, _: (frame_of(s), 0, place[1])),
        pl.BlockSpec((1, rows, width), lambda s, *_: (frame_of(s), 0, 0)),
    )


def near_call(lay, heads, whole, place, table, queries, local, early=()):
    here, rows, width = queries[1].shape
    steps = here - 2 if whole else 2
    own, other = token_blocks(rows, width, (lambda s: s + 1) if whole else (lambda s: s * (here - 1)))
    count = lay.own + (2 * lay.early if whole else 0)
    bufs = [pltpu.VMEM((count, TILE, width), BF)] * 2
    sums = [pltpu.VMEM((2 * heads, rows, 128), F32)] * 2
    sems = [pltpu.SemaphoreType.DMA((here, 4))]
    if whole:
        out_specs = [own, pl.BlockSpec((1, rows, width), lambda s, *_: (s, 0, 0))]
        out_shape = [jax.ShapeDtypeStruct(queries[0].shape, BF), jax.ShapeDtypeStruct((steps, rows, width), BF)]
        scratch = [sums[0], *bufs, *sums, *sems]
        scratch += [pltpu.VMEM((TILE, width), BF)] * 2 + [pltpu.SemaphoreType.DMA((4,))]
    else:
        out_specs = [
            pl.BlockSpec((1, 2 * heads, rows, 128), lambda s, *_: (s, 0, 0, 0)),
            pl.BlockSpec((1, rows, 128), lambda s, *_: (s, 0, 0)),
        ]
        out_shape = [jax.ShapeDtypeStruct((2, 2 * heads, rows, 128), F32), jax.ShapeDtypeStruct((2, rows, 128), F32)]
        scratch = [*bufs, *sums, *sems]
    return pl.pallas_call(
        functools.partial(near_kernel, lay, heads, whole),
        grid_spec=pltpu.PrefetchScalarGridSpec(
            num_scalar_prefetch=2,
            grid=(steps,),
            in_specs=[own, other] + [ANY] * (4 + len(early)),
            out_specs=out_specs,
            scratch_shapes=scratch,
        ),
        out_shape=out_shape,
        compiler_params=pltpu.CompilerParams(vmem_limit_bytes=VMEM_LIMIT),
        cost_estimate=cost(steps * rows * heads * (128 if whole else 8) * TILE),
        name="attend_middle" if whole else "attend_edges",
    )(place, table, *queries, *in_hbm((*local, *early)))


def far_kernel(lay, heads, place_ref, table_ref, q_own, q_other, acc_ref, stat_ref, *refs):
    core = place_ref[1]
    q_refs = (q_own, q_other)
    local, received, out_refs = refs[:4], Received(lay, refs[4:10]), refs[11:13]
    kbuf, vbuf, acc_s, m_s, l_s, tk, tv, sems, exact_sems = refs[13:]
    step = pl.program_id(0)
    frame = step * (lay.here - 1)
    room = kbuf.shape[1]

    def bufs(at, i):
        return kbuf.at[at, i], vbuf.at[at, i]

    def start(at):
        base = lay.far + at * (lay.here - 1) * STRIDE

        def one(i, _):
            received.start(table_ref[base + 1 + i], lay.places, bufs(at, i), sems.at[at * room + i])
            return 0

        lax.fori_loop(0, table_ref[base], one, 0)

    @pl.when(step == 0)
    def _():
        start(0)
        start(1)

    load_stats(stat_ref, m_s, l_s, heads)
    acc_s[...] = acc_ref[0]
    base = lay.far + frame * STRIDE

    def wait(i, _):
        received.wait(bufs(step, i), sems.at[step * room + i])
        return 0

    lax.fori_loop(0, table_ref[base], wait, 0)
    attend_list(q_refs, kbuf.at[step], vbuf.at[step], table_ref, base, m_s, l_s, acc_s, heads, packed=True)

    @pl.when(jnp.max(l_s[...]) > LARGE)
    def _():
        exact_frame(lay, heads, frame, core, table_ref, q_refs, local, received, acc_s, m_s, l_s, tk, tv, exact_sems)

    finish(out_refs, acc_s, l_s, heads)


def far_call(lay, heads, place, table, queries, acc, stats, local, early, late, out):
    here, rows, width = queries[1].shape
    own, other = token_blocks(rows, width, lambda s: s * (here - 1))
    anys = [*local, *early, *late]
    room = sum(lay.lengths[column] for way in (0, 1) for frame, column, _ in lay.remote(way) if frame == 0)
    sums = pltpu.VMEM((2 * heads, rows, 128), F32)
    return pl.pallas_call(
        functools.partial(far_kernel, lay, heads),
        grid_spec=pltpu.PrefetchScalarGridSpec(
            num_scalar_prefetch=2,
            grid=(2,),
            in_specs=[
                own,
                other,
                pl.BlockSpec((1, 2 * heads, rows, 128), lambda s, *_: (s, 0, 0, 0)),
                pl.BlockSpec((1, rows, 128), lambda s, *_: (s, 0, 0)),
            ]
            + [ANY] * (len(anys) + 1),
            out_specs=[own, pl.BlockSpec((1, rows, width), lambda s, *_: (s, 0, 0))],
            scratch_shapes=[
                pltpu.VMEM((2, room, TILE, width), BF),
                pltpu.VMEM((2, room, TILE, width), BF),
                sums,
                sums,
                sums,
                pltpu.VMEM((TILE, width), BF),
                pltpu.VMEM((TILE, width), BF),
                pltpu.SemaphoreType.DMA((2 * room, 2)),
                pltpu.SemaphoreType.DMA((2,)),
            ],
        ),
        out_shape=[jax.ShapeDtypeStruct(out.shape, BF), jax.ShapeDtypeStruct((2, rows, width), BF)],
        input_output_aliases={6 + len(anys): 0},
        compiler_params=pltpu.CompilerParams(vmem_limit_bytes=VMEM_LIMIT),
        cost_estimate=cost(2 * rows * heads * 14 * TILE),
        name="attend_late",
    )(place, table, *queries, acc, stats, *in_hbm(anys), out)


def place_kernel(place_ref, block_ref, _, out_ref):
    out_ref[...] = block_ref[...]


def place_call(place, blocks, out, frame_of):
    steps, rows, width = blocks.shape
    return pl.pallas_call(
        place_kernel,
        grid_spec=pltpu.PrefetchScalarGridSpec(
            num_scalar_prefetch=1,
            grid=(steps,),
            in_specs=[pl.BlockSpec((1, rows, width), lambda s, place: (s, 0, 0)), ANY],
            out_specs=pl.BlockSpec((1, rows, width), lambda s, place: (frame_of(s), 0, 1 - place[1])),
        ),
        out_shape=jax.ShapeDtypeStruct(out.shape, BF),
        input_output_aliases={2: 0},
        compiler_params=pltpu.CompilerParams(vmem_limit_bytes=VMEM_LIMIT),
        name="place_columns",
    )(place, blocks, out)


def in_hbm(arrays):
    return [pltpu.with_memory_space_constraint(a, pltpu.HBM) for a in arrays]


def paired(block, way):
    pairs = range(way, lax.axis_size("frame") - 1, 2)
    return lax.ppermute(block, "frame", [p for i in pairs for p in ((i, i + 1), (i + 1, i))])


def swapped(block):
    return lax.ppermute(block, "seq", [(0, 1), (1, 0)])


def per_device(queries, key_rows, value_rows, list_one, list_two, list_four, tile_counts):
    here, rows, width = queries.shape
    heads = -(-width // HEAD_DIM // 2)
    part = heads * HEAD_DIM
    frames = list_one.shape[0]
    lists = (list_one, list_two, list_four)
    lay = Layout(here, 2 * rows // TILE, frames, tuple(a.shape[2] for a in lists))
    core = lax.axis_index("seq")
    place = jnp.stack([lax.axis_index("frame") * here, core]).astype(jnp.int32)
    if width < 2 * part:
        spare = ((0, 0), (0, 0), (0, 2 * part - width))
        queries, key_rows, value_rows = (jnp.pad(a, spare) for a in (queries, key_rows, value_rows))

    def exchanged(a):
        return swapped(lax.dynamic_slice_in_dim(a, (1 - core) * part, part, axis=2))

    def tiled(a):
        return a.reshape(here, lay.half, TILE, a.shape[2])

    k_other = tiled(exchanged(key_rows))
    v_other = tiled(exchanged(value_rows))
    by_frame = [jnp.transpose(a, (1, 2, 0)) for a in lists] + [jnp.transpose(tile_counts, (2, 1, 0))]
    table = make_table(lay, place, by_frame)
    local = (tiled(key_rows), k_other, tiled(value_rows), v_other)

    def both_ways(pair):
        return paired(pair[0], 0), paired(pair[1], 1)

    keys = pack_call(lay, 0, lay.first, place, table, local[:2])
    keys, v_other, queries, table = lax.optimization_barrier((keys, v_other, queries, table))
    keys = both_ways(keys)
    queries = (queries, exchanged(queries))
    local = (*local[:3], v_other)
    values = pack_call(lay, 0, lay.first, place, table, local[2:])
    values, table = lax.optimization_barrier((values, table))
    values = both_ways(values)
    late = both_ways(pack_call(lay, lay.first, lay.second, place, table, local))
    keys, table = lax.optimization_barrier((keys, table))
    acc, stats = near_call(lay, heads, False, place, table, queries, local)
    values, stats = lax.optimization_barrier((values, stats))
    early = (*keys, *values)
    out, sent = near_call(lay, heads, True, place, table, queries, local, early)
    late, sent = lax.optimization_barrier((late, sent))
    middle = swapped(sent)
    out, sent = far_call(lay, heads, place, table, queries, acc, stats, local, early, late, out)
    out = place_call(place, middle, out, lambda s: s + 1)
    out = place_call(place, swapped(sent), out, lambda s: s * (here - 1))
    return out[:, :, :width]


def solution(mesh):
    placed = (
        P(("clips", "frame"), "seq", "head"),
        P(("clips", "frame"), "seq", "head"),
        P(("clips", "frame"), "seq", "head"),
        P("clips", None, None),
        P("clips", None, None),
        P("clips", None, None),
        P("clips", None, None),
    )
    return jax.shard_map(
        per_device,
        mesh=mesh,
        in_specs=placed,
        out_specs=P(("clips", "frame"), "seq", "head"),
        check_vma=False,
    )
```
